32 devices in a mesh: seq: 16 (over z, y, core), batch: 2 (over x).
Axes of the slice: x: 2, y: 2, z: 4, core: 2. Of those that a mesh axis runs over, the one named last changes fastest.
Arguments:
- tokens: bfloat16 [2, 2048, 1024], P('batch', 'seq'), may hold values from -6 to 6
- ln_gain: bfloat16 [1024], P(('seq', 'batch')), may hold values from 0.099609375 to 1.8984375
- ln_bias: bfloat16 [1024], P(('seq', 'batch')), may hold values from -3 to 3
- w_qkv: bfloat16 [1024, 3072], P(('seq', 'batch')), may hold values from -0.25 to 0.25
- b_qkv: bfloat16 [3072], P(('seq', 'batch')), may hold values from -2 to 2
- w_out: bfloat16 [1024, 1024], P(('seq', 'batch')), may hold values from -1 to 1
- w_up: bfloat16 [1024, 4096], P(('seq', 'batch')), may hold values from -0.1875 to 0.1875
- b_up: bfloat16 [4096], P(('seq', 'batch')), may hold values from -3 to 3
- w_down: bfloat16 [4096, 1024], P(('seq', 'batch')), may hold values from -0.125 to 0.125
- b_out: bfloat16 [1024], P(('seq', 'batch')), may hold values from -3 to 3
- cotangent: bfloat16 [2, 2048, 1024], P('batch', 'seq'), may hold values from -6 to 6
Outputs:
- out: bfloat16 [2, 2048, 1024], P('batch', 'seq')
- d_tokens: float32 [2, 2048, 1024], P('batch', 'seq')
- d_ln_gain: float32 [1024], P(('seq', 'batch'))
- d_ln_bias: float32 [1024], P(('seq', 'batch'))
- d_w_qkv: float32 [1024, 3072], P(('seq', 'batch'))
- d_b_qkv: float32 [3072], P(('seq', 'batch'))
- d_w_out: float32 [1024, 1024], P(('seq', 'batch'))
- d_w_up: float32 [1024, 4096], P(('seq', 'batch'))
- d_b_up: float32 [4096], P(('seq', 'batch'))
- d_w_down: float32 [4096, 1024], P(('seq', 'batch'))
- d_b_out: float32 [1024], P(('seq', 'batch'))
The draws below stay inside these ranges and needn't reach their ends.
All inputs are finite; a program needn't handle non-finite values.
Results may differ from the reference program's by a relative error of at most 0.015.
Values may be sent and summed in bfloat16 or wider, within the bound.
A program may use at most 192 MiB of HBM per device.

```python
import math
import jax
import jax.numpy as jnp
from jax import lax

D = 1024
HEADS = 16
HEAD_DIM = 64
ROTARY = 16
FF = 4096
LEN = 2048
SEQS = 2


def steps_of(rng, dims, cuts, least, largest):
    gain = 1.0
    for axis_at, parts in cuts:
        steps = jax.random.uniform(jax.random.fold_in(jax.random.fold_in(rng, 6), axis_at), (parts,), jnp.float32, least / len(cuts), largest / len(cuts))
        gain = gain * jnp.repeat(jnp.exp(steps), dims[axis_at] // parts).reshape((-1,) + (1,) * (len(dims) - 1 - axis_at))
    return gain


def normal_values(key, dims, scale, most, pieces=(), kind=jnp.bfloat16):
    factor_of = steps_of(key, dims, pieces, -0.22, 0.18) if pieces else 1.0
    array = jax.random.normal(key, dims, jnp.float32) * scale * factor_of
    return jnp.minimum(jnp.maximum(array, -most), most).astype(kind)


def setup_inputs(seed: int = 0) -> dict:
    seeds = jax.random.split(jax.random.key(seed), 12)
    tokens = normal_values(seeds[0], (SEQS, LEN, D), 1.0, 6.0, ((0, 2), (1, 16)))
    ln_gain = jnp.clip(1.0 + 0.18 * jax.random.normal(seeds[1], (D,), jnp.float32), 0.099609375, 1.8984375).astype(jnp.bfloat16)
    ln_bias = normal_values(seeds[2], (D,), 0.5, 3.0, ((0, 32),))
    w_qkv = normal_values(seeds[3], (D, 3 * D), (D // 2) ** -0.5, 0.25, ((0, 32),))
    b_qkv = normal_values(seeds[4], (3 * D,), 0.3, 2.0, ((0, 32),))
    w_out = normal_values(seeds[5], (D, D), (D // 32) ** -0.5, 1.0, ((0, 32),))
    w_up = normal_values(seeds[6], (D, FF), D ** -0.5, 0.1875, ((0, 32),))
    b_up = normal_values(seeds[7], (FF,), 0.5, 3.0, ((0, 32),))
    w_down = normal_values(seeds[8], (FF, D), (FF // 2) ** -0.5, 0.125, ((0, 32),))
    b_out = normal_values(seeds[9], (D,), 0.5, 3.0, ((0, 32),))
    cotangent = normal_values(seeds[10], (SEQS, LEN, D), 1.0, 6.0, ((0, 2), (1, 16)))
    return dict(tokens=tokens, ln_gain=ln_gain, ln_bias=ln_bias, w_qkv=w_qkv, b_qkv=b_qkv, w_out=w_out, w_up=w_up, b_up=b_up, w_down=w_down, b_out=b_out, cotangent=cotangent)


@jax.custom_vjp
def low(v):
    return lax.optimization_barrier(v.astype(jnp.bfloat16)).astype(jnp.float32)

@jax.custom_vjp
def low_back(v):
    return v

def low_keep(v):
    return (low(v), None)

def low_pass(kept, grad):
    return (grad,)

def back_keep(v):
    return (v, None)

def back_low(kept, grad):
    return (low(grad),)
low.defvjp(low_keep, low_pass)
low_back.defvjp(back_keep, back_low)
highest = lax.Precision.HIGHEST
eps_norm = 1e-05
neg_big = -1e+30
rotary_base = 10000.0

def rotary_tables(positions, half_width):
    frequency = rotary_base ** (-(2.0 * jnp.arange(half_width, dtype=jnp.float32)) / (2.0 * half_width))
    angles = positions[:, None] * frequency[None, :]
    return (jnp.cos(angles)[:, None, :], jnp.sin(angles)[:, None, :])

def rotate(section, cosine_table, sine_table):
    half_width = cosine_table.shape[-1]
    first_half = section[..., :half_width]
    second_half = section[..., half_width:2 * half_width]
    return jnp.concatenate([first_half * cosine_table - second_half * sine_table, second_half * cosine_table + first_half * sine_table, section[..., 2 * half_width:]], -1)

def attend_block(queries, key_rows, value_rows, offset):
    scores = jnp.einsum('qhd,khd->hqk', queries, key_rows, precision=highest) * HEAD_DIM ** (-0.5)
    scores = low_back(scores)
    query_pos = offset + jnp.arange(queries.shape[0], dtype=jnp.int32)
    key_pos = jnp.arange(key_rows.shape[0], dtype=jnp.int32)
    allowed = key_pos[None, :] <= query_pos[:, None]
    scores = jnp.where(allowed[None], scores, neg_big)
    probs = low(jax.nn.softmax(scores, axis=-1))
    return jnp.einsum('hqk,khd->qhd', probs, value_rows, precision=highest)

def block_layer(inputs, norm_gain, norm_shift, w_qkv, b_qkv, w_out, w_up, b_up, w_down, b_out):
    length, model_width = inputs.shape
    average = lax.optimization_barrier(jnp.mean(inputs, -1, keepdims=True))
    centered = inputs - average
    unit_rows = centered * lax.rsqrt(lax.optimization_barrier(jnp.mean(centered * centered, -1, keepdims=True)) + eps_norm)
    normed = low(unit_rows * norm_gain + norm_shift)
    joined_qkv = low_back(jnp.dot(normed, w_qkv, precision=highest) + b_qkv).reshape(length, 3, HEADS, HEAD_DIM)
    positions = jnp.arange(length, dtype=jnp.int32).astype(jnp.float32)
    cosine_table, sine_table = rotary_tables(positions, ROTARY // 2)
    queries = low(rotate(joined_qkv[:, 0], cosine_table, sine_table))
    key_rows = low(rotate(joined_qkv[:, 1], cosine_table, sine_table))
    value_rows = low(joined_qkv[:, 2])
    block_rows = math.gcd(length, 512)
    query_blocks = queries.reshape(length // block_rows, block_rows, HEADS, HEAD_DIM)
    offsets = jnp.arange(length // block_rows, dtype=jnp.int32) * block_rows

    def one_block(entry):
        return attend_block(entry[0], key_rows, value_rows, entry[1])
    mixed_heads = lax.map(jax.checkpoint(one_block), (query_blocks, offsets))
    mixed_heads = low(low_back(mixed_heads.reshape(length, model_width)))
    attn_out = jnp.dot(mixed_heads, w_out, precision=highest)
    up_proj = low_back(jnp.dot(normed, w_up, precision=highest) + b_up)
    activation = low(jax.nn.gelu(up_proj, approximate=False))
    mlp_out = jnp.dot(activation, w_down, precision=highest)
    return inputs + attn_out + mlp_out + b_out

def reference(tokens, ln_gain, ln_bias, w_qkv, b_qkv, w_out, w_up, b_up, w_down, b_out, cotangent):
    params = tuple((entry.astype(jnp.float32) for entry in (ln_gain, ln_bias, w_qkv, b_qkv, w_out, w_up, b_up, w_down, b_out)))

    def forward(inputs, *weights):

        def advance(state_in, sequence):
            return (state_in, block_layer(sequence, *weights))
        _, outputs = lax.scan(advance, jnp.zeros((), jnp.float32), inputs)
        return outputs
    outputs, pullback = jax.vjp(forward, tokens.astype(jnp.float32), *params)
    grads = pullback(cotangent.astype(jnp.float32))
    return (outputs.astype(jnp.bfloat16), grads[0], grads[1], grads[2], grads[3], grads[4], grads[5], grads[6], grads[7], grads[8], grads[9])
```

```python
import math

import jax
import jax.numpy as jnp
import numpy as np
from jax import lax
from jax.experimental import pallas as pl
from jax.experimental.pallas import tpu as pltpu
from jax.sharding import PartitionSpec as P

HEADS = 16
ROTARY = 16


eps_norm = 1e-05
neg_big = -1e30
rotary_base = 10000.0


def rotary_tables(positions, half_width):
    frequency = rotary_base ** (
        -(2.0 * jnp.arange(half_width, dtype=jnp.float32)) / (2.0 * half_width)
    )
    angles = positions[:, None] * frequency[None, :]
    return (jnp.cos(angles)[:, None, :], jnp.sin(angles)[:, None, :])


def rotate(section, cosine_table, sine_table):
    half_width = cosine_table.shape[-1]
    first_half = section[..., :half_width]
    second_half = section[..., half_width : 2 * half_width]
    return jnp.concatenate(
        [
            first_half * cosine_table - second_half * sine_table,
            second_half * cosine_table + first_half * sine_table,
            section[..., 2 * half_width :],
        ],
        -1,
    )


def exact_gelu(values):
    return jax.nn.gelu(values, approximate=False)


def contract_rows(left, right):
    return lax.dot_general(
        left, right, (((0,), (0,)), ((), ())), preferred_element_type=jnp.float32
    )


def times_transposed(left, right):
    return lax.dot_general(
        left, right, (((1,), (1,)), ((), ())), preferred_element_type=jnp.float32
    )


def masked_scores(queries, key_rows, query_pos, key_pos, score_scale):
    scores = (
        jnp.einsum("qhd,khd->hqk", queries, key_rows, preferred_element_type=jnp.float32)
        * score_scale
    )
    allowed = key_pos[None, :] <= query_pos[:, None]
    return jnp.where(allowed[None], scores, neg_big)


def split_blocks(flat_rows, block_rows, head_count, head_dim):
    length = flat_rows.shape[0]
    return flat_rows.reshape(length // block_rows, block_rows, head_count, head_dim)


def attend(queries, key_all, value_all, query_pos, score_scale, block_rows):
    head_count, head_dim = (queries.shape[1], queries.shape[2])
    length = key_all.shape[0]
    key_blocks = split_blocks(key_all, block_rows, head_count, head_dim)
    value_blocks = split_blocks(value_all, block_rows, head_count, head_dim)
    position_blocks = jnp.arange(length, dtype=jnp.int32).reshape(length // block_rows, block_rows)

    def statistics(state_in, entry):
        running_max, running_sum = state_in
        key_rows, key_pos = entry
        scores = masked_scores(queries, key_rows, query_pos, key_pos, score_scale)
        new_max = jnp.maximum(running_max, jnp.max(scores, -1))
        running_sum = running_sum * jnp.exp(running_max - new_max) + jnp.sum(
            jnp.exp(scores - new_max[..., None]), -1
        )
        return ((new_max, running_sum), None)

    start_state = (
        jnp.full((head_count, queries.shape[0]), neg_big, jnp.float32),
        jnp.zeros((head_count, queries.shape[0]), jnp.float32),
    )
    (running_max, running_sum), _ = lax.scan(statistics, start_state, (key_blocks, position_blocks))
    log_total = running_max + jnp.log(running_sum)

    def attend_accumulate(mixed_heads, entry):
        key_rows, value_rows, key_pos = entry
        scores = masked_scores(queries, key_rows, query_pos, key_pos, score_scale)
        probs_low = jnp.exp(scores - log_total[..., None]).astype(jnp.bfloat16)
        return (
            mixed_heads
            + jnp.einsum("hqk,khd->qhd", probs_low, value_rows, preferred_element_type=jnp.float32),
            None,
        )

    mixed_heads, _ = lax.scan(
        attend_accumulate,
        jnp.zeros(queries.shape, jnp.float32),
        (key_blocks, value_blocks, position_blocks),
    )
    return (mixed_heads, log_total)


def query_grads(
    queries,
    grad_heads,
    key_all,
    value_all,
    log_total,
    delta_rows,
    query_pos,
    score_scale,
    block_rows,
):
    head_count, head_dim = (queries.shape[1], queries.shape[2])
    length = key_all.shape[0]
    key_blocks = split_blocks(key_all, block_rows, head_count, head_dim)
    value_blocks = split_blocks(value_all, block_rows, head_count, head_dim)
    position_blocks = jnp.arange(length, dtype=jnp.int32).reshape(length // block_rows, block_rows)

    def query_accumulate(grad_queries, entry):
        key_rows, value_rows, key_pos = entry
        scores = masked_scores(queries, key_rows, query_pos, key_pos, score_scale)
        probs = jnp.exp(scores - log_total[..., None])
        grad_probs = jnp.einsum(
            "qhd,khd->hqk", grad_heads, value_rows, preferred_element_type=jnp.float32
        )
        grad_scores = (probs * (grad_probs - delta_rows[..., None])).astype(jnp.bfloat16)
        return (
            grad_queries
            + jnp.einsum("hqk,khd->qhd", grad_scores, key_rows, preferred_element_type=jnp.float32),
            None,
        )

    grad_queries, _ = lax.scan(
        query_accumulate,
        jnp.zeros(queries.shape, jnp.float32),
        (key_blocks, value_blocks, position_blocks),
    )
    return grad_queries * score_scale


def key_terms(
    queries,
    grad_heads,
    log_total,
    delta_rows,
    query_pos,
    key_rows,
    value_rows,
    key_pos,
    score_scale,
):
    scores = masked_scores(queries, key_rows, query_pos, key_pos, score_scale)
    probs = jnp.exp(scores - log_total[..., None])
    grad_probs = jnp.einsum(
        "qhd,khd->hqk", grad_heads, value_rows, preferred_element_type=jnp.float32
    )
    grad_scores = (probs * (grad_probs - delta_rows[..., None])).astype(jnp.bfloat16)
    grad_keys = (
        jnp.einsum("hqk,qhd->khd", grad_scores, queries, preferred_element_type=jnp.float32)
        * score_scale
    )
    grad_values = jnp.einsum(
        "hqk,qhd->khd", probs.astype(jnp.bfloat16), grad_heads, preferred_element_type=jnp.float32
    )
    key_count = key_rows.shape[0]
    return jnp.concatenate(
        [grad_keys.reshape(key_count, -1), grad_values.reshape(key_count, -1)], -1
    )


def local(tokens, ln_gain, ln_bias, w_qkv, b_qkv, w_out, w_up, b_up, w_down, b_out, cotangent):
    seq_count, tok_rows, model_width = tokens.shape
    head_count = HEADS
    head_dim = model_width // head_count
    score_scale = head_dim ** (-0.5)
    length = tok_rows * lax.axis_size("seq")
    block_rows = math.gcd(length, 512)
    token_count = seq_count * tok_rows
    owned_shards = (ln_gain, ln_bias, w_qkv, b_qkv, w_out, w_up, b_up, w_down, b_out)
    norm_gain, norm_shift, wqkv, bqkv, wout, wup, bup, wdown, bout = (
        lax.all_gather(owned_shards[0], ("seq", "batch"), axis=0, tiled=True),
        lax.all_gather(owned_shards[1], ("seq", "batch"), axis=0, tiled=True),
        lax.all_gather(owned_shards[2], ("seq", "batch"), axis=0, tiled=True),
        lax.all_gather(owned_shards[3], ("seq", "batch"), axis=0, tiled=True),
        lax.all_gather(owned_shards[4], ("seq", "batch"), axis=0, tiled=True),
        lax.all_gather(owned_shards[5], ("seq", "batch"), axis=0, tiled=True),
        lax.all_gather(owned_shards[6], ("seq", "batch"), axis=0, tiled=True),
        lax.all_gather(owned_shards[7], ("seq", "batch"), axis=0, tiled=True),
        lax.all_gather(owned_shards[8], ("seq", "batch"), axis=0, tiled=True),
    )
    inputs = tokens.reshape(token_count, model_width).astype(jnp.float32)
    average = jnp.mean(inputs, -1, keepdims=True)
    centered = inputs - average
    inv_root = lax.rsqrt(jnp.mean(centered * centered, -1, keepdims=True) + eps_norm)
    unit_rows = centered * inv_root
    normed = (unit_rows * norm_gain.astype(jnp.float32) + norm_shift.astype(jnp.float32)).astype(
        jnp.bfloat16
    )
    joined_qkv = (
        jnp.dot(normed, wqkv, preferred_element_type=jnp.float32) + bqkv.astype(jnp.float32)
    ).reshape(seq_count, tok_rows, 3, head_count, head_dim)
    query_pos = lax.axis_index("seq") * tok_rows + jnp.arange(tok_rows, dtype=jnp.int32)
    cosine_table, sine_table = rotary_tables(query_pos.astype(jnp.float32), ROTARY // 2)
    queries = rotate(joined_qkv[:, :, 0], cosine_table, sine_table).astype(jnp.bfloat16)
    key_local = rotate(joined_qkv[:, :, 1], cosine_table, sine_table).astype(jnp.bfloat16)
    value_local = joined_qkv[:, :, 2].astype(jnp.bfloat16)
    key_all, value_all = (
        lax.all_gather(
            key_local.reshape(seq_count, tok_rows, model_width), "seq", axis=1, tiled=True
        ),
        lax.all_gather(
            value_local.reshape(seq_count, tok_rows, model_width), "seq", axis=1, tiled=True
        ),
    )

    def forward_sequence(entry):
        query_seq, key_seq, value_seq = entry
        return attend(query_seq, key_seq, value_seq, query_pos, score_scale, block_rows)

    mixed_heads, log_total = lax.map(forward_sequence, (queries, key_all, value_all))
    mixed_low = mixed_heads.reshape(token_count, model_width).astype(jnp.bfloat16)
    attn_out = jnp.dot(mixed_low, wout, preferred_element_type=jnp.float32)
    up_proj = jnp.dot(normed, wup, preferred_element_type=jnp.float32) + bup.astype(jnp.float32)
    activation = exact_gelu(up_proj).astype(jnp.bfloat16)
    mlp_out = jnp.dot(activation, wdown, preferred_element_type=jnp.float32)
    result = (inputs + attn_out + mlp_out + bout.astype(jnp.float32)).astype(jnp.bfloat16)
    norm_gain, norm_shift, wqkv, bqkv, wout, wup, bup, wdown, bout = (
        lax.all_gather(owned_shards[0], ("seq", "batch"), axis=0, tiled=True),
        lax.all_gather(owned_shards[1], ("seq", "batch"), axis=0, tiled=True),
        lax.all_gather(owned_shards[2], ("seq", "batch"), axis=0, tiled=True),
        lax.all_gather(owned_shards[3], ("seq", "batch"), axis=0, tiled=True),
        lax.all_gather(owned_shards[4], ("seq", "batch"), axis=0, tiled=True),
        lax.all_gather(owned_shards[5], ("seq", "batch"), axis=0, tiled=True),
        lax.all_gather(owned_shards[6], ("seq", "batch"), axis=0, tiled=True),
        lax.all_gather(owned_shards[7], ("seq", "batch"), axis=0, tiled=True),
        lax.all_gather(owned_shards[8], ("seq", "batch"), axis=0, tiled=True),
    )
    cotangent_rows = cotangent.reshape(token_count, model_width)
    cotangent_f = cotangent_rows.astype(jnp.float32)
    grad_bout = jnp.sum(cotangent_f, 0)
    grad_wout = contract_rows(mixed_low, cotangent_rows)
    grad_wdown = contract_rows(activation, cotangent_rows)
    grad_act = times_transposed(cotangent_rows, wdown)
    _, gelu_back = jax.vjp(exact_gelu, up_proj)
    grad_up = gelu_back(grad_act)[0].astype(jnp.bfloat16)
    grad_wup = contract_rows(normed, grad_up)
    grad_bup = jnp.sum(grad_up.astype(jnp.float32), 0)
    grad_heads = (
        times_transposed(cotangent_rows, wout)
        .astype(jnp.bfloat16)
        .reshape(seq_count, tok_rows, head_count, head_dim)
    )
    delta_rows = jnp.swapaxes(jnp.sum(grad_heads.astype(jnp.float32) * mixed_heads, -1), 1, 2)

    def backward_sequence(entry):
        query_seq, grad_seq, key_seq, value_seq, total_seq, delta_seq = entry
        return query_grads(
            query_seq,
            grad_seq,
            key_seq,
            value_seq,
            total_seq,
            delta_seq,
            query_pos,
            score_scale,
            block_rows,
        )

    grad_queries = lax.map(
        backward_sequence, (queries, grad_heads, key_all, value_all, log_total, delta_rows)
    )
    row_count = tok_rows * lax.axis_size("seq")
    sub_rows = math.gcd(row_count, 512)

    def one_block(block_index):
        first_key = block_index * sub_rows
        key_pos = first_key + jnp.arange(sub_rows, dtype=jnp.int32)

        def one_sequence(entry):
            query_seq, grad_seq, total_seq, delta_seq, key_seq, value_seq = entry
            key_rows = lax.dynamic_slice_in_dim(key_seq, first_key, sub_rows, 0).reshape(
                sub_rows, head_count, head_dim
            )
            value_rows = lax.dynamic_slice_in_dim(value_seq, first_key, sub_rows, 0).reshape(
                sub_rows, head_count, head_dim
            )
            return key_terms(
                query_seq,
                grad_seq,
                total_seq,
                delta_seq,
                query_pos,
                key_rows,
                value_rows,
                key_pos,
                score_scale,
            )

        per_sequence = lax.map(
            one_sequence, (queries, grad_heads, log_total, delta_rows, key_all, value_all)
        )
        return jnp.swapaxes(per_sequence, 0, 1)

    block_terms = lax.map(one_block, jnp.arange(row_count // sub_rows, dtype=jnp.int32))
    summed = lax.psum_scatter(
        block_terms.reshape(row_count, seq_count, 2 * model_width).astype(jnp.bfloat16),
        "seq",
        scatter_dimension=0,
        tiled=True,
    ).astype(jnp.float32)
    key_grads_all = jnp.swapaxes(summed, 0, 1)
    grad_keys = key_grads_all[..., :model_width].reshape(seq_count, tok_rows, head_count, head_dim)
    grad_values = key_grads_all[..., model_width:].reshape(
        seq_count, tok_rows, head_count, head_dim
    )
    grad_q_turned = rotate(grad_queries, cosine_table, -sine_table)
    grad_k_turned = rotate(grad_keys, cosine_table, -sine_table)
    grad_joined = (
        jnp.stack([grad_q_turned, grad_k_turned, grad_values], 2)
        .reshape(token_count, 3 * model_width)
        .astype(jnp.bfloat16)
    )
    grad_wqkv = contract_rows(normed, grad_joined)
    grad_bqkv = jnp.sum(grad_joined.astype(jnp.float32), 0)
    grad_normed = times_transposed(grad_joined, wqkv) + times_transposed(grad_up, wup)
    grad_gain = jnp.sum(grad_normed * unit_rows, 0)
    grad_shift = jnp.sum(grad_normed, 0)
    grad_unit = grad_normed * norm_gain.astype(jnp.float32)
    grad_inputs = cotangent_f + inv_root * (
        grad_unit
        - jnp.mean(grad_unit, -1, keepdims=True)
        - unit_rows * jnp.mean(grad_unit * unit_rows, -1, keepdims=True)
    )
    owner_grads = (
        lax.psum_scatter(grad_gain, ("seq", "batch"), scatter_dimension=0, tiled=True),
        lax.psum_scatter(grad_shift, ("seq", "batch"), scatter_dimension=0, tiled=True),
        lax.psum_scatter(grad_wqkv, ("seq", "batch"), scatter_dimension=0, tiled=True),
        lax.psum_scatter(grad_bqkv, ("seq", "batch"), scatter_dimension=0, tiled=True),
        lax.psum_scatter(grad_wout, ("seq", "batch"), scatter_dimension=0, tiled=True),
        lax.psum_scatter(grad_wup, ("seq", "batch"), scatter_dimension=0, tiled=True),
        lax.psum_scatter(grad_bup, ("seq", "batch"), scatter_dimension=0, tiled=True),
        lax.psum_scatter(grad_wdown, ("seq", "batch"), scatter_dimension=0, tiled=True),
        lax.psum_scatter(grad_bout, ("seq", "batch"), scatter_dimension=0, tiled=True),
    )
    return (
        result.reshape(seq_count, tok_rows, model_width),
        grad_inputs.reshape(seq_count, tok_rows, model_width),
        owner_grads[0],
        owner_grads[1],
        owner_grads[2],
        owner_grads[3],
        owner_grads[4],
        owner_grads[5],
        owner_grads[6],
        owner_grads[7],
        owner_grads[8],
    )


MESH = pl.DeviceIdType.MESH
F32, BF16 = jnp.float32, jnp.bfloat16
TOK = 128
BT = 256
MODEL = 1024
SEQ = 16
CHIPS = 8
UP = 256
HD = 64
WIDE = 512
VEC = 448
GRADS = 448


def dot(left, right):
    return jnp.dot(left, right, preferred_element_type=F32)


def dot_nt(left, right):
    return lax.dot_general(left, right, (((1,), (1,)), ((), ())), preferred_element_type=F32)


def lanes(block):
    if isinstance(block, int):
        return slice(block * BT, (block + 1) * BT)
    return pl.ds(pl.multiple_of(block * BT, BT), BT)


def turn(rows, cosine, sine):
    first, second = rows[0:8], rows[8:16]
    return jnp.concatenate(
        [first * cosine - second * sine, second * cosine + first * sine, rows[16:]], 0
    )


def remote(src, dst, send_sem, recv_sem, device):
    return pltpu.make_async_remote_copy(
        src_ref=src,
        dst_ref=dst,
        send_sem=send_sem,
        recv_sem=recv_sem,
        device_id=device,
        device_id_type=MESH,
    )


def fused(
    tokens, cot, w_qkv, w_out, w_up, w_down, vec, cost, sint,
    out, d_tok, d_qkv, d_out, d_up, d_down, d_vec,
    tok, g, wsend, wc, wct, wd, gv, bct, normed, unit, amt, dactt, qt, kt, vt, k, v, sbuf, e,
    linv, ot, gt, dost, delta, dkt, dvt, part, rc1, ry1, rzl1, rzr1, rc2, ry2, rzl2, rzr2, tmp,
    dgain, dshift, dbout, dwct, dwd, dsend, drecv, dws, xrecv, arecv,
    w_ss, w_rs, x_ss, x_rs, wd_ss, wd_rs, t_ss, t_rs, g_ss, g_rs,
    c1_ss, c1_rs, y1_ss, y1_rs, zp1_ss, zl1_rs, zm1_ss, zr1_rs,
    c2_ss, c2_rs, y2_ss, y2_rs, zp2_ss, zl2_rs, zm2_ss, zr2_rs,
    d_ss, d_rs, dx_ss, dx_rs, a_ss, a_rs,
):
    s = lax.axis_index("seq")
    b = lax.axis_index("batch")
    z, y, c = s // 4, (s // 2) % 2, s % 2
    oy, oc, ob = 1 - y, 1 - c, 1 - b
    sib = (s + 1 - 2 * c, b)
    yn = (s + 2 - 4 * y, b)
    zp = (lax.rem(s + 4, SEQ), b)
    zm = (lax.rem(s + SEQ - 4, SEQ), b)
    xn = (s, ob)
    offsets = [(dz, dy, dc) for dz in (0, 1, 3, 2) for dy in (0, 1) for dc in (0, 1)][1:]

    def shifted(offset, sign):
        dz, dy, dc = offset
        return (
            4 * lax.rem(z + 4 + sign * dz, 4)
            + 2 * lax.rem(y + 2 + sign * dy, 2)
            + lax.rem(c + 2 + sign * dc, 2)
        )

    high = z // 2
    zo = [z, z + 1 - 2 * lax.rem(z, 2), 2 - high, 3 - 3 * high]

    barrier = pltpu.get_barrier_semaphore()
    for off in offsets:
        pl.semaphore_signal(
            barrier, inc=1, device_id=(shifted(off, 1), b), device_id_type=MESH
        )
    pl.semaphore_signal(barrier, inc=1, device_id=xn, device_id_type=MESH)

    for t in range(SEQ):
        wsend[t] = jnp.concatenate(
            [
                w_up[:, UP * t : UP * (t + 1)],
                w_qkv[:, HD * t : HD * (t + 1)],
                w_qkv[:, MODEL + HD * t : MODEL + HD * (t + 1)],
                w_qkv[:, 2 * MODEL + HD * t : 2 * MODEL + HD * (t + 1)],
                vec[...],
            ],
            1,
        )
    wc[2 * s + b] = wsend[s]
    tok[s] = tokens[...]
    g[s] = cot[...]
    down_own = pl.ds(pl.multiple_of(128 * b, 128), 128)
    down_other = pl.ds(pl.multiple_of(128 * ob, 128), 128)
    out_own = pl.ds(pl.multiple_of(UP + 32 * b, 32), 32)
    out_other = pl.ds(pl.multiple_of(UP + 32 * ob, 32), 32)
    wd[down_own] = w_down[...]
    wd[out_own] = w_out[...]
    pl.semaphore_wait(barrier, SEQ)

    def w_copy(source, target):
        return remote(
            wsend.at[target], wc.at[2 * source + b], w_ss.at[target], w_rs.at[source], (target, b)
        )

    def x_copy(source, plane):
        return remote(
            wc.at[2 * source + plane], wc.at[2 * source + plane],
            x_ss.at[source], x_rs.at[source], xn,
        )

    wd_copies = [
        remote(w_down, wd.at[down_own], wd_ss.at[0], wd_rs.at[0], xn),
        remote(w_out, wd.at[out_own], wd_ss.at[1], wd_rs.at[1], xn),
    ]

    def gather(buf, ss, rs):
        def send(shard, way, device):
            return remote(buf.at[shard], buf.at[shard], ss.at[way, shard], rs.at[shard], device)

        def arrived(shard):
            send(shard, 0, sib).wait_recv()

        def own(act):
            @pl.when(z < 3)
            def _():
                act(send(s, 0, zp))

            @pl.when(z > 0)
            def _():
                act(send(s, 1, zm))

            act(send(s, 2, yn))
            act(send(s, 3, sib))

        def on_z(t, act):
            shard = 4 * zo[t] + 2 * y + c

            @pl.when(jnp.logical_and(zo[t] < z, z < 3))
            def _():
                act(send(shard, 0, zp))

            @pl.when(jnp.logical_and(zo[t] > z, z > 0))
            def _():
                act(send(shard, 1, zm))

            act(send(shard, 2, yn))
            act(send(shard, 3, sib))

        def on_y(t, act):
            act(send(4 * zo[t] + 2 * oy + c, 3, sib))

        start = lambda copy: copy.start()
        finish = lambda copy: copy.wait_send()

        def step_z(t):
            arrived(4 * zo[t] + 2 * y + c)
            on_z(t, start)

        def step_y(t):
            arrived(4 * zo[t] + 2 * oy + c)
            on_y(t, start)

        def step_core(t, row):
            arrived(4 * zo[t] + 2 * row + oc)

        def drain():
            own(finish)
            for t in range(1, 4):
                on_z(t, finish)
            for t in range(4):
                on_y(t, finish)

        return (lambda: own(start)), step_z, step_y, step_core, drain

    tok_own, tok_z, tok_y, tok_core, tok_drain = gather(tok, t_ss, t_rs)
    g_own, g_z, g_y, g_core, g_drain = gather(g, g_ss, g_rs)

    for off in offsets:
        w_copy(s, shifted(off, 1)).start()
    x_copy(s, b).start()
    tok_own()
    for off in offsets:
        source = shifted(off, -1)
        w_copy(source, s).wait_recv()
        x_copy(source, b).start()
    for copy in wd_copies:
        copy.start()
    tok_z(1)
    tok_y(0)
    for t in range(SEQ):
        x_copy(t, ob).wait_recv()

    wct[...] = wc[...].reshape(MODEL, WIDE).T
    rows = wct[VEC : VEC + 16, :].astype(F32)
    gv[0:1] = rows[0:1]
    gv[1:2] = rows[1:2]
    gv[2:3] = rows[2:3]
    cols = []
    for half in range(2):
        tail = wc[2 * s + half][:, VEC - HD :].astype(F32)
        for i in range(4):
            cols.append(tail[:, HD + 3 + i : HD + 4 + i])
    lane_of = lax.broadcasted_iota(jnp.int32, (32, 128), 1)
    for which in range(3):
        for half in range(2):
            chunk = 32 * which + 2 * s + half
            tail = wc[chunk // 3][:, VEC - HD :].astype(F32)
            cols.append(
                jnp.sum(jnp.where(lane_of == HD + 7 + lax.rem(chunk, 3), tail, 0.0), 1, keepdims=True)
            )
    bct[...] = jnp.concatenate(cols, 0)

    def project(i):
        x = tok[pl.ds(2 * i, 2)].reshape(BT, MODEL).astype(F32)
        centered = x - jnp.mean(x, -1, keepdims=True)
        inv = lax.rsqrt(jnp.mean(centered * centered, -1, keepdims=True) + eps_norm)
        u = centered * inv
        n = (u * gv[0:1] + gv[1:2]).astype(BF16)
        normed[i] = n
        unit[i] = u.astype(BF16)
        jt = dot_nt(wct[0:VEC], n) + bct[...]
        up = jt[0:UP]
        half = 0.5 + 0.5 * lax.erf(up * 0.7071067811865476)
        at = lanes(i)
        amt[0:UP, at] = (up * half).astype(BF16)
        dactt[:, at] = half + up * (jnp.exp(-0.5 * up * up) * 0.3989422804014327)
        cs, sn = cost[:, at], sint[:, at]
        qt[:, at] = (turn(jt[256:320], cs, sn) * 0.125).astype(BF16)
        keys = turn(jt[320:384], cs, sn)
        kt[:, at] = keys.astype(BF16)
        vt[:, at] = jt[384:448].astype(BF16)
        k[i] = keys.T.astype(BF16)
        v[i] = jt[384:448].T.astype(BF16)

    def chip_of(t, row):
        return 2 * zo[t] + row

    for t in range(4):
        tok_core(t, y)
        project(chip_of(t, y))
        if t + 2 < 4:
            tok_z(t + 2)
        if t == 1:
            g_own()
        tok_core(t, oy)
        project(chip_of(t, oy))
        if t + 1 < 4:
            tok_y(t + 1)

    def attend_fwd(qb):
        at = lanes(qb)
        base = qb * (qb + 1) // 2
        q = qt[:, at]
        top = None
        for kb in range(qb + 1):
            st = dot(k[kb], q)
            if kb == qb:
                key_at = lax.broadcasted_iota(jnp.int32, (BT, BT), 0)
                query_at = lax.broadcasted_iota(jnp.int32, (BT, BT), 1)
                st = jnp.where(key_at <= query_at, st, neg_big)
            sbuf[kb] = st
            here = jnp.max(st, 0, keepdims=True)
            top = here if top is None else jnp.maximum(top, here)
        total = jnp.zeros((1, BT), F32)
        o = jnp.zeros((HD, BT), F32)
        for kb in range(qb + 1):
            ee = jnp.exp(sbuf[kb] - top)
            total = total + jnp.sum(ee, 0, keepdims=True)
            eb = ee.astype(BF16)
            e[base + kb] = eb
            o = o + dot(vt[:, lanes(kb)], eb)
        li = 1.0 / total
        linv[:, at] = li
        o = o * li
        ot[:, at] = o
        amt[UP : UP + HD, at] = o.astype(BF16)

    def reducer(rc, ry, rzl, rzr, c_ss, c_rs, y_ss, y_rs, zp_ss, zl_rs, zm_ss, zr_rs):
        order = [zo[3], zo[2], zo[1], zo[0]]

        def core_copy(t, row, color):
            chip = 2 * order[t] + row
            return remote(
                part.at[2 * chip + color], rc.at[chip], c_ss.at[chip], c_rs.at[chip], sib
            )

        def y_copy(t, row):
            return remote(
                rc.at[2 * order[t] + row], ry.at[order[t]], y_ss.at[order[t]], y_rs.at[order[t]], yn
            )

        def zp_copy(t):
            at = order[t]
            return remote(rc.at[2 * at + y], rzl.at[at], zp_ss.at[at], zl_rs.at[at], zp)

        def zm_copy(t):
            at = order[t]
            return remote(rc.at[2 * at + y], rzr.at[at], zm_ss.at[at], zr_rs.at[at], zm)

        def send_core(t, row):
            core_copy(t, row, oc).start()

        def send_y(t):
            chip = 2 * order[t] + oy
            core_copy(t, oy, oc).wait_recv()
            rc[chip] = (rc[chip].astype(F32) + part[2 * chip + c].astype(F32)).astype(BF16)
            y_copy(t, oy).start()

        def sum_here(t):
            chip = 2 * order[t] + y
            core_copy(t, y, oc).wait_recv()
            y_copy(t, y).wait_recv()
            tmp[...] = (
                rc[chip].astype(F32) + part[2 * chip + c].astype(F32) + ry[order[t]].astype(F32)
            )

        def add_left(t):
            zp_copy(t).wait_recv()
            tmp[...] += rzl[order[t]].astype(F32)

        def add_right(t):
            zm_copy(t).wait_recv()
            tmp[...] += rzr[order[t]].astype(F32)

        def pass_on(t):
            at = order[t]
            sum_here(t)

            @pl.when(jnp.logical_and(at > z, z > 0))
            def _():
                add_left(t)

            @pl.when(jnp.logical_and(at < z, z < 3))
            def _():
                add_right(t)

            rc[2 * at + y] = tmp[...].astype(BF16)

            @pl.when(at > z)
            def _():
                zp_copy(t).start()

            @pl.when(at < z)
            def _():
                zm_copy(t).start()

        def last():
            sum_here(3)

            @pl.when(z > 0)
            def _():
                add_left(3)

            @pl.when(z < 3)
            def _():
                add_right(3)

        def drain_core():
            for t in range(4):
                for row in (oy, y):
                    core_copy(t, row, oc).wait_send()

        def drain():
            for t in range(4):
                y_copy(t, oy).wait_send()
            for t in range(3):
                at = order[t]

                @pl.when(at > z)
                def _():
                    zp_copy(t).wait_send()

                @pl.when(at < z)
                def _():
                    zm_copy(t).wait_send()

        return order, send_core, send_y, pass_on, last, drain_core, drain

    order, core1, y1, pass1, last1, drain_core1, drain1 = reducer(
        rc1, ry1, rzl1, rzr1, c1_ss, c1_rs, y1_ss, y1_rs, zp1_ss, zl1_rs, zm1_ss, zr1_rs
    )
    _, core2, y2, pass2, last2, drain_core2, drain2 = reducer(
        rc2, ry2, rzl2, rzr2, c2_ss, c2_rs, y2_ss, y2_rs, zp2_ss, zl2_rs, zm2_ss, zr2_rs
    )

    def out_block(t, row):
        i = 2 * order[t] + row
        part[pl.ds(2 * i, 2)] = (
            dot(amt[:, lanes(i)].T, wd[...]).astype(BF16).reshape(2, TOK, MODEL)
        )
        core1(t, row)

    def grads_at(i):
        gb = g[pl.ds(2 * i, 2)].reshape(BT, MODEL)
        at = lanes(i)
        r = dot_nt(wd[...], gb)
        gt[0:UP, at] = (r[0:UP] * dactt[:, at]).astype(BF16)
        li = linv[:, at]
        gm = r[UP : UP + HD]
        dost[:, at] = (gm * li).astype(BF16)
        delta[:, at] = jnp.sum(gm * ot[:, at], 0, keepdims=True) * li
        dbout[...] += jnp.sum(gb.astype(F32).reshape(BT // 8, 8, MODEL), 0)

    def attend_bwd(qb):
        at = lanes(qb)
        base = qb * (qb + 1) // 2
        do, q, de = dost[:, at], qt[:, at], delta[:, at]
        dq = jnp.zeros((HD, BT), F32)
        for kb in range(qb + 1):
            ks = lanes(kb)
            eb = e[base + kb]
            dp = dot(v[kb], do)
            ds = (eb.astype(F32) * (dp - de)).astype(BF16)
            dv = dot_nt(do, eb)
            dk = dot_nt(q, ds)
            if kb == qb:
                dvt[:, ks] = dv
                dkt[:, ks] = dk
            else:
                dvt[:, ks] += dv
                dkt[:, ks] += dk
            dq = dq + dot(kt[:, ks], ds)
        gt[256:320, at] = turn(dq * 0.125, cost[:, at], -sint[:, at]).astype(BF16)

    def norm_grads(t, row):
        i = 2 * order[t] + row
        gn = dot(gt[:, lanes(i)].T, wct[0:GRADS])
        part[pl.ds(2 * i, 2)] = gn.astype(BF16).reshape(2, TOK, MODEL)
        core2(t, row)
        dshift[...] += jnp.sum(gn.reshape(BT // 8, 8, MODEL), 0)
        dgain[...] += jnp.sum((gn * unit[i].astype(F32)).reshape(BT // 8, 8, MODEL), 0)

    dgain[...] = jnp.zeros_like(dgain)
    dshift[...] = jnp.zeros_like(dshift)
    dbout[...] = jnp.zeros_like(dbout)
    for copy in wd_copies:
        copy.wait_send()
    remote(w_down, wd.at[down_other], wd_ss.at[0], wd_rs.at[0], xn).wait_recv()
    remote(w_out, wd.at[out_other], wd_ss.at[1], wd_rs.at[1], xn).wait_recv()

    g_z(1)
    g_y(0)
    for qb in range(CHIPS):
        attend_fwd(qb)
    g_z(2)
    g_core(0, y)
    grads_at(chip_of(0, y))
    out_block(0, oy)
    out_block(0, y)
    out_block(1, oy)
    out_block(1, y)
    g_y(1)
    g_core(0, oy)
    grads_at(chip_of(0, oy))
    g_core(1, y)
    grads_at(chip_of(1, y))
    out_block(2, oy)
    out_block(2, y)
    out_block(3, oy)
    out_block(3, y)
    g_z(3)
    for t in range(4):
        y1(t)
    g_core(1, oy)
    grads_at(chip_of(1, oy))
    g_core(2, y)
    grads_at(chip_of(2, y))
    g_y(2)
    g_core(2, oy)
    grads_at(chip_of(2, oy))
    g_core(3, y)
    grads_at(chip_of(3, y))
    g_y(3)
    g_core(3, oy)
    grads_at(chip_of(3, oy))

    for qb in range(CHIPS):
        attend_bwd(qb)
    pass1(0)
    gt[320:384, :] = turn(dkt[...], cost[...], -sint[...]).astype(BF16)
    gt[384:448, :] = dvt[...].astype(BF16)

    gg = g.reshape(SEQ * TOK, MODEL)
    for n in range(4):
        dwd[:, lanes(n)] = dot(amt[...], gg[:, lanes(n)])
    dsend[0:128] = dwd[down_other].astype(BF16)
    dsend[128:160] = dwd[out_other].astype(BF16)
    d_copy = remote(dsend, drecv, d_ss, d_rs, xn)
    d_copy.start()

    pass1(1)
    pass1(2)
    last1()
    out[...] = (tmp[...] + tokens[...].astype(F32) + gv[2:3]).astype(BF16)
    drain_core1()
    for t in range(4):
        norm_grads(t, oy)
        norm_grads(t, y)
    for t in range(4):
        y2(t)

    nn = normed.reshape(SEQ * TOK, MODEL)
    for n in range(4):
        dwct[0:GRADS, lanes(n)] = dot(gt[...], nn[:, lanes(n)])
    dwct[GRADS:WIDE] = jnp.zeros((WIDE - GRADS, MODEL), F32)
    dwct[VEC : VEC + 1] = jnp.sum(dgain[...], 0, keepdims=True)
    dwct[VEC + 1 : VEC + 2] = jnp.sum(dshift[...], 0, keepdims=True)
    dwct[VEC + 2 : VEC + 3] = jnp.sum(dbout[...], 0, keepdims=True)
    bias_col = jnp.sum(gt[...].astype(F32), 1, keepdims=True)
    bias_cols = jnp.concatenate(
        [jnp.zeros((32, HD + 3), F32)]
        + [bias_col[32 * n : 32 * (n + 1)] for n in range(14)]
        + [jnp.zeros((32, 128 - HD - 17), F32)],
        1,
    )
    for j in range(2 * SEQ // 4):
        turned = dwct[:, 128 * j : 128 * (j + 1)].T
        for i in range(4):
            piece = turned[32 * i : 32 * (i + 1)]
            dev = 4 * j + i
            dws[dev % 2, dev // 2, :, 0:384] = piece[:, 0:384].astype(BF16)
            dws[dev % 2, dev // 2, :, 384:512] = (piece[:, 384:512] + bias_cols).astype(BF16)
    dx_copy = remote(dws.at[ob], xrecv, dx_ss, dx_rs, xn)
    dx_copy.start()
    pass2(0)
    pass2(1)
    dx_copy.wait_recv()
    dws[b] = (dws[b].astype(F32) + xrecv[...].astype(F32)).astype(BF16)

    def a_copy(source, target):
        return remote(
            dws.at[b, target], arecv.at[source], a_ss.at[target], a_rs.at[source], (target, b)
        )

    for off in offsets:
        a_copy(s, shifted(off, 1)).start()
    arecv[s] = dws[b, s]
    d_copy.wait_recv()
    d_down[...] = dwd[down_own] + drecv[0:128].astype(F32)
    d_out[...] = dwd[out_own] + drecv[128:160].astype(F32)
    pass2(2)
    last2()

    x = tokens[...].astype(F32)
    centered = x - jnp.mean(x, -1, keepdims=True)
    inv = lax.rsqrt(jnp.mean(centered * centered, -1, keepdims=True) + eps_norm)
    u = centered * inv
    gu = tmp[...] * gv[0:1]
    d_tok[...] = cot[...].astype(F32) + inv * (
        gu - jnp.mean(gu, -1, keepdims=True) - u * jnp.mean(gu * u, -1, keepdims=True)
    )

    for off in offsets:
        a_copy(shifted(off, -1), s).wait_recv()
    sums = jnp.zeros((32, 128), F32)
    for t in range(0, SEQ, 2):
        even, odd = arecv[t].astype(F32), arecv[t + 1].astype(F32)
        d_up[:, UP * t : UP * (t + 1)] = even[:, 0:UP]
        d_up[:, UP * (t + 1) : UP * (t + 2)] = odd[:, 0:UP]
        for which in range(3):
            lo = UP + HD * which
            d_qkv[:, MODEL * which + HD * t : MODEL * which + HD * (t + 2)] = jnp.concatenate(
                [even[:, lo : lo + HD], odd[:, lo : lo + HD]], 1
            )
        sums = sums + even[:, 384:512] + odd[:, 384:512]
    mine = arecv[s][:, 384:512].astype(F32)
    picked = [sums[:, HD : HD + 1], sums[:, HD + 1 : HD + 2], mine[:, HD + 2 : HD + 3]]

    def pick(block, lane):
        return jnp.sum(jnp.where(lane_of == lane, block, 0.0), 1, keepdims=True)

    for i in range(4):
        picked.append(pick(mine, HD + 3 + 4 * b + i))
    for i in range(3):
        chunk = 3 * (2 * s + b) + i
        block = arecv[lax.rem(chunk, 32) // 2][:, 384:512].astype(F32)
        picked.append(pick(block, HD + 3 + 8 + 2 * (chunk // 32) + lax.rem(chunk, 2)))
    d_vec[...] = jnp.concatenate(picked + [jnp.zeros((32, 118), F32)], 1)

    for off in offsets:
        w_copy(s, shifted(off, 1)).wait_send()
        a_copy(s, shifted(off, 1)).wait_send()
    for t in range(SEQ):
        x_copy(t, b).wait_send()
    tok_drain()
    g_drain()
    drain1()
    drain_core2()
    drain2()
    d_copy.wait_send()
    dx_copy.wait_send()


def fast_local(
    tokens, ln_gain, ln_bias, w_qkv, b_qkv, w_out, w_up, b_up, w_down, b_out, cotangent
):
    vec = jnp.concatenate([ln_gain, ln_bias, b_out, b_up, b_qkv]).reshape(10, 32).T
    vec = jnp.pad(vec, ((0, 0), (0, HD - 10)))
    length = SEQ * TOK
    frequency = rotary_base ** (-(2.0 * np.arange(8)) / 16.0)
    angles = frequency.astype(np.float32)[:, None] * np.arange(length, dtype=np.float32)[None]
    cost = jnp.asarray(np.cos(angles.astype(np.float64)).astype(np.float32))
    sint = jnp.asarray(np.sin(angles.astype(np.float64)).astype(np.float32))
    vm = pl.BlockSpec(memory_space=pltpu.VMEM)
    shape = jax.ShapeDtypeStruct
    dma = pltpu.SemaphoreType.DMA

    def reduce_buffers():
        return [
            pltpu.VMEM((CHIPS, TOK, MODEL), BF16),
            pltpu.VMEM((4, TOK, MODEL), BF16),
            pltpu.VMEM((4, TOK, MODEL), BF16),
            pltpu.VMEM((4, TOK, MODEL), BF16),
        ]

    reduce_sems = [dma((8,)), dma((8,))] + [dma((4,))] * 6
    results = pl.pallas_call(
        fused,
        out_shape=[
            shape((TOK, MODEL), BF16),
            shape((TOK, MODEL), F32),
            shape((32, 3 * MODEL), F32),
            shape((32, MODEL), F32),
            shape((32, 4 * MODEL), F32),
            shape((128, MODEL), F32),
            shape((32, 128), F32),
        ],
        in_specs=[vm] * 9,
        out_specs=[vm] * 7,
        scratch_shapes=[
            pltpu.VMEM((SEQ, TOK, MODEL), BF16),
            pltpu.VMEM((SEQ, TOK, MODEL), BF16),
            pltpu.VMEM((SEQ, 32, WIDE), BF16),
            pltpu.VMEM((2 * SEQ, 32, WIDE), BF16),
            pltpu.VMEM((WIDE, MODEL), BF16),
            pltpu.VMEM((UP + HD, MODEL), BF16),
            pltpu.VMEM((8, MODEL), F32),
            pltpu.VMEM((VEC, 1), F32),
            pltpu.VMEM((CHIPS, BT, MODEL), BF16),
            pltpu.VMEM((CHIPS, BT, MODEL), BF16),
            pltpu.VMEM((UP + HD, length), BF16),
            pltpu.VMEM((UP, length), F32),
            pltpu.VMEM((HD, length), BF16),
            pltpu.VMEM((HD, length), BF16),
            pltpu.VMEM((HD, length), BF16),
            pltpu.VMEM((CHIPS, BT, HD), BF16),
            pltpu.VMEM((CHIPS, BT, HD), BF16),
            pltpu.VMEM((CHIPS, BT, BT), F32),
            pltpu.VMEM((36, BT, BT), BF16),
            pltpu.VMEM((1, length), F32),
            pltpu.VMEM((HD, length), F32),
            pltpu.VMEM((GRADS, length), BF16),
            pltpu.VMEM((HD, length), BF16),
            pltpu.VMEM((1, length), F32),
            pltpu.VMEM((HD, length), F32),
            pltpu.VMEM((HD, length), F32),
            pltpu.VMEM((SEQ, TOK, MODEL), BF16),
        ]
        + reduce_buffers()
        + reduce_buffers()
        + [
            pltpu.VMEM((TOK, MODEL), F32),
            pltpu.VMEM((8, MODEL), F32),
            pltpu.VMEM((8, MODEL), F32),
            pltpu.VMEM((8, MODEL), F32),
            pltpu.VMEM((WIDE, MODEL), F32),
            pltpu.VMEM((UP + HD, MODEL), F32),
            pltpu.VMEM((160, MODEL), BF16),
            pltpu.VMEM((160, MODEL), BF16),
            pltpu.VMEM((2, SEQ, 32, WIDE), BF16),
            pltpu.VMEM((SEQ, 32, WIDE), BF16),
            pltpu.VMEM((SEQ, 32, WIDE), BF16),
            dma((SEQ,)), dma((SEQ,)), dma((SEQ,)), dma((SEQ,)), dma((2,)), dma((2,)),
            dma((4, SEQ)), dma((SEQ,)), dma((4, SEQ)), dma((SEQ,)),
        ]
        + reduce_sems
        + reduce_sems
        + [dma, dma, dma, dma, dma((SEQ,)), dma((SEQ,))],
        compiler_params=pltpu.CompilerParams(
            collective_id=0, has_side_effects=True, vmem_limit_bytes=62 * 2**20
        ),
    )(
        tokens.reshape(TOK, MODEL), cotangent.reshape(TOK, MODEL),
        w_qkv, w_out, w_up, w_down, vec, cost, sint,
    )
    out, d_tok, d_qkv, d_out, d_up, d_down, d_vec = results
    vectors = d_vec[:, 0:10].T
    return (
        out.reshape(tokens.shape),
        d_tok.reshape(tokens.shape),
        vectors[0],
        vectors[1],
        d_qkv,
        vectors[7:10].reshape(96),
        d_out,
        d_up,
        vectors[3:7].reshape(128),
        d_down,
        vectors[2],
    )


def solution(mesh):
    in_specs = (
        P("batch", "seq", None),
        P(("seq", "batch")),
        P(("seq", "batch")),
        P(("seq", "batch"), None),
        P(("seq", "batch")),
        P(("seq", "batch"), None),
        P(("seq", "batch"), None),
        P(("seq", "batch")),
        P(("seq", "batch"), None),
        P(("seq", "batch")),
        P("batch", "seq", None),
    )
    out_specs = (
        P("batch", "seq", None),
        P("batch", "seq", None),
        P(("seq", "batch")),
        P(("seq", "batch")),
        P(("seq", "batch"), None),
        P(("seq", "batch")),
        P(("seq", "batch"), None),
        P(("seq", "batch"), None),
        P(("seq", "batch")),
        P(("seq", "batch"), None),
        P(("seq", "batch")),
    )
    fits = mesh.shape["seq"] == SEQ and mesh.shape["batch"] == 2
    body = fast_local if fits else local
    return jax.shard_map(body, mesh=mesh, in_specs=in_specs, out_specs=out_specs, check_vma=False)
```

```python
import math

import jax
import jax.numpy as jnp
import numpy as np
from jax import lax
from jax.experimental import pallas as pl
from jax.experimental.pallas import tpu as pltpu
from jax.sharding import PartitionSpec as P

HEADS = 16
ROTARY = 16


eps_norm = 1e-05
neg_big = -1e30
rotary_base = 10000.0


def rotary_tables(positions, half_width):
    frequency = rotary_base ** (
        -(2.0 * jnp.arange(half_width, dtype=jnp.float32)) / (2.0 * half_width)
    )
    angles = positions[:, None] * frequency[None, :]
    return (jnp.cos(angles)[:, None, :], jnp.sin(angles)[:, None, :])


def rotate(section, cosine_table, sine_table):
    half_width = cosine_table.shape[-1]
    first_half = section[..., :half_width]
    second_half = section[..., half_width : 2 * half_width]
    return jnp.concatenate(
        [
            first_half * cosine_table - second_half * sine_table,
            second_half * cosine_table + first_half * sine_table,
            section[..., 2 * half_width :],
        ],
        -1,
    )


def exact_gelu(values):
    return jax.nn.gelu(values, approximate=False)


def contract_rows(left, right):
    return lax.dot_general(
        left, right, (((0,), (0,)), ((), ())), preferred_element_type=jnp.float32
    )


def times_transposed(left, right):
    return lax.dot_general(
        left, right, (((1,), (1,)), ((), ())), preferred_element_type=jnp.float32
    )


def masked_scores(queries, key_rows, query_pos, key_pos, score_scale):
    scores = (
        jnp.einsum("qhd,khd->hqk", queries, key_rows, preferred_element_type=jnp.float32)
        * score_scale
    )
    allowed = key_pos[None, :] <= query_pos[:, None]
    return jnp.where(allowed[None], scores, neg_big)


def split_blocks(flat_rows, block_rows, head_count, head_dim):
    length = flat_rows.shape[0]
    return flat_rows.reshape(length // block_rows, block_rows, head_count, head_dim)


def attend(queries, key_all, value_all, query_pos, score_scale, block_rows):
    head_count, head_dim = (queries.shape[1], queries.shape[2])
    length = key_all.shape[0]
    key_blocks = split_blocks(key_all, block_rows, head_count, head_dim)
    value_blocks = split_blocks(value_all, block_rows, head_count, head_dim)
    position_blocks = jnp.arange(length, dtype=jnp.int32).reshape(length // block_rows, block_rows)

    def statistics(state_in, entry):
        running_max, running_sum = state_in
        key_rows, key_pos = entry
        scores = masked_scores(queries, key_rows, query_pos, key_pos, score_scale)
        new_max = jnp.maximum(running_max, jnp.max(scores, -1))
        running_sum = running_sum * jnp.exp(running_max - new_max) + jnp.sum(
            jnp.exp(scores - new_max[..., None]), -1
        )
        return ((new_max, running_sum), None)

    start_state = (
        jnp.full((head_count, queries.shape[0]), neg_big, jnp.float32),
        jnp.zeros((head_count, queries.shape[0]), jnp.float32),
    )
    (running_max, running_sum), _ = lax.scan(statistics, start_state, (key_blocks, position_blocks))
    log_total = running_max + jnp.log(running_sum)

    def attend_accumulate(mixed_heads, entry):
        key_rows, value_rows, key_pos = entry
        scores = masked_scores(queries, key_rows, query_pos, key_pos, score_scale)
        probs_low = jnp.exp(scores - log_total[..., None]).astype(jnp.bfloat16)
        return (
            mixed_heads
            + jnp.einsum("hqk,khd->qhd", probs_low, value_rows, preferred_element_type=jnp.float32),
            None,
        )

    mixed_heads, _ = lax.scan(
        attend_accumulate,
        jnp.zeros(queries.shape, jnp.float32),
        (key_blocks, value_blocks, position_blocks),
    )
    return (mixed_heads, log_total)


def query_grads(
    queries,
    grad_heads,
    key_all,
    value_all,
    log_total,
    delta_rows,
    query_pos,
    score_scale,
    block_rows,
):
    head_count, head_dim = (queries.shape[1], queries.shape[2])
    length = key_all.shape[0]
    key_blocks = split_blocks(key_all, block_rows, head_count, head_dim)
    value_blocks = split_blocks(value_all, block_rows, head_count, head_dim)
    position_blocks = jnp.arange(length, dtype=jnp.int32).reshape(length // block_rows, block_rows)

    def query_accumulate(grad_queries, entry):
        key_rows, value_rows, key_pos = entry
        scores = masked_scores(queries, key_rows, query_pos, key_pos, score_scale)
        probs = jnp.exp(scores - log_total[..., None])
        grad_probs = jnp.einsum(
            "qhd,khd->hqk", grad_heads, value_rows, preferred_element_type=jnp.float32
        )
        grad_scores = (probs * (grad_probs - delta_rows[..., None])).astype(jnp.bfloat16)
        return (
            grad_queries
            + jnp.einsum("hqk,khd->qhd", grad_scores, key_rows, preferred_element_type=jnp.float32),
            None,
        )

    grad_queries, _ = lax.scan(
        query_accumulate,
        jnp.zeros(queries.shape, jnp.float32),
        (key_blocks, value_blocks, position_blocks),
    )
    return grad_queries * score_scale


def key_terms(
    queries,
    grad_heads,
    log_total,
    delta_rows,
    query_pos,
    key_rows,
    value_rows,
    key_pos,
    score_scale,
):
    scores = masked_scores(queries, key_rows, query_pos, key_pos, score_scale)
    probs = jnp.exp(scores - log_total[..., None])
    grad_probs = jnp.einsum(
        "qhd,khd->hqk", grad_heads, value_rows, preferred_element_type=jnp.float32
    )
    grad_scores = (probs * (grad_probs - delta_rows[..., None])).astype(jnp.bfloat16)
    grad_keys = (
        jnp.einsum("hqk,qhd->khd", grad_scores, queries, preferred_element_type=jnp.float32)
        * score_scale
    )
    grad_values = jnp.einsum(
        "hqk,qhd->khd", probs.astype(jnp.bfloat16), grad_heads, preferred_element_type=jnp.float32
    )
    key_count = key_rows.shape[0]
    return jnp.concatenate(
        [grad_keys.reshape(key_count, -1), grad_values.reshape(key_count, -1)], -1
    )


def local(tokens, ln_gain, ln_bias, w_qkv, b_qkv, w_out, w_up, b_up, w_down, b_out, cotangent):
    seq_count, tok_rows, model_width = tokens.shape
    head_count = HEADS
    head_dim = model_width // head_count
    score_scale = head_dim ** (-0.5)
    length = tok_rows * lax.axis_size("seq")
    block_rows = math.gcd(length, 512)
    token_count = seq_count * tok_rows
    owned_shards = (ln_gain, ln_bias, w_qkv, b_qkv, w_out, w_up, b_up, w_down, b_out)
    norm_gain, norm_shift, wqkv, bqkv, wout, wup, bup, wdown, bout = (
        lax.all_gather(owned_shards[0], ("seq", "batch"), axis=0, tiled=True),
        lax.all_gather(owned_shards[1], ("seq", "batch"), axis=0, tiled=True),
        lax.all_gather(owned_shards[2], ("seq", "batch"), axis=0, tiled=True),
        lax.all_gather(owned_shards[3], ("seq", "batch"), axis=0, tiled=True),
        lax.all_gather(owned_shards[4], ("seq", "batch"), axis=0, tiled=True),
        lax.all_gather(owned_shards[5], ("seq", "batch"), axis=0, tiled=True),
        lax.all_gather(owned_shards[6], ("seq", "batch"), axis=0, tiled=True),
        lax.all_gather(owned_shards[7], ("seq", "batch"), axis=0, tiled=True),
        lax.all_gather(owned_shards[8], ("seq", "batch"), axis=0, tiled=True),
    )
    inputs = tokens.reshape(token_count, model_width).astype(jnp.float32)
    average = jnp.mean(inputs, -1, keepdims=True)
    centered = inputs - average
    inv_root = lax.rsqrt(jnp.mean(centered * centered, -1, keepdims=True) + eps_norm)
    unit_rows = centered * inv_root
    normed = (unit_rows * norm_gain.astype(jnp.float32) + norm_shift.astype(jnp.float32)).astype(
        jnp.bfloat16
    )
    joined_qkv = (
        jnp.dot(normed, wqkv, preferred_element_type=jnp.float32) + bqkv.astype(jnp.float32)
    ).reshape(seq_count, tok_rows, 3, head_count, head_dim)
    query_pos = lax.axis_index("seq") * tok_rows + jnp.arange(tok_rows, dtype=jnp.int32)
    cosine_table, sine_table = rotary_tables(query_pos.astype(jnp.float32), ROTARY // 2)
    queries = rotate(joined_qkv[:, :, 0], cosine_table, sine_table).astype(jnp.bfloat16)
    key_local = rotate(joined_qkv[:, :, 1], cosine_table, sine_table).astype(jnp.bfloat16)
    value_local = joined_qkv[:, :, 2].astype(jnp.bfloat16)
    key_all, value_all = (
        lax.all_gather(
            key_local.reshape(seq_count, tok_rows, model_width), "seq", axis=1, tiled=True
        ),
        lax.all_gather(
            value_local.reshape(seq_count, tok_rows, model_width), "seq", axis=1, tiled=True
        ),
    )

    def forward_sequence(entry):
        query_seq, key_seq, value_seq = entry
        return attend(query_seq, key_seq, value_seq, query_pos, score_scale, block_rows)

    mixed_heads, log_total = lax.map(forward_sequence, (queries, key_all, value_all))
    mixed_low = mixed_heads.reshape(token_count, model_width).astype(jnp.bfloat16)
    attn_out = jnp.dot(mixed_low, wout, preferred_element_type=jnp.float32)
    up_proj = jnp.dot(normed, wup, preferred_element_type=jnp.float32) + bup.astype(jnp.float32)
    activation = exact_gelu(up_proj).astype(jnp.bfloat16)
    mlp_out = jnp.dot(activation, wdown, preferred_element_type=jnp.float32)
    result = (inputs + attn_out + mlp_out + bout.astype(jnp.float32)).astype(jnp.bfloat16)
    norm_gain, norm_shift, wqkv, bqkv, wout, wup, bup, wdown, bout = (
        lax.all_gather(owned_shards[0], ("seq", "batch"), axis=0, tiled=True),
        lax.all_gather(owned_shards[1], ("seq", "batch"), axis=0, tiled=True),
        lax.all_gather(owned_shards[2], ("seq", "batch"), axis=0, tiled=True),
        lax.all_gather(owned_shards[3], ("seq", "batch"), axis=0, tiled=True),
        lax.all_gather(owned_shards[4], ("seq", "batch"), axis=0, tiled=True),
        lax.all_gather(owned_shards[5], ("seq", "batch"), axis=0, tiled=True),
        lax.all_gather(owned_shards[6], ("seq", "batch"), axis=0, tiled=True),
        lax.all_gather(owned_shards[7], ("seq", "batch"), axis=0, tiled=True),
        lax.all_gather(owned_shards[8], ("seq", "batch"), axis=0, tiled=True),
    )
    cotangent_rows = cotangent.reshape(token_count, model_width)
    cotangent_f = cotangent_rows.astype(jnp.float32)
    grad_bout = jnp.sum(cotangent_f, 0)
    grad_wout = contract_rows(mixed_low, cotangent_rows)
    grad_wdown = contract_rows(activation, cotangent_rows)
    grad_act = times_transposed(cotangent_rows, wdown)
    _, gelu_back = jax.vjp(exact_gelu, up_proj)
    grad_up = gelu_back(grad_act)[0].astype(jnp.bfloat16)
    grad_wup = contract_rows(normed, grad_up)
    grad_bup = jnp.sum(grad_up.astype(jnp.float32), 0)
    grad_heads = (
        times_transposed(cotangent_rows, wout)
        .astype(jnp.bfloat16)
        .reshape(seq_count, tok_rows, head_count, head_dim)
    )
    delta_rows = jnp.swapaxes(jnp.sum(grad_heads.astype(jnp.float32) * mixed_heads, -1), 1, 2)

    def backward_sequence(entry):
        query_seq, grad_seq, key_seq, value_seq, total_seq, delta_seq = entry
        return query_grads(
            query_seq,
            grad_seq,
            key_seq,
            value_seq,
            total_seq,
            delta_seq,
            query_pos,
            score_scale,
            block_rows,
        )

    grad_queries = lax.map(
        backward_sequence, (queries, grad_heads, key_all, value_all, log_total, delta_rows)
    )
    row_count = tok_rows * lax.axis_size("seq")
    sub_rows = math.gcd(row_count, 512)

    def one_block(block_index):
        first_key = block_index * sub_rows
        key_pos = first_key + jnp.arange(sub_rows, dtype=jnp.int32)

        def one_sequence(entry):
            query_seq, grad_seq, total_seq, delta_seq, key_seq, value_seq = entry
            key_rows = lax.dynamic_slice_in_dim(key_seq, first_key, sub_rows, 0).reshape(
                sub_rows, head_count, head_dim
            )
            value_rows = lax.dynamic_slice_in_dim(value_seq, first_key, sub_rows, 0).reshape(
                sub_rows, head_count, head_dim
            )
            return key_terms(
                query_seq,
                grad_seq,
                total_seq,
                delta_seq,
                query_pos,
                key_rows,
                value_rows,
                key_pos,
                score_scale,
            )

        per_sequence = lax.map(
            one_sequence, (queries, grad_heads, log_total, delta_rows, key_all, value_all)
        )
        return jnp.swapaxes(per_sequence, 0, 1)

    block_terms = lax.map(one_block, jnp.arange(row_count // sub_rows, dtype=jnp.int32))
    summed = lax.psum_scatter(
        block_terms.reshape(row_count, seq_count, 2 * model_width).astype(jnp.bfloat16),
        "seq",
        scatter_dimension=0,
        tiled=True,
    ).astype(jnp.float32)
    key_grads_all = jnp.swapaxes(summed, 0, 1)
    grad_keys = key_grads_all[..., :model_width].reshape(seq_count, tok_rows, head_count, head_dim)
    grad_values = key_grads_all[..., model_width:].reshape(
        seq_count, tok_rows, head_count, head_dim
    )
    grad_q_turned = rotate(grad_queries, cosine_table, -sine_table)
    grad_k_turned = rotate(grad_keys, cosine_table, -sine_table)
    grad_joined = (
        jnp.stack([grad_q_turned, grad_k_turned, grad_values], 2)
        .reshape(token_count, 3 * model_width)
        .astype(jnp.bfloat16)
    )
    grad_wqkv = contract_rows(normed, grad_joined)
    grad_bqkv = jnp.sum(grad_joined.astype(jnp.float32), 0)
    grad_normed = times_transposed(grad_joined, wqkv) + times_transposed(grad_up, wup)
    grad_gain = jnp.sum(grad_normed * unit_rows, 0)
    grad_shift = jnp.sum(grad_normed, 0)
    grad_unit = grad_normed * norm_gain.astype(jnp.float32)
    grad_inputs = cotangent_f + inv_root * (
        grad_unit
        - jnp.mean(grad_unit, -1, keepdims=True)
        - unit_rows * jnp.mean(grad_unit * unit_rows, -1, keepdims=True)
    )
    owner_grads = (
        lax.psum_scatter(grad_gain, ("seq", "batch"), scatter_dimension=0, tiled=True),
        lax.psum_scatter(grad_shift, ("seq", "batch"), scatter_dimension=0, tiled=True),
        lax.psum_scatter(grad_wqkv, ("seq", "batch"), scatter_dimension=0, tiled=True),
        lax.psum_scatter(grad_bqkv, ("seq", "batch"), scatter_dimension=0, tiled=True),
        lax.psum_scatter(grad_wout, ("seq", "batch"), scatter_dimension=0, tiled=True),
        lax.psum_scatter(grad_wup, ("seq", "batch"), scatter_dimension=0, tiled=True),
        lax.psum_scatter(grad_bup, ("seq", "batch"), scatter_dimension=0, tiled=True),
        lax.psum_scatter(grad_wdown, ("seq", "batch"), scatter_dimension=0, tiled=True),
        lax.psum_scatter(grad_bout, ("seq", "batch"), scatter_dimension=0, tiled=True),
    )
    return (
        result.reshape(seq_count, tok_rows, model_width),
        grad_inputs.reshape(seq_count, tok_rows, model_width),
        owner_grads[0],
        owner_grads[1],
        owner_grads[2],
        owner_grads[3],
        owner_grads[4],
        owner_grads[5],
        owner_grads[6],
        owner_grads[7],
        owner_grads[8],
    )


MESH = pl.DeviceIdType.MESH
F32, BF16 = jnp.float32, jnp.bfloat16
TOK = 128
BT = 256
MODEL = 1024
SEQ = 16
CHIPS = 8
UP = 256
HD = 64
WIDE = 512
VEC = 448
GRADS = 448


def dot(left, right):
    return jnp.dot(left, right, preferred_element_type=F32)


def dot_nt(left, right):
    return lax.dot_general(left, right, (((1,), (1,)), ((), ())), preferred_element_type=F32)


def lanes(block):
    if isinstance(block, int):
        return slice(block * BT, (block + 1) * BT)
    return pl.ds(pl.multiple_of(block * BT, BT), BT)


def turn(rows, cosine, sine):
    first, second = rows[0:8], rows[8:16]
    return jnp.concatenate(
        [first * cosine - second * sine, second * cosine + first * sine, rows[16:]], 0
    )


def remote(src, dst, send_sem, recv_sem, device):
    return pltpu.make_async_remote_copy(
        src_ref=src,
        dst_ref=dst,
        send_sem=send_sem,
        recv_sem=recv_sem,
        device_id=device,
        device_id_type=MESH,
    )


def fused(
    tokens, cot, w_qkv, w_out, w_up, w_down, gain, shift, bout, bup, bqkv, cost, sint,
    out, gn_sum, norm_gain, d_rows, arecv, ln_sums,
    tok, g, wsend, wc, wct, wd, gv, bct, normed, unit, amt, dactt, qt, kt, vt, k, v, sbuf, e,
    linv, ot, gt, dost, delta, dkt, dvt, part1, rc1, ry1, rzl1, rzr1, rc2, ry2, rzl2, rzr2, tmp,
    dgain, dshift, dbout, dwct, dwd, dsend, drecv, dws, xrecv, vsend, vrecv, vparts,
    w_ss, w_rs, x_ss, x_rs, wd_ss, wd_rs, t_ss, t_rs, g_ss, g_rs,
    c1_ss, c1_rs, y1_ss, y1_rs, zp1_ss, zl1_rs, zm1_ss, zr1_rs,
    c2_ss, c2_rs, y2_ss, y2_rs, zp2_ss, zl2_rs, zm2_ss, zr2_rs,
    d_ss, d_rs, dx_ss, dx_rs, a_ss, a_rs, vx_ss, vx_rs, v_ss, v_rs,
):
    s = lax.axis_index("seq")
    b = lax.axis_index("batch")
    z, y, c = s // 4, (s // 2) % 2, s % 2
    oy, oc, ob = 1 - y, 1 - c, 1 - b
    sib = (s + 1 - 2 * c, b)
    yn = (s + 2 - 4 * y, b)
    zp = (lax.rem(s + 4, SEQ), b)
    zm = (lax.rem(s + SEQ - 4, SEQ), b)
    xn = (s, ob)
    offsets = [(dz, dy, dc) for dz in (0, 1, 3, 2) for dy in (0, 1) for dc in (0, 1)][1:]

    def shifted(offset, sign):
        dz, dy, dc = offset
        return (
            4 * lax.rem(z + 4 + sign * dz, 4)
            + 2 * lax.rem(y + 2 + sign * dy, 2)
            + lax.rem(c + 2 + sign * dc, 2)
        )

    high = z // 2
    zo = [z, z + 1 - 2 * lax.rem(z, 2), 2 - high, 3 - 3 * high]

    barrier = pltpu.get_barrier_semaphore()
    for off in offsets:
        pl.semaphore_signal(
            barrier, inc=1, device_id=(shifted(off, 1), b), device_id_type=MESH
        )
    pl.semaphore_signal(barrier, inc=1, device_id=xn, device_id_type=MESH)

    vectors = [gain[...], shift[...], bout[...]]
    vectors += [bup[:, 32 * i : 32 * (i + 1)] for i in range(4)]
    vectors += [bqkv[:, 32 * i : 32 * (i + 1)] for i in range(3)]
    vec = jnp.concatenate([w.astype(F32) for w in vectors] + [jnp.zeros((6, 32), F32)], 0).T
    vec = jnp.concatenate([vec, jnp.zeros((32, HD - 16), F32)], 1).astype(BF16)
    for t in range(SEQ):
        wsend[t] = jnp.concatenate(
            [
                w_up[:, UP * t : UP * (t + 1)],
                w_qkv[:, HD * t : HD * (t + 1)],
                w_qkv[:, MODEL + HD * t : MODEL + HD * (t + 1)],
                w_qkv[:, 2 * MODEL + HD * t : 2 * MODEL + HD * (t + 1)],
                vec,
            ],
            1,
        )
    wc[2 * s + b] = wsend[s]
    tok[s] = tokens[...]
    g[s] = cot[...]
    down_own = pl.ds(pl.multiple_of(128 * b, 128), 128)
    down_other = pl.ds(pl.multiple_of(128 * ob, 128), 128)
    out_own = pl.ds(pl.multiple_of(UP + 32 * b, 32), 32)
    out_other = pl.ds(pl.multiple_of(UP + 32 * ob, 32), 32)
    wd[down_own] = w_down[...]
    wd[out_own] = w_out[...]
    pl.semaphore_wait(barrier, SEQ)

    def w_copy(source, target):
        return remote(
            wsend.at[target], wc.at[2 * source + b], w_ss.at[target], w_rs.at[source], (target, b)
        )

    def x_copy(source, plane):
        return remote(
            wc.at[2 * source + plane], wc.at[2 * source + plane],
            x_ss.at[source], x_rs.at[source], xn,
        )

    wd_copies = [
        remote(w_down, wd.at[down_own], wd_ss.at[0], wd_rs.at[0], xn),
        remote(w_out, wd.at[out_own], wd_ss.at[1], wd_rs.at[1], xn),
    ]

    def gather(buf, ss, rs):
        def send(shard, way, device):
            return remote(buf.at[shard], buf.at[shard], ss.at[way, shard], rs.at[shard], device)

        def arrived(shard):
            send(shard, 0, sib).wait_recv()

        def own(act):
            @pl.when(z < 3)
            def _():
                act(send(s, 0, zp))

            @pl.when(z > 0)
            def _():
                act(send(s, 1, zm))

            act(send(s, 2, yn))
            act(send(s, 3, sib))

        def on_z(t, act):
            shard = 4 * zo[t] + 2 * y + c

            @pl.when(jnp.logical_and(zo[t] < z, z < 3))
            def _():
                act(send(shard, 0, zp))

            @pl.when(jnp.logical_and(zo[t] > z, z > 0))
            def _():
                act(send(shard, 1, zm))

            act(send(shard, 2, yn))
            act(send(shard, 3, sib))

        def on_y(t, act):
            act(send(4 * zo[t] + 2 * oy + c, 3, sib))

        start = lambda copy: copy.start()
        finish = lambda copy: copy.wait_send()

        def step_z(t):
            arrived(4 * zo[t] + 2 * y + c)
            on_z(t, start)

        def step_y(t):
            arrived(4 * zo[t] + 2 * oy + c)
            on_y(t, start)

        def step_core(t, row):
            arrived(4 * zo[t] + 2 * row + oc)

        def drain():
            own(finish)
            for t in range(1, 4):
                on_z(t, finish)
            for t in range(4):
                on_y(t, finish)

        return (lambda: own(start)), step_z, step_y, step_core, drain

    tok_own, tok_z, tok_y, tok_core, tok_drain = gather(tok, t_ss, t_rs)
    g_own, g_z, g_y, g_core, g_drain = gather(g, g_ss, g_rs)

    tok_own()
    for off in offsets:
        w_copy(s, shifted(off, 1)).start()
    x_copy(s, b).start()
    tok_z(1)
    tok_y(0)
    for off in offsets:
        source = shifted(off, -1)
        w_copy(source, s).wait_recv()
        x_copy(source, b).start()
    for copy in wd_copies:
        copy.start()
    for t in range(SEQ):
        x_copy(t, ob).wait_recv()

    wct[...] = wc[...].reshape(MODEL, WIDE).T
    rows = wct[VEC : VEC + 16, :].astype(F32)
    gv[0:1] = rows[0:1]
    gv[1:2] = rows[1:2]
    gv[2:3] = rows[2:3]
    cols = []
    for half in range(2):
        tail = wc[2 * s + half][:, VEC - HD :].astype(F32)
        for i in range(4):
            cols.append(tail[:, HD + 3 + i : HD + 4 + i])
    lane_of = lax.broadcasted_iota(jnp.int32, (32, 128), 1)
    for which in range(3):
        for half in range(2):
            chunk = 32 * which + 2 * s + half
            tail = wc[chunk // 3][:, VEC - HD :].astype(F32)
            cols.append(
                jnp.sum(jnp.where(lane_of == HD + 7 + lax.rem(chunk, 3), tail, 0.0), 1, keepdims=True)
            )
    bct[...] = jnp.concatenate(cols, 0)

    def project(i):
        x = tok[pl.ds(2 * i, 2)].reshape(BT, MODEL).astype(F32)
        centered = x - jnp.mean(x, -1, keepdims=True)
        inv = lax.rsqrt(jnp.mean(centered * centered, -1, keepdims=True) + eps_norm)
        u = centered * inv
        n = (u * gv[0:1] + gv[1:2]).astype(BF16)
        normed[i] = n
        unit[i] = u.astype(BF16)
        jt = dot_nt(wct[0:VEC], n) + bct[...]
        up = jt[0:UP]
        half = 0.5 + 0.5 * lax.erf(up * 0.7071067811865476)
        at = lanes(i)
        amt[0:UP, at] = (up * half).astype(BF16)
        dactt[:, at] = half + up * (jnp.exp(-0.5 * up * up) * 0.3989422804014327)
        cs, sn = cost[:, at], sint[:, at]
        qt[:, at] = (turn(jt[256:320], cs, sn) * 0.125).astype(BF16)
        keys = turn(jt[320:384], cs, sn)
        kt[:, at] = keys.astype(BF16)
        vt[:, at] = jt[384:448].astype(BF16)
        k[i] = keys.T.astype(BF16)
        v[i] = jt[384:448].T.astype(BF16)

    def chip_of(t, row):
        return 2 * zo[t] + row

    for t in range(4):
        tok_core(t, y)
        project(chip_of(t, y))
        if t + 2 < 4:
            tok_z(t + 2)
        if t == 1:
            g_own()
        tok_core(t, oy)
        project(chip_of(t, oy))
        if t + 1 < 4:
            tok_y(t + 1)

    def e_put(n, block):
        m, at = 2 * (n // 4), 256 * (n % 4)
        e[m : m + 2, :, at : at + 256] = block.reshape(2, TOK, BT)

    def e_get(n):
        m, at = 2 * (n // 4), 256 * (n % 4)
        return e[m : m + 2, :, at : at + 256].reshape(BT, BT)

    def attend_fwd(qb):
        at = lanes(qb)
        base = qb * (qb + 1) // 2
        q = qt[:, at]
        top = None
        for kb in range(qb + 1):
            st = dot(k[kb], q)
            if kb == qb:
                key_at = lax.broadcasted_iota(jnp.int32, (BT, BT), 0)
                query_at = lax.broadcasted_iota(jnp.int32, (BT, BT), 1)
                st = jnp.where(key_at <= query_at, st, neg_big)
            sbuf[kb] = st
            here = jnp.max(st, 0, keepdims=True)
            top = here if top is None else jnp.maximum(top, here)
        total = jnp.zeros((1, BT), F32)
        o = jnp.zeros((HD, BT), F32)
        for kb in range(qb + 1):
            ee = jnp.exp(sbuf[kb] - top)
            total = total + jnp.sum(ee, 0, keepdims=True)
            eb = ee.astype(BF16)
            e_put(base + kb, eb)
            o = o + dot(vt[:, lanes(kb)], eb)
        li = 1.0 / total
        linv[:, at] = li
        o = o * li
        ot[:, at] = o
        amt[UP : UP + HD, at] = o.astype(BF16)

    def reducer(part, rc, ry, rzl, rzr, c_ss, c_rs, y_ss, y_rs, zp_ss, zl_rs, zm_ss, zr_rs):
        order = [zo[3], zo[2], zo[1], zo[0]]

        def core_copy(t, row, color):
            chip = 2 * order[t] + row
            return remote(
                part.at[2 * chip + color], rc.at[chip], c_ss.at[chip], c_rs.at[chip], sib
            )

        def y_copy(t, row):
            return remote(
                rc.at[2 * order[t] + row], ry.at[order[t]], y_ss.at[order[t]], y_rs.at[order[t]], yn
            )

        def zp_copy(t):
            at = order[t]
            return remote(rc.at[2 * at + y], rzl.at[at], zp_ss.at[at], zl_rs.at[at], zp)

        def zm_copy(t):
            at = order[t]
            return remote(rc.at[2 * at + y], rzr.at[at], zm_ss.at[at], zr_rs.at[at], zm)

        def send_core(t, row):
            core_copy(t, row, oc).start()

        def send_y(t):
            chip = 2 * order[t] + oy
            core_copy(t, oy, oc).wait_recv()
            rc[chip] = (rc[chip].astype(F32) + part[2 * chip + c].astype(F32)).astype(BF16)
            y_copy(t, oy).start()

        def sum_here(t):
            chip = 2 * order[t] + y
            core_copy(t, y, oc).wait_recv()
            y_copy(t, y).wait_recv()
            tmp[...] = (
                rc[chip].astype(F32) + part[2 * chip + c].astype(F32) + ry[order[t]].astype(F32)
            )

        def add_left(t):
            zp_copy(t).wait_recv()
            tmp[...] += rzl[order[t]].astype(F32)

        def add_right(t):
            zm_copy(t).wait_recv()
            tmp[...] += rzr[order[t]].astype(F32)

        def pass_on(t):
            at = order[t]
            sum_here(t)

            @pl.when(jnp.logical_and(at > z, z > 0))
            def _():
                add_left(t)

            @pl.when(jnp.logical_and(at < z, z < 3))
            def _():
                add_right(t)

            rc[2 * at + y] = tmp[...].astype(BF16)

            @pl.when(at > z)
            def _():
                zp_copy(t).start()

            @pl.when(at < z)
            def _():
                zm_copy(t).start()

        def last():
            sum_here(3)

            @pl.when(z > 0)
            def _():
                add_left(3)

            @pl.when(z < 3)
            def _():
                add_right(3)

        def drain_core():
            for t in range(4):
                for row in (oy, y):
                    core_copy(t, row, oc).wait_send()

        def drain():
            for t in range(4):
                y_copy(t, oy).wait_send()
            for t in range(3):
                at = order[t]

                @pl.when(at > z)
                def _():
                    zp_copy(t).wait_send()

                @pl.when(at < z)
                def _():
                    zm_copy(t).wait_send()

        return order, send_core, send_y, pass_on, last, drain_core, drain

    order, core1, y1, pass1, last1, drain_core1, drain1 = reducer(
        part1, rc1, ry1, rzl1, rzr1, c1_ss, c1_rs, y1_ss, y1_rs, zp1_ss, zl1_rs, zm1_ss, zr1_rs
    )
    _, core2, y2, pass2, last2, drain_core2, drain2 = reducer(
        e, rc2, ry2, rzl2, rzr2, c2_ss, c2_rs, y2_ss, y2_rs, zp2_ss, zl2_rs, zm2_ss, zr2_rs
    )

    def out_block(t, row):
        i = 2 * order[t] + row
        part1[pl.ds(2 * i, 2)] = (
            dot(amt[:, lanes(i)].T, wd[...]).astype(BF16).reshape(2, TOK, MODEL)
        )
        core1(t, row)

    def grads_at(i):
        gb = g[pl.ds(2 * i, 2)].reshape(BT, MODEL)
        at = lanes(i)
        r = dot_nt(wd[...], gb)
        gt[0:UP, at] = (r[0:UP] * dactt[:, at]).astype(BF16)
        li = linv[:, at]
        gm = r[UP : UP + HD]
        dost[:, at] = (gm * li).astype(BF16)
        delta[:, at] = jnp.sum(gm * ot[:, at], 0, keepdims=True) * li
        dbout[...] += jnp.sum(gb.astype(F32).reshape(BT // 8, 8, MODEL), 0)

    def attend_bwd(qb):
        at = lanes(qb)
        base = qb * (qb + 1) // 2
        do, q, de = dost[:, at], qt[:, at], delta[:, at]
        dq = jnp.zeros((HD, BT), F32)
        for kb in range(qb + 1):
            ks = lanes(kb)
            eb = e_get(base + kb)
            dp = dot(v[kb], do)
            ds = (eb.astype(F32) * (dp - de)).astype(BF16)
            dv = dot_nt(do, eb)
            dk = dot_nt(q, ds)
            if kb == qb:
                dvt[:, ks] = dv
                dkt[:, ks] = dk
            else:
                dvt[:, ks] += dv
                dkt[:, ks] += dk
            dq = dq + dot(kt[:, ks], ds)
        gt[256:320, at] = turn(dq * 0.125, cost[:, at], -sint[:, at]).astype(BF16)

    def norm_grads(t, row):
        i = 2 * order[t] + row
        gn = dot(gt[:, lanes(i)].T, wct[0:GRADS])
        e[pl.ds(2 * i, 2)] = gn.astype(BF16).reshape(2, TOK, MODEL)
        core2(t, row)
        dshift[...] += jnp.sum(gn.reshape(BT // 8, 8, MODEL), 0)
        dgain[...] += jnp.sum((gn * unit[i].astype(F32)).reshape(BT // 8, 8, MODEL), 0)

    dgain[...] = jnp.zeros_like(dgain)
    dshift[...] = jnp.zeros_like(dshift)
    dbout[...] = jnp.zeros_like(dbout)
    for copy in wd_copies:
        copy.wait_send()
    remote(w_down, wd.at[down_other], wd_ss.at[0], wd_rs.at[0], xn).wait_recv()
    remote(w_out, wd.at[out_other], wd_ss.at[1], wd_rs.at[1], xn).wait_recv()

    g_z(1)
    g_y(0)
    for qb in range(CHIPS):
        attend_fwd(qb)
    g_z(2)
    g_core(0, y)
    grads_at(chip_of(0, y))
    out_block(0, oy)
    out_block(0, y)
    out_block(1, oy)
    out_block(1, y)
    g_y(1)
    g_core(0, oy)
    grads_at(chip_of(0, oy))
    g_core(1, y)
    grads_at(chip_of(1, y))
    out_block(2, oy)
    out_block(2, y)
    out_block(3, oy)
    out_block(3, y)
    g_z(3)
    for t in range(4):
        y1(t)
    g_core(1, oy)
    grads_at(chip_of(1, oy))
    g_core(2, y)
    grads_at(chip_of(2, y))
    g_y(2)
    g_core(2, oy)
    grads_at(chip_of(2, oy))
    g_core(3, y)
    grads_at(chip_of(3, y))
    g_y(3)
    g_core(3, oy)
    grads_at(chip_of(3, oy))

    for qb in range(CHIPS):
        attend_bwd(qb)
    gt[320:384, :] = turn(dkt[...], cost[...], -sint[...]).astype(BF16)
    gt[384:448, :] = dvt[...].astype(BF16)
    pass1(0)

    nn = normed.reshape(SEQ * TOK, MODEL)
    for n in range(4):
        dwct[0:GRADS, lanes(n)] = dot(gt[...], nn[:, lanes(n)])
    dwct[GRADS:WIDE] = jnp.zeros((WIDE - GRADS, MODEL), F32)
    dwct[VEC : VEC + 1] = jnp.sum(dbout[...], 0, keepdims=True)
    bias_col = jnp.sum(gt[...].astype(F32), 1, keepdims=True)
    bias_cols = jnp.concatenate(
        [jnp.zeros((32, HD + 1), F32)]
        + [bias_col[32 * n : 32 * (n + 1)] for n in range(14)]
        + [jnp.zeros((32, 128 - HD - 15), F32)],
        1,
    )
    for j in range(2 * SEQ // 4):
        turned = dwct[:, 128 * j : 128 * (j + 1)].T
        for i in range(4):
            piece = turned[32 * i : 32 * (i + 1)]
            dev = 4 * j + i
            dws[dev % 2, dev // 2, :, 0:384] = piece[:, 0:384].astype(BF16)
            dws[dev % 2, dev // 2, :, 384:512] = (piece[:, 384:512] + bias_cols).astype(BF16)
    dx_copy = remote(dws.at[ob], xrecv, dx_ss, dx_rs, xn)
    dx_copy.start()

    for t in range(4):
        norm_grads(t, oy)
    for t in range(4):
        y2(t)
    pass1(1)
    for t in range(4):
        norm_grads(t, y)
    vsend[0:1] = jnp.sum(dgain[...], 0, keepdims=True)
    vsend[1:2] = jnp.sum(dshift[...], 0, keepdims=True)
    vsend[2:8] = jnp.zeros((6, MODEL), F32)
    vx_copy = remote(vsend, vrecv, vx_ss, vx_rs, xn)
    vx_copy.start()

    gg = g.reshape(SEQ * TOK, MODEL)
    for n in range(4):
        dwd[:, lanes(n)] = dot(amt[...], gg[:, lanes(n)])
    dsend[0:128] = dwd[down_other].astype(BF16)
    dsend[128:160] = dwd[out_other].astype(BF16)
    d_copy = remote(dsend, drecv, d_ss, d_rs, xn)
    d_copy.start()

    pass1(2)
    dx_copy.wait_recv()
    dws[b] = (dws[b].astype(F32) + xrecv[...].astype(F32)).astype(BF16)

    def a_copy(source, target):
        return remote(
            dws.at[b, target], arecv.at[source], a_ss.at[target], a_rs.at[source], (target, b)
        )

    for off in offsets:
        a_copy(s, shifted(off, 1)).start()
    arecv[s] = dws[b, s]
    last1()
    out[...] = (tmp[...] + tokens[...].astype(F32) + gv[2:3]).astype(BF16)

    vx_copy.wait()
    vrecv[...] += vsend[...]

    def v_copy(source, target):
        piece = pl.ds(pl.multiple_of(128 * (target // 2), 128), 128)
        return remote(
            vrecv.at[:, piece], vparts.at[source], v_ss.at[target], v_rs.at[source], (target, b)
        )

    for off in offsets:
        v_copy(s, shifted(off, 1)).start()
    vparts[s] = vrecv[:, pl.ds(pl.multiple_of(128 * (s // 2), 128), 128)]
    pass2(0)
    d_copy.wait_recv()
    d_rows[0:128] = dwd[down_own] + drecv[0:128].astype(F32)
    d_rows[128:160] = dwd[out_own] + drecv[128:160].astype(F32)
    norm_gain[...] = gv[...]
    pass2(1)
    pass2(2)
    for off in offsets:
        v_copy(shifted(off, -1), s).wait_recv()
    ln_sums[...] = jnp.sum(vparts[...], 0)
    last2()
    gn_sum[...] = tmp[...]
    for off in offsets:
        a_copy(shifted(off, -1), s).wait_recv()

    for off in offsets:
        w_copy(s, shifted(off, 1)).wait_send()
        a_copy(s, shifted(off, 1)).wait_send()
        v_copy(s, shifted(off, 1)).wait_send()
    for t in range(SEQ):
        x_copy(t, b).wait_send()
    tok_drain()
    g_drain()
    drain_core1()
    drain1()
    drain_core2()
    drain2()
    d_copy.wait_send()
    dx_copy.wait_send()


def finish(
    tokens_h, cot_h, out_h, gn_sum_h, norm_gain_h, d_rows_h, arecv_h, ln_sums_h,
    out, d_tok, d_gain, d_shift, d_qkv, d_bqkv, d_out, d_up, d_bup, d_down, d_bout,
    tokens, cot, gn_sum, norm_gain, d_rows, arecv, ln_sums, sems,
):
    moves = [
        pltpu.make_async_copy(src, dst, sems.at[n])
        for n, (src, dst) in enumerate(
            [
                (gn_sum_h, gn_sum), (tokens_h, tokens), (norm_gain_h, norm_gain), (cot_h, cot),
                (arecv_h, arecv), (d_rows_h, d_rows), (ln_sums_h, ln_sums), (out_h, out),
            ]
        )
    ]
    for move in moves:
        move.start()
    for move in moves:
        move.wait()
    s = lax.axis_index("seq")
    b = lax.axis_index("batch")
    x = tokens[...].astype(F32)
    centered = x - jnp.mean(x, -1, keepdims=True)
    inv = lax.rsqrt(jnp.mean(centered * centered, -1, keepdims=True) + eps_norm)
    u = centered * inv
    gu = gn_sum[...] * norm_gain[0:1]
    d_tok[...] = cot[...].astype(F32) + inv * (
        gu - jnp.mean(gu, -1, keepdims=True) - u * jnp.mean(gu * u, -1, keepdims=True)
    )
    d_down[...] = d_rows[0:128]
    d_out[...] = d_rows[128:160]
    for t in range(0, SEQ, 2):
        even, odd = arecv[t].astype(F32), arecv[t + 1].astype(F32)
        d_up[:, UP * t : UP * (t + 1)] = even[:, 0:UP]
        d_up[:, UP * (t + 1) : UP * (t + 2)] = odd[:, 0:UP]
        for which in range(3):
            lo = UP + HD * which
            d_qkv[:, MODEL * which + HD * t : MODEL * which + HD * (t + 2)] = jnp.concatenate(
                [even[:, lo : lo + HD], odd[:, lo : lo + HD]], 1
            )
    lane_of = lax.broadcasted_iota(jnp.int32, (32, 128), 1)

    def pick(block, lane):
        return jnp.sum(jnp.where(lane_of == lane, block, 0.0), 1, keepdims=True)

    mine = arecv[s][:, 384:512].astype(F32)
    picked = [mine[:, HD : HD + 1]]
    for i in range(4):
        picked.append(pick(mine, HD + 1 + 4 * b + i))
    for i in range(3):
        chunk = 3 * (2 * s + b) + i
        block = arecv[lax.rem(chunk, 32) // 2][:, 384:512].astype(F32)
        picked.append(pick(block, HD + 1 + 8 + 2 * (chunk // 32) + lax.rem(chunk, 2)))
    rows = jnp.concatenate(picked + [jnp.zeros((32, 120), F32)], 1).T
    d_bout[...] = rows[0:1]
    d_bup[...] = jnp.concatenate([rows[1 + i : 2 + i] for i in range(4)], 1)
    d_bqkv[...] = jnp.concatenate([rows[5 + i : 6 + i] for i in range(3)], 1)
    turned = pltpu.roll(ln_sums[...], lax.rem(128 - 32 * lax.rem(2 * s + b, 4), 128), 1)
    d_gain[...] = turned[0:1, 0:32]
    d_shift[...] = turned[1:2, 0:32]


def fast_local(
    tokens, ln_gain, ln_bias, w_qkv, b_qkv, w_out, w_up, b_up, w_down, b_out, cotangent
):
    length = SEQ * TOK
    frequency = rotary_base ** (-(2.0 * np.arange(8)) / 16.0)
    angles = frequency.astype(np.float32)[:, None] * np.arange(length, dtype=np.float32)[None]
    cost = jnp.asarray(np.cos(angles.astype(np.float64)).astype(np.float32))
    sint = jnp.asarray(np.sin(angles.astype(np.float64)).astype(np.float32))
    vm = pl.BlockSpec(memory_space=pltpu.VMEM)
    shape = jax.ShapeDtypeStruct
    dma = pltpu.SemaphoreType.DMA

    def reduce_buffers():
        return [
            pltpu.VMEM((CHIPS, TOK, MODEL), BF16),
            pltpu.VMEM((4, TOK, MODEL), BF16),
            pltpu.VMEM((4, TOK, MODEL), BF16),
            pltpu.VMEM((4, TOK, MODEL), BF16),
        ]

    reduce_sems = [dma((8,)), dma((8,))] + [dma((4,))] * 6
    results = pl.pallas_call(
        fused,
        out_shape=[
            shape((TOK, MODEL), BF16),
            shape((TOK, MODEL), F32),
            shape((8, MODEL), F32),
            shape((160, MODEL), F32),
            shape((SEQ, 32, WIDE), BF16),
            shape((8, 128), F32),
        ],
        in_specs=[vm] * 13,
        out_specs=[vm] * 6,
        scratch_shapes=[
            pltpu.VMEM((SEQ, TOK, MODEL), BF16),
            pltpu.VMEM((SEQ, TOK, MODEL), BF16),
            pltpu.VMEM((SEQ, 32, WIDE), BF16),
            pltpu.VMEM((2 * SEQ, 32, WIDE), BF16),
            pltpu.VMEM((WIDE, MODEL), BF16),
            pltpu.VMEM((UP + HD, MODEL), BF16),
            pltpu.VMEM((8, MODEL), F32),
            pltpu.VMEM((VEC, 1), F32),
            pltpu.VMEM((CHIPS, BT, MODEL), BF16),
            pltpu.VMEM((CHIPS, BT, MODEL), BF16),
            pltpu.VMEM((UP + HD, length), BF16),
            pltpu.VMEM((UP, length), F32),
            pltpu.VMEM((HD, length), BF16),
            pltpu.VMEM((HD, length), BF16),
            pltpu.VMEM((HD, length), BF16),
            pltpu.VMEM((CHIPS, BT, HD), BF16),
            pltpu.VMEM((CHIPS, BT, HD), BF16),
            pltpu.VMEM((CHIPS, BT, BT), F32),
            pltpu.VMEM((18, TOK, MODEL), BF16),
            pltpu.VMEM((1, length), F32),
            pltpu.VMEM((HD, length), F32),
            pltpu.VMEM((GRADS, length), BF16),
            pltpu.VMEM((HD, length), BF16),
            pltpu.VMEM((1, length), F32),
            pltpu.VMEM((HD, length), F32),
            pltpu.VMEM((HD, length), F32),
            pltpu.VMEM((SEQ, TOK, MODEL), BF16),
        ]
        + reduce_buffers()
        + reduce_buffers()
        + [
            pltpu.VMEM((TOK, MODEL), F32),
            pltpu.VMEM((8, MODEL), F32),
            pltpu.VMEM((8, MODEL), F32),
            pltpu.VMEM((8, MODEL), F32),
            pltpu.VMEM((WIDE, MODEL), F32),
            pltpu.VMEM((UP + HD, MODEL), F32),
            pltpu.VMEM((160, MODEL), BF16),
            pltpu.VMEM((160, MODEL), BF16),
            pltpu.VMEM((2, SEQ, 32, WIDE), BF16),
            pltpu.VMEM((SEQ, 32, WIDE), BF16),
            pltpu.VMEM((8, MODEL), F32),
            pltpu.VMEM((8, MODEL), F32),
            pltpu.VMEM((SEQ, 8, 128), F32),
            dma((SEQ,)), dma((SEQ,)), dma((SEQ,)), dma((SEQ,)), dma((2,)), dma((2,)),
            dma((4, SEQ)), dma((SEQ,)), dma((4, SEQ)), dma((SEQ,)),
        ]
        + reduce_sems
        + reduce_sems
        + [dma, dma, dma, dma, dma((SEQ,)), dma((SEQ,)), dma, dma, dma((SEQ,)), dma((SEQ,))],
        compiler_params=pltpu.CompilerParams(
            collective_id=0, has_side_effects=True, vmem_limit_bytes=62 * 2**20
        ),
    )(
        tokens.reshape(TOK, MODEL), cotangent.reshape(TOK, MODEL),
        w_qkv, w_out, w_up, w_down,
        ln_gain.reshape(1, 32), ln_bias.reshape(1, 32), b_out.reshape(1, 32),
        b_up.reshape(1, 128), b_qkv.reshape(1, 96), cost, sint,
    )
    out, gn_sum, norm_gain, d_rows, arecv, ln_sums = results
    (out, d_tok, d_gain, d_shift, d_qkv, d_bqkv, d_out, d_up, d_bup, d_down, d_bout) = pl.pallas_call(
        finish,
        out_shape=[
            shape((TOK, MODEL), BF16),
            shape((TOK, MODEL), F32),
            shape((1, 32), F32),
            shape((1, 32), F32),
            shape((32, 3 * MODEL), F32),
            shape((1, 96), F32),
            shape((32, MODEL), F32),
            shape((32, 4 * MODEL), F32),
            shape((1, 128), F32),
            shape((128, MODEL), F32),
            shape((1, 32), F32),
        ],
        in_specs=[pl.BlockSpec(memory_space=pl.ANY)] * 8,
        out_specs=[vm] * 11,
        scratch_shapes=[
            pltpu.VMEM((TOK, MODEL), BF16),
            pltpu.VMEM((TOK, MODEL), BF16),
            pltpu.VMEM((TOK, MODEL), F32),
            pltpu.VMEM((8, MODEL), F32),
            pltpu.VMEM((160, MODEL), F32),
            pltpu.VMEM((SEQ, 32, WIDE), BF16),
            pltpu.VMEM((8, 128), F32),
            dma((8,)),
        ],
        compiler_params=pltpu.CompilerParams(vmem_limit_bytes=62 * 2**20),
    )(
        tokens.reshape(TOK, MODEL), cotangent.reshape(TOK, MODEL),
        out, gn_sum, norm_gain, d_rows, arecv, ln_sums,
    )
    return (
        out.reshape(tokens.shape),
        d_tok.reshape(tokens.shape),
        d_gain.reshape(32),
        d_shift.reshape(32),
        d_qkv,
        d_bqkv.reshape(96),
        d_out,
        d_up,
        d_bup.reshape(128),
        d_down,
        d_bout.reshape(32),
    )


def solution(mesh):
    in_specs = (
        P("batch", "seq", None),
        P(("seq", "batch")),
        P(("seq", "batch")),
        P(("seq", "batch"), None),
        P(("seq", "batch")),
        P(("seq", "batch"), None),
        P(("seq", "batch"), None),
        P(("seq", "batch")),
        P(("seq", "batch"), None),
        P(("seq", "batch")),
        P("batch", "seq", None),
    )
    out_specs = (
        P("batch", "seq", None),
        P("batch", "seq", None),
        P(("seq", "batch")),
        P(("seq", "batch")),
        P(("seq", "batch"), None),
        P(("seq", "batch")),
        P(("seq", "batch"), None),
        P(("seq", "batch"), None),
        P(("seq", "batch")),
        P(("seq", "batch"), None),
        P(("seq", "batch")),
    )
    fits = mesh.shape["seq"] == SEQ and mesh.shape["batch"] == 2
    body = fast_local if fits else local
    return jax.shard_map(body, mesh=mesh, in_specs=in_specs, out_specs=out_specs, check_vma=False)
```

```python
import math

import jax
import jax.numpy as jnp
import numpy as np
from jax import lax
from jax.experimental import pallas as pl
from jax.experimental.pallas import tpu as pltpu
from jax.sharding import PartitionSpec as P

HEADS = 16
ROTARY = 16


eps_norm = 1e-05
neg_big = -1e30
rotary_base = 10000.0


def rotary_tables(positions, half_width):
    frequency = rotary_base ** (
        -(2.0 * jnp.arange(half_width, dtype=jnp.float32)) / (2.0 * half_width)
    )
    angles = positions[:, None] * frequency[None, :]
    return (jnp.cos(angles)[:, None, :], jnp.sin(angles)[:, None, :])


def rotate(section, cosine_table, sine_table):
    half_width = cosine_table.shape[-1]
    first_half = section[..., :half_width]
    second_half = section[..., half_width : 2 * half_width]
    return jnp.concatenate(
        [
            first_half * cosine_table - second_half * sine_table,
            second_half * cosine_table + first_half * sine_table,
            section[..., 2 * half_width :],
        ],
        -1,
    )


def exact_gelu(values):
    return jax.nn.gelu(values, approximate=False)


def contract_rows(left, right):
    return lax.dot_general(
        left, right, (((0,), (0,)), ((), ())), preferred_element_type=jnp.float32
    )


def times_transposed(left, right):
    return lax.dot_general(
        left, right, (((1,), (1,)), ((), ())), preferred_element_type=jnp.float32
    )


def masked_scores(queries, key_rows, query_pos, key_pos, score_scale):
    scores = (
        jnp.einsum("qhd,khd->hqk", queries, key_rows, preferred_element_type=jnp.float32)
        * score_scale
    )
    allowed = key_pos[None, :] <= query_pos[:, None]
    return jnp.where(allowed[None], scores, neg_big)


def split_blocks(flat_rows, block_rows, head_count, head_dim):
    length = flat_rows.shape[0]
    return flat_rows.reshape(length // block_rows, block_rows, head_count, head_dim)


def attend(queries, key_all, value_all, query_pos, score_scale, block_rows):
    head_count, head_dim = (queries.shape[1], queries.shape[2])
    length = key_all.shape[0]
    key_blocks = split_blocks(key_all, block_rows, head_count, head_dim)
    value_blocks = split_blocks(value_all, block_rows, head_count, head_dim)
    position_blocks = jnp.arange(length, dtype=jnp.int32).reshape(length // block_rows, block_rows)

    def statistics(state_in, entry):
        running_max, running_sum = state_in
        key_rows, key_pos = entry
        scores = masked_scores(queries, key_rows, query_pos, key_pos, score_scale)
        new_max = jnp.maximum(running_max, jnp.max(scores, -1))
        running_sum = running_sum * jnp.exp(running_max - new_max) + jnp.sum(
            jnp.exp(scores - new_max[..., None]), -1
        )
        return ((new_max, running_sum), None)

    start_state = (
        jnp.full((head_count, queries.shape[0]), neg_big, jnp.float32),
        jnp.zeros((head_count, queries.shape[0]), jnp.float32),
    )
    (running_max, running_sum), _ = lax.scan(statistics, start_state, (key_blocks, position_blocks))
    log_total = running_max + jnp.log(running_sum)

    def attend_accumulate(mixed_heads, entry):
        key_rows, value_rows, key_pos = entry
        scores = masked_scores(queries, key_rows, query_pos, key_pos, score_scale)
        probs_low = jnp.exp(scores - log_total[..., None]).astype(jnp.bfloat16)
        return (
            mixed_heads
            + jnp.einsum("hqk,khd->qhd", probs_low, value_rows, preferred_element_type=jnp.float32),
            None,
        )

    mixed_heads, _ = lax.scan(
        attend_accumulate,
        jnp.zeros(queries.shape, jnp.float32),
        (key_blocks, value_blocks, position_blocks),
    )
    return (mixed_heads, log_total)


def query_grads(
    queries,
    grad_heads,
    key_all,
    value_all,
    log_total,
    delta_rows,
    query_pos,
    score_scale,
    block_rows,
):
    head_count, head_dim = (queries.shape[1], queries.shape[2])
    length = key_all.shape[0]
    key_blocks = split_blocks(key_all, block_rows, head_count, head_dim)
    value_blocks = split_blocks(value_all, block_rows, head_count, head_dim)
    position_blocks = jnp.arange(length, dtype=jnp.int32).reshape(length // block_rows, block_rows)

    def query_accumulate(grad_queries, entry):
        key_rows, value_rows, key_pos = entry
        scores = masked_scores(queries, key_rows, query_pos, key_pos, score_scale)
        probs = jnp.exp(scores - log_total[..., None])
        grad_probs = jnp.einsum(
            "qhd,khd->hqk", grad_heads, value_rows, preferred_element_type=jnp.float32
        )
        grad_scores = (probs * (grad_probs - delta_rows[..., None])).astype(jnp.bfloat16)
        return (
            grad_queries
            + jnp.einsum("hqk,khd->qhd", grad_scores, key_rows, preferred_element_type=jnp.float32),
            None,
        )

    grad_queries, _ = lax.scan(
        query_accumulate,
        jnp.zeros(queries.shape, jnp.float32),
        (key_blocks, value_blocks, position_blocks),
    )
    return grad_queries * score_scale


def key_terms(
    queries,
    grad_heads,
    log_total,
    delta_rows,
    query_pos,
    key_rows,
    value_rows,
    key_pos,
    score_scale,
):
    scores = masked_scores(queries, key_rows, query_pos, key_pos, score_scale)
    probs = jnp.exp(scores - log_total[..., None])
    grad_probs = jnp.einsum(
        "qhd,khd->hqk", grad_heads, value_rows, preferred_element_type=jnp.float32
    )
    grad_scores = (probs * (grad_probs - delta_rows[..., None])).astype(jnp.bfloat16)
    grad_keys = (
        jnp.einsum("hqk,qhd->khd", grad_scores, queries, preferred_element_type=jnp.float32)
        * score_scale
    )
    grad_values = jnp.einsum(
        "hqk,qhd->khd", probs.astype(jnp.bfloat16), grad_heads, preferred_element_type=jnp.float32
    )
    key_count = key_rows.shape[0]
    return jnp.concatenate(
        [grad_keys.reshape(key_count, -1), grad_values.reshape(key_count, -1)], -1
    )


def local(tokens, ln_gain, ln_bias, w_qkv, b_qkv, w_out, w_up, b_up, w_down, b_out, cotangent):
    seq_count, tok_rows, model_width = tokens.shape
    head_count = HEADS
    head_dim = model_width // head_count
    score_scale = head_dim ** (-0.5)
    length = tok_rows * lax.axis_size("seq")
    block_rows = math.gcd(length, 512)
    token_count = seq_count * tok_rows
    owned_shards = (ln_gain, ln_bias, w_qkv, b_qkv, w_out, w_up, b_up, w_down, b_out)
    norm_gain, norm_shift, wqkv, bqkv, wout, wup, bup, wdown, bout = (
        lax.all_gather(owned_shards[0], ("seq", "batch"), axis=0, tiled=True),
        lax.all_gather(owned_shards[1], ("seq", "batch"), axis=0, tiled=True),
        lax.all_gather(owned_shards[2], ("seq", "batch"), axis=0, tiled=True),
        lax.all_gather(owned_shards[3], ("seq", "batch"), axis=0, tiled=True),
        lax.all_gather(owned_shards[4], ("seq", "batch"), axis=0, tiled=True),
        lax.all_gather(owned_shards[5], ("seq", "batch"), axis=0, tiled=True),
        lax.all_gather(owned_shards[6], ("seq", "batch"), axis=0, tiled=True),
        lax.all_gather(owned_shards[7], ("seq", "batch"), axis=0, tiled=True),
        lax.all_gather(owned_shards[8], ("seq", "batch"), axis=0, tiled=True),
    )
    inputs = tokens.reshape(token_count, model_width).astype(jnp.float32)
    average = jnp.mean(inputs, -1, keepdims=True)
    centered = inputs - average
    inv_root = lax.rsqrt(jnp.mean(centered * centered, -1, keepdims=True) + eps_norm)
    unit_rows = centered * inv_root
    normed = (unit_rows * norm_gain.astype(jnp.float32) + norm_shift.astype(jnp.float32)).astype(
        jnp.bfloat16
    )
    joined_qkv = (
        jnp.dot(normed, wqkv, preferred_element_type=jnp.float32) + bqkv.astype(jnp.float32)
    ).reshape(seq_count, tok_rows, 3, head_count, head_dim)
    query_pos = lax.axis_index("seq") * tok_rows + jnp.arange(tok_rows, dtype=jnp.int32)
    cosine_table, sine_table = rotary_tables(query_pos.astype(jnp.float32), ROTARY // 2)
    queries = rotate(joined_qkv[:, :, 0], cosine_table, sine_table).astype(jnp.bfloat16)
    key_local = rotate(joined_qkv[:, :, 1], cosine_table, sine_table).astype(jnp.bfloat16)
    value_local = joined_qkv[:, :, 2].astype(jnp.bfloat16)
    key_all, value_all = (
        lax.all_gather(
            key_local.reshape(seq_count, tok_rows, model_width), "seq", axis=1, tiled=True
        ),
        lax.all_gather(
            value_local.reshape(seq_count, tok_rows, model_width), "seq", axis=1, tiled=True
        ),
    )

    def forward_sequence(entry):
        query_seq, key_seq, value_seq = entry
        return attend(query_seq, key_seq, value_seq, query_pos, score_scale, block_rows)

    mixed_heads, log_total = lax.map(forward_sequence, (queries, key_all, value_all))
    mixed_low = mixed_heads.reshape(token_count, model_width).astype(jnp.bfloat16)
    attn_out = jnp.dot(mixed_low, wout, preferred_element_type=jnp.float32)
    up_proj = jnp.dot(normed, wup, preferred_element_type=jnp.float32) + bup.astype(jnp.float32)
    activation = exact_gelu(up_proj).astype(jnp.bfloat16)
    mlp_out = jnp.dot(activation, wdown, preferred_element_type=jnp.float32)
    result = (inputs + attn_out + mlp_out + bout.astype(jnp.float32)).astype(jnp.bfloat16)
    norm_gain, norm_shift, wqkv, bqkv, wout, wup, bup, wdown, bout = (
        lax.all_gather(owned_shards[0], ("seq", "batch"), axis=0, tiled=True),
        lax.all_gather(owned_shards[1], ("seq", "batch"), axis=0, tiled=True),
        lax.all_gather(owned_shards[2], ("seq", "batch"), axis=0, tiled=True),
        lax.all_gather(owned_shards[3], ("seq", "batch"), axis=0, tiled=True),
        lax.all_gather(owned_shards[4], ("seq", "batch"), axis=0, tiled=True),
        lax.all_gather(owned_shards[5], ("seq", "batch"), axis=0, tiled=True),
        lax.all_gather(owned_shards[6], ("seq", "batch"), axis=0, tiled=True),
        lax.all_gather(owned_shards[7], ("seq", "batch"), axis=0, tiled=True),
        lax.all_gather(owned_shards[8], ("seq", "batch"), axis=0, tiled=True),
    )
    cotangent_rows = cotangent.reshape(token_count, model_width)
    cotangent_f = cotangent_rows.astype(jnp.float32)
    grad_bout = jnp.sum(cotangent_f, 0)
    grad_wout = contract_rows(mixed_low, cotangent_rows)
    grad_wdown = contract_rows(activation, cotangent_rows)
    grad_act = times_transposed(cotangent_rows, wdown)
    _, gelu_back = jax.vjp(exact_gelu, up_proj)
    grad_up = gelu_back(grad_act)[0].astype(jnp.bfloat16)
    grad_wup = contract_rows(normed, grad_up)
    grad_bup = jnp.sum(grad_up.astype(jnp.float32), 0)
    grad_heads = (
        times_transposed(cotangent_rows, wout)
        .astype(jnp.bfloat16)
        .reshape(seq_count, tok_rows, head_count, head_dim)
    )
    delta_rows = jnp.swapaxes(jnp.sum(grad_heads.astype(jnp.float32) * mixed_heads, -1), 1, 2)

    def backward_sequence(entry):
        query_seq, grad_seq, key_seq, value_seq, total_seq, delta_seq = entry
        return query_grads(
            query_seq,
            grad_seq,
            key_seq,
            value_seq,
            total_seq,
            delta_seq,
            query_pos,
            score_scale,
            block_rows,
        )

    grad_queries = lax.map(
        backward_sequence, (queries, grad_heads, key_all, value_all, log_total, delta_rows)
    )
    row_count = tok_rows * lax.axis_size("seq")
    sub_rows = math.gcd(row_count, 512)

    def one_block(block_index):
        first_key = block_index * sub_rows
        key_pos = first_key + jnp.arange(sub_rows, dtype=jnp.int32)

        def one_sequence(entry):
            query_seq, grad_seq, total_seq, delta_seq, key_seq, value_seq = entry
            key_rows = lax.dynamic_slice_in_dim(key_seq, first_key, sub_rows, 0).reshape(
                sub_rows, head_count, head_dim
            )
            value_rows = lax.dynamic_slice_in_dim(value_seq, first_key, sub_rows, 0).reshape(
                sub_rows, head_count, head_dim
            )
            return key_terms(
                query_seq,
                grad_seq,
                total_seq,
                delta_seq,
                query_pos,
                key_rows,
                value_rows,
                key_pos,
                score_scale,
            )

        per_sequence = lax.map(
            one_sequence, (queries, grad_heads, log_total, delta_rows, key_all, value_all)
        )
        return jnp.swapaxes(per_sequence, 0, 1)

    block_terms = lax.map(one_block, jnp.arange(row_count // sub_rows, dtype=jnp.int32))
    summed = lax.psum_scatter(
        block_terms.reshape(row_count, seq_count, 2 * model_width).astype(jnp.bfloat16),
        "seq",
        scatter_dimension=0,
        tiled=True,
    ).astype(jnp.float32)
    key_grads_all = jnp.swapaxes(summed, 0, 1)
    grad_keys = key_grads_all[..., :model_width].reshape(seq_count, tok_rows, head_count, head_dim)
    grad_values = key_grads_all[..., model_width:].reshape(
        seq_count, tok_rows, head_count, head_dim
    )
    grad_q_turned = rotate(grad_queries, cosine_table, -sine_table)
    grad_k_turned = rotate(grad_keys, cosine_table, -sine_table)
    grad_joined = (
        jnp.stack([grad_q_turned, grad_k_turned, grad_values], 2)
        .reshape(token_count, 3 * model_width)
        .astype(jnp.bfloat16)
    )
    grad_wqkv = contract_rows(normed, grad_joined)
    grad_bqkv = jnp.sum(grad_joined.astype(jnp.float32), 0)
    grad_normed = times_transposed(grad_joined, wqkv) + times_transposed(grad_up, wup)
    grad_gain = jnp.sum(grad_normed * unit_rows, 0)
    grad_shift = jnp.sum(grad_normed, 0)
    grad_unit = grad_normed * norm_gain.astype(jnp.float32)
    grad_inputs = cotangent_f + inv_root * (
        grad_unit
        - jnp.mean(grad_unit, -1, keepdims=True)
        - unit_rows * jnp.mean(grad_unit * unit_rows, -1, keepdims=True)
    )
    owner_grads = (
        lax.psum_scatter(grad_gain, ("seq", "batch"), scatter_dimension=0, tiled=True),
        lax.psum_scatter(grad_shift, ("seq", "batch"), scatter_dimension=0, tiled=True),
        lax.psum_scatter(grad_wqkv, ("seq", "batch"), scatter_dimension=0, tiled=True),
        lax.psum_scatter(grad_bqkv, ("seq", "batch"), scatter_dimension=0, tiled=True),
        lax.psum_scatter(grad_wout, ("seq", "batch"), scatter_dimension=0, tiled=True),
        lax.psum_scatter(grad_wup, ("seq", "batch"), scatter_dimension=0, tiled=True),
        lax.psum_scatter(grad_bup, ("seq", "batch"), scatter_dimension=0, tiled=True),
        lax.psum_scatter(grad_wdown, ("seq", "batch"), scatter_dimension=0, tiled=True),
        lax.psum_scatter(grad_bout, ("seq", "batch"), scatter_dimension=0, tiled=True),
    )
    return (
        result.reshape(seq_count, tok_rows, model_width),
        grad_inputs.reshape(seq_count, tok_rows, model_width),
        owner_grads[0],
        owner_grads[1],
        owner_grads[2],
        owner_grads[3],
        owner_grads[4],
        owner_grads[5],
        owner_grads[6],
        owner_grads[7],
        owner_grads[8],
    )


MESH = pl.DeviceIdType.MESH
F32, BF16 = jnp.float32, jnp.bfloat16
TOK = 128
BT = 256
MODEL = 1024
SEQ = 16
CHIPS = 8
UP = 256
HD = 64
WIDE = 512
VEC = 448
GRADS = 448


def dot(left, right):
    return jnp.dot(left, right, preferred_element_type=F32)


def dot_nt(left, right):
    return lax.dot_general(left, right, (((1,), (1,)), ((), ())), preferred_element_type=F32)


def lanes(block):
    if isinstance(block, int):
        return slice(block * BT, (block + 1) * BT)
    return pl.ds(pl.multiple_of(block * BT, BT), BT)


def turn(rows, cosine, sine):
    first, second = rows[0:8], rows[8:16]
    return jnp.concatenate(
        [first * cosine - second * sine, second * cosine + first * sine, rows[16:]], 0
    )


def remote(src, dst, send_sem, recv_sem, device):
    return pltpu.make_async_remote_copy(
        src_ref=src,
        dst_ref=dst,
        send_sem=send_sem,
        recv_sem=recv_sem,
        device_id=device,
        device_id_type=MESH,
    )


def fused(
    tokens, cot, w_qkv, w_out, w_up, w_down, gain, shift, bout, bup, bqkv, cost, sint,
    out, gn_sum, norm_gain, d_rows, arecv, ln_sums,
    tok, g, wsend, wc, wct, wd, gv, bct, normed, unit, amt, dactt, qt, kt, vt, k, v, sbuf, e,
    linv, ot, gt, dost, delta, dkt, dvt, part1, rc1, ry1, rzl1, rzr1, rc2, ry2, rzl2, rzr2, tmp,
    dgain, dshift, dbout, dwct, dwd, dsend, drecv, dws, xrecv, vsend, vrecv, vparts,
    w_ss, w_rs, x_ss, x_rs, wd_ss, wd_rs, t_ss, t_rs, g_ss, g_rs,
    c1_ss, c1_rs, y1_ss, y1_rs, zp1_ss, zl1_rs, zm1_ss, zr1_rs,
    c2_ss, c2_rs, y2_ss, y2_rs, zp2_ss, zl2_rs, zm2_ss, zr2_rs,
    d_ss, d_rs, dx_ss, dx_rs, a_ss, a_rs, vx_ss, vx_rs, v_ss, v_rs,
):
    s = lax.axis_index("seq")
    b = lax.axis_index("batch")
    z, y, c = s // 4, (s // 2) % 2, s % 2
    oy, oc, ob = 1 - y, 1 - c, 1 - b
    sib = (s + 1 - 2 * c, b)
    yn = (s + 2 - 4 * y, b)
    zp = (lax.rem(s + 4, SEQ), b)
    zm = (lax.rem(s + SEQ - 4, SEQ), b)
    xn = (s, ob)
    offsets = [(dz, dy, dc) for dz in (0, 1, 3, 2) for dy in (0, 1) for dc in (0, 1)][1:]

    def shifted(offset, sign):
        dz, dy, dc = offset
        return (
            4 * lax.rem(z + 4 + sign * dz, 4)
            + 2 * lax.rem(y + 2 + sign * dy, 2)
            + lax.rem(c + 2 + sign * dc, 2)
        )

    high = z // 2
    zo = [z, z + 1 - 2 * lax.rem(z, 2), 2 - high, 3 - 3 * high]
    inner = jnp.logical_and(z > 0, z < 3)
    outer = jnp.logical_or(z == 0, z == 3)

    def mid(*steps):
        @pl.when(inner)
        def _():
            for step in steps:
                step[0](*step[1:])

    def end(*steps):
        @pl.when(outer)
        def _():
            for step in steps:
                step[0](*step[1:])

    def both(*steps):
        for step in steps:
            step[0](*step[1:])

    barrier = pltpu.get_barrier_semaphore()
    for off in offsets:
        pl.semaphore_signal(
            barrier, inc=1, device_id=(shifted(off, 1), b), device_id_type=MESH
        )
    pl.semaphore_signal(barrier, inc=1, device_id=xn, device_id_type=MESH)

    vectors = [gain[...], shift[...], bout[...]]
    vectors += [bup[:, 32 * i : 32 * (i + 1)] for i in range(4)]
    vectors += [bqkv[:, 32 * i : 32 * (i + 1)] for i in range(3)]
    vec = jnp.concatenate([w.astype(F32) for w in vectors] + [jnp.zeros((6, 32), F32)], 0).T
    vec = jnp.concatenate([vec, jnp.zeros((32, HD - 16), F32)], 1).astype(BF16)
    for t in range(SEQ):
        wsend[t] = jnp.concatenate(
            [
                w_up[:, UP * t : UP * (t + 1)],
                w_qkv[:, HD * t : HD * (t + 1)],
                w_qkv[:, MODEL + HD * t : MODEL + HD * (t + 1)],
                w_qkv[:, 2 * MODEL + HD * t : 2 * MODEL + HD * (t + 1)],
                vec,
            ],
            1,
        )
    wc[2 * s + b] = wsend[s]
    tok[s] = tokens[...]
    g[s] = cot[...]
    down_own = pl.ds(pl.multiple_of(128 * b, 128), 128)
    down_other = pl.ds(pl.multiple_of(128 * ob, 128), 128)
    out_own = pl.ds(pl.multiple_of(UP + 32 * b, 32), 32)
    out_other = pl.ds(pl.multiple_of(UP + 32 * ob, 32), 32)
    wd[down_own] = w_down[...]
    wd[out_own] = w_out[...]
    pl.semaphore_wait(barrier, SEQ)

    def w_copy(source, target):
        return remote(
            wsend.at[target], wc.at[2 * source + b], w_ss.at[target], w_rs.at[source], (target, b)
        )

    def x_copy(source, plane):
        return remote(
            wc.at[2 * source + plane], wc.at[2 * source + plane],
            x_ss.at[source], x_rs.at[source], xn,
        )

    wd_copies = [
        remote(w_down, wd.at[down_own], wd_ss.at[0], wd_rs.at[0], xn),
        remote(w_out, wd.at[out_own], wd_ss.at[1], wd_rs.at[1], xn),
    ]

    def gather(buf, ss, rs):
        def send(shard, way, device):
            return remote(buf.at[shard], buf.at[shard], ss.at[way, shard], rs.at[shard], device)

        def arrived(shard):
            send(shard, 0, sib).wait_recv()

        def on_own_z(act):
            @pl.when(z < 3)
            def _():
                act(send(s, 0, zp))

            @pl.when(z > 0)
            def _():
                act(send(s, 1, zm))

        def on_own_y(act):
            act(send(s, 2, yn))
            act(send(s, 3, sib))

        def own_z():
            on_own_z(start)

        def own_y():
            on_own_y(start)

        def on_z(t, act):
            shard = 4 * zo[t] + 2 * y + c

            @pl.when(jnp.logical_and(zo[t] < z, z < 3))
            def _():
                act(send(shard, 0, zp))

            @pl.when(jnp.logical_and(zo[t] > z, z > 0))
            def _():
                act(send(shard, 1, zm))

            act(send(shard, 2, yn))
            act(send(shard, 3, sib))

        def on_y(t, act):
            act(send(4 * zo[t] + 2 * oy + c, 3, sib))

        start = lambda copy: copy.start()
        finish = lambda copy: copy.wait_send()

        def step_z(t):
            arrived(4 * zo[t] + 2 * y + c)
            on_z(t, start)

        def step_y(t):
            arrived(4 * zo[t] + 2 * oy + c)
            on_y(t, start)

        def step_core(t, row):
            arrived(4 * zo[t] + 2 * row + oc)

        def drain():
            on_own_z(finish)
            on_own_y(finish)
            for t in range(1, 4):
                on_z(t, finish)
            for t in range(4):
                on_y(t, finish)

        return own_z, own_y, step_z, step_y, step_core, drain

    tok_oz, tok_oy, tok_z, tok_y, tok_core, tok_drain = gather(tok, t_ss, t_rs)
    g_oz, g_oy, g_z, g_y, g_core, g_drain = gather(g, g_ss, g_rs)

    def w_send():
        for off in offsets:
            w_copy(s, shifted(off, 1)).start()

    def w_arrive(lo, hi):
        for off in offsets[lo:hi]:
            source = shifted(off, -1)
            w_copy(source, s).wait_recv()
            x_copy(source, b).start()

    both((tok_oz,), (tok_oy,))
    for off in offsets: w_copy(s, shifted(off, 1)).start()
    x_copy(s, b).start()
    mid((tok_z, 1), (tok_z, 2), (tok_y, 0))
    end((tok_z, 1), (tok_y, 0))
    both((g_oy,))
    end((g_oz,))
    both((w_arrive, 0, 7))
    both((w_arrive, 7, 15))
    mid((tok_z, 3), (g_oz,), (tok_y, 1))
    end((tok_z, 2), (tok_y, 1))
    for copy in wd_copies: copy.start()
    for t in range(SEQ): x_copy(t, ob).wait_recv()
    wct[...] = wc[...].reshape(MODEL, WIDE).T
    rows = wct[VEC : VEC + 16, :].astype(F32)
    gv[0:1] = rows[0:1]
    gv[1:2] = rows[1:2]
    gv[2:3] = rows[2:3]
    cols = []
    for half in range(2):
        tail = wc[2 * s + half][:, VEC - HD :].astype(F32)
        for i in range(4):
            cols.append(tail[:, HD + 3 + i : HD + 4 + i])
    lane_of = lax.broadcasted_iota(jnp.int32, (32, 128), 1)
    for which in range(3):
        for half in range(2):
            chunk = 32 * which + 2 * s + half
            tail = wc[chunk // 3][:, VEC - HD :].astype(F32)
            cols.append(
                jnp.sum(jnp.where(lane_of == HD + 7 + lax.rem(chunk, 3), tail, 0.0), 1, keepdims=True)
            )
    bct[...] = jnp.concatenate(cols, 0)

    def project(i):
        x = tok[pl.ds(2 * i, 2)].reshape(BT, MODEL).astype(F32)
        centered = x - jnp.mean(x, -1, keepdims=True)
        inv = lax.rsqrt(jnp.mean(centered * centered, -1, keepdims=True) + eps_norm)
        u = centered * inv
        n = (u * gv[0:1] + gv[1:2]).astype(BF16)
        normed[i] = n
        unit[i] = u.astype(BF16)
        jt = dot_nt(wct[0:VEC], n) + bct[...]
        up = jt[0:UP]
        half = 0.5 + 0.5 * lax.erf(up * 0.7071067811865476)
        at = lanes(i)
        amt[0:UP, at] = (up * half).astype(BF16)
        dactt[:, at] = half + up * (jnp.exp(-0.5 * up * up) * 0.3989422804014327)
        cs, sn = cost[:, at], sint[:, at]
        qt[:, at] = (turn(jt[256:320], cs, sn) * 0.125).astype(BF16)
        keys = turn(jt[320:384], cs, sn)
        kt[:, at] = keys.astype(BF16)
        vt[:, at] = jt[384:448].astype(BF16)
        k[i] = keys.T.astype(BF16)
        v[i] = jt[384:448].T.astype(BF16)

    def chip_of(t, row):
        return 2 * zo[t] + row

    def proj(t, row):
        tok_core(t, row)
        project(chip_of(t, row))

    both((proj, 0, y), (proj, 0, oy), (proj, 1, y))
    both((proj, 1, oy))
    end((tok_z, 3), (g_y, 0))
    mid((g_z, 1), (g_y, 0), (tok_y, 2))
    both((proj, 2, y))
    mid((g_z, 2))
    end((tok_y, 2))
    both((proj, 2, oy))
    both((proj, 3, y))
    end((g_z, 1))
    both((tok_y, 3), (proj, 3, oy))
    mid((g_z, 3))

    def e_put(n, block):
        m, at = 2 * (n // 4), 256 * (n % 4)
        e[m : m + 2, :, at : at + 256] = block.reshape(2, TOK, BT)

    def e_get(n):
        m, at = 2 * (n // 4), 256 * (n % 4)
        return e[m : m + 2, :, at : at + 256].reshape(BT, BT)

    def attend_fwd(qb):
        at = lanes(qb)
        base = qb * (qb + 1) // 2
        q = qt[:, at]
        top = None
        for kb in range(qb + 1):
            st = dot(k[kb], q)
            if kb == qb:
                key_at = lax.broadcasted_iota(jnp.int32, (BT, BT), 0)
                query_at = lax.broadcasted_iota(jnp.int32, (BT, BT), 1)
                st = jnp.where(key_at <= query_at, st, neg_big)
            sbuf[kb] = st
            here = jnp.max(st, 0, keepdims=True)
            top = here if top is None else jnp.maximum(top, here)
        total = jnp.zeros((1, BT), F32)
        o = jnp.zeros((HD, BT), F32)
        for kb in range(qb + 1):
            ee = jnp.exp(sbuf[kb] - top)
            total = total + jnp.sum(ee, 0, keepdims=True)
            eb = ee.astype(BF16)
            e_put(base + kb, eb)
            o = o + dot(vt[:, lanes(kb)], eb)
        li = 1.0 / total
        linv[:, at] = li
        o = o * li
        ot[:, at] = o
        amt[UP : UP + HD, at] = o.astype(BF16)

    def reducer(part, rc, ry, rzl, rzr, c_ss, c_rs, y_ss, y_rs, zp_ss, zl_rs, zm_ss, zr_rs):
        order = [zo[3], zo[2], zo[1], zo[0]]

        def core_copy(t, row, color):
            chip = 2 * order[t] + row
            return remote(
                part.at[2 * chip + color], rc.at[chip], c_ss.at[chip], c_rs.at[chip], sib
            )

        def y_copy(t, row):
            return remote(
                rc.at[2 * order[t] + row], ry.at[order[t]], y_ss.at[order[t]], y_rs.at[order[t]], yn
            )

        def zp_copy(t):
            at = order[t]
            return remote(rc.at[2 * at + y], rzl.at[at], zp_ss.at[at], zl_rs.at[at], zp)

        def zm_copy(t):
            at = order[t]
            return remote(rc.at[2 * at + y], rzr.at[at], zm_ss.at[at], zr_rs.at[at], zm)

        def send_core(t, row):
            core_copy(t, row, oc).start()

        def send_y(t):
            chip = 2 * order[t] + oy
            core_copy(t, oy, oc).wait_recv()
            rc[chip] = (rc[chip].astype(F32) + part[2 * chip + c].astype(F32)).astype(BF16)
            y_copy(t, oy).start()

        def sum_here(t):
            chip = 2 * order[t] + y
            core_copy(t, y, oc).wait_recv()
            y_copy(t, y).wait_recv()
            tmp[...] = (
                rc[chip].astype(F32) + part[2 * chip + c].astype(F32) + ry[order[t]].astype(F32)
            )

        def add_left(t):
            zp_copy(t).wait_recv()
            tmp[...] += rzl[order[t]].astype(F32)

        def add_right(t):
            zm_copy(t).wait_recv()
            tmp[...] += rzr[order[t]].astype(F32)

        def pass_on(t):
            at = order[t]
            sum_here(t)

            @pl.when(jnp.logical_and(at > z, z > 0))
            def _():
                add_left(t)

            @pl.when(jnp.logical_and(at < z, z < 3))
            def _():
                add_right(t)

            rc[2 * at + y] = tmp[...].astype(BF16)

            @pl.when(at > z)
            def _():
                zp_copy(t).start()

            @pl.when(at < z)
            def _():
                zm_copy(t).start()

        def last():
            sum_here(3)

            @pl.when(z > 0)
            def _():
                add_left(3)

            @pl.when(z < 3)
            def _():
                add_right(3)

        def drain_core():
            for t in range(4):
                for row in (oy, y):
                    core_copy(t, row, oc).wait_send()

        def drain():
            for t in range(4):
                y_copy(t, oy).wait_send()
            for t in range(3):
                at = order[t]

                @pl.when(at > z)
                def _():
                    zp_copy(t).wait_send()

                @pl.when(at < z)
                def _():
                    zm_copy(t).wait_send()

        return order, send_core, send_y, pass_on, last, drain_core, drain

    order, core1, y1, pass1, last1, drain_core1, drain1 = reducer(
        part1, rc1, ry1, rzl1, rzr1, c1_ss, c1_rs, y1_ss, y1_rs, zp1_ss, zl1_rs, zm1_ss, zr1_rs
    )
    _, core2, y2, pass2, last2, drain_core2, drain2 = reducer(
        e, rc2, ry2, rzl2, rzr2, c2_ss, c2_rs, y2_ss, y2_rs, zp2_ss, zl2_rs, zm2_ss, zr2_rs
    )

    def out_block(t, row):
        i = 2 * order[t] + row
        part1[pl.ds(2 * i, 2)] = (
            dot(amt[:, lanes(i)].T, wd[...]).astype(BF16).reshape(2, TOK, MODEL)
        )
        core1(t, row)

    def grads_at(i):
        gb = g[pl.ds(2 * i, 2)].reshape(BT, MODEL)
        at = lanes(i)
        r = dot_nt(wd[...], gb)
        gt[0:UP, at] = (r[0:UP] * dactt[:, at]).astype(BF16)
        li = linv[:, at]
        gm = r[UP : UP + HD]
        dost[:, at] = (gm * li).astype(BF16)
        delta[:, at] = jnp.sum(gm * ot[:, at], 0, keepdims=True) * li
        dbout[...] += jnp.sum(gb.astype(F32).reshape(BT // 8, 8, MODEL), 0)

    def attend_bwd(qb):
        at = lanes(qb)
        base = qb * (qb + 1) // 2
        do, q, de = dost[:, at], qt[:, at], delta[:, at]
        dq = jnp.zeros((HD, BT), F32)
        for kb in range(qb + 1):
            ks = lanes(kb)
            eb = e_get(base + kb)
            dp = dot(v[kb], do)
            ds = (eb.astype(F32) * (dp - de)).astype(BF16)
            dv = dot_nt(do, eb)
            dk = dot_nt(q, ds)
            if kb == qb:
                dvt[:, ks] = dv
                dkt[:, ks] = dk
            else:
                dvt[:, ks] += dv
                dkt[:, ks] += dk
            dq = dq + dot(kt[:, ks], ds)
        gt[256:320, at] = turn(dq * 0.125, cost[:, at], -sint[:, at]).astype(BF16)

    def norm_grads(t, row):
        i = 2 * order[t] + row
        gn = dot(gt[:, lanes(i)].T, wct[0:GRADS])
        e[pl.ds(2 * i, 2)] = gn.astype(BF16).reshape(2, TOK, MODEL)
        core2(t, row)
        dshift[...] += jnp.sum(gn.reshape(BT // 8, 8, MODEL), 0)
        dgain[...] += jnp.sum((gn * unit[i].astype(F32)).reshape(BT // 8, 8, MODEL), 0)

    dgain[...] = jnp.zeros_like(dgain)
    dshift[...] = jnp.zeros_like(dshift)
    dbout[...] = jnp.zeros_like(dbout)

    def wd_arrive():
        for copy in wd_copies:
            copy.wait_send()
        remote(w_down, wd.at[down_other], wd_ss.at[0], wd_rs.at[0], xn).wait_recv()
        remote(w_out, wd.at[out_other], wd_ss.at[1], wd_rs.at[1], xn).wait_recv()

    def fwd(lo, hi):
        for qb in range(lo, hi):
            attend_fwd(qb)

    def grads(t, row):
        g_core(t, row)
        grads_at(chip_of(t, row))

    def bwd(lo, hi):
        for qb in range(lo, hi):
            attend_bwd(qb)

    def bwd_keys():
        gt[320:384, :] = turn(dkt[...], cost[...], -sint[...]).astype(BF16)
        gt[384:448, :] = dvt[...].astype(BF16)

    dx_copies = [remote(dws.at[p, ob], xrecv.at[p], dx_ss.at[p], dx_rs.at[p], xn) for p in range(2)]

    def turn_out(p, extra):
        for j in range(2 * SEQ // 4):
            turned = dwct[256 * p : 256 * (p + 1), 128 * j : 128 * (j + 1)].T
            for i in range(4):
                piece = turned[32 * i : 32 * (i + 1)]
                dev = 4 * j + i
                at = dws.at[p, dev % 2, dev // 2]
                if extra is None:
                    at[...] = piece.astype(BF16)
                else:
                    at[:, 0:128] = piece[:, 0:128].astype(BF16)
                    at[:, 128:256] = (piece[:, 128:256] + extra).astype(BF16)
        dx_copies[p].start()

    def up_grads():
        nn = normed.reshape(SEQ * TOK, MODEL)
        for n in range(4):
            dwct[0:256, lanes(n)] = dot(gt[0:256], nn[:, lanes(n)])
        turn_out(0, None)

    def qkv_grads():
        nn = normed.reshape(SEQ * TOK, MODEL)
        for n in range(4):
            dwct[256:GRADS, lanes(n)] = dot(gt[256:GRADS], nn[:, lanes(n)])
        dwct[GRADS:WIDE] = jnp.zeros((WIDE - GRADS, MODEL), F32)
        dwct[VEC : VEC + 1] = jnp.sum(dbout[...], 0, keepdims=True)
        bias_col = jnp.sum(gt[...].astype(F32), 1, keepdims=True)
        turn_out(
            1,
            jnp.concatenate(
                [jnp.zeros((32, HD + 1), F32)]
                + [bias_col[32 * n : 32 * (n + 1)] for n in range(14)]
                + [jnp.zeros((32, 128 - HD - 15), F32)],
                1,
            ),
        )

    vx_copy = remote(vsend, vrecv, vx_ss, vx_rs, xn)

    def ln_grads():
        vsend[0:1] = jnp.sum(dgain[...], 0, keepdims=True)
        vsend[1:2] = jnp.sum(dshift[...], 0, keepdims=True)
        vsend[2:8] = jnp.zeros((6, MODEL), F32)
        vx_copy.start()

    d_copy = remote(dsend, drecv, d_ss, d_rs, xn)

    def down_grads():
        gg = g.reshape(SEQ * TOK, MODEL)
        for n in range(4):
            dwd[:, lanes(n)] = dot(amt[...], gg[:, lanes(n)])
        dsend[0:128] = dwd[down_other].astype(BF16)
        dsend[128:160] = dwd[out_other].astype(BF16)
        d_copy.start()

    def a_copy(p, source, target):
        return remote(
            dws.at[p, b, target], arecv.at[p, source], a_ss.at[p, target], a_rs.at[p, source],
            (target, b),
        )

    def wide_out(p):
        dx_copies[p].wait_recv()
        dws[p, b] = (dws[p, b].astype(F32) + xrecv[p].astype(F32)).astype(BF16)
        for off in offsets:
            a_copy(p, s, shifted(off, 1)).start()
        arecv[p, s] = dws[p, b, s]

    def end1():
        last1()
        out[...] = (tmp[...] + tokens[...].astype(F32) + gv[2:3]).astype(BF16)

    def v_copy(source, target):
        piece = pl.ds(pl.multiple_of(128 * (target // 2), 128), 128)
        return remote(
            vrecv.at[:, piece], vparts.at[source], v_ss.at[target], v_rs.at[source], (target, b)
        )

    def ln_out():
        vx_copy.wait()
        vrecv[...] += vsend[...]
        for off in offsets:
            v_copy(s, shifted(off, 1)).start()
        vparts[s] = vrecv[:, pl.ds(pl.multiple_of(128 * (s // 2), 128), 128)]

    def down_out():
        d_copy.wait_recv()
        d_rows[0:128] = dwd[down_own] + drecv[0:128].astype(F32)
        d_rows[128:160] = dwd[out_own] + drecv[128:160].astype(F32)
        norm_gain[...] = gv[...]

    def ln_arrive():
        for off in offsets:
            v_copy(shifted(off, -1), s).wait_recv()
        ln_sums[...] = jnp.sum(vparts[...], 0)

    def end2():
        last2()
        gn_sum[...] = tmp[...]

    def wide_arrive():
        for off in offsets:
            a_copy(0, shifted(off, -1), s).wait_recv()
            a_copy(1, shifted(off, -1), s).wait_recv()

    both((wd_arrive,), (fwd, 0, 5))
    mid((g_y, 1))
    end((g_z, 2))
    both((fwd, 5, 8))
    end((g_y, 1))
    both((grads, 0, y), (out_block, 0, oy), (out_block, 1, oy), (out_block, 2, oy), (out_block, 3, oy))
    end((g_z, 3))
    both((y1, 0), (y1, 1), (y1, 2), (y1, 3))
    both((out_block, 0, y), (out_block, 1, y), (out_block, 2, y), (out_block, 3, y))
    both((grads, 0, oy), (grads, 1, y), (grads, 1, oy), (grads, 2, y), (g_y, 2), (grads, 2, oy), (grads, 3, y))
    both((g_y, 3), (grads, 3, oy))
    both((up_grads,))
    end((pass1, 0))
    both((bwd, 0, 8), (bwd_keys,))
    end((pass1, 1))
    both((qkv_grads,))
    both((wide_out, 0))
    both((norm_grads, 0, oy), (norm_grads, 1, oy), (norm_grads, 2, oy), (norm_grads, 3, oy))
    both((y2, 0), (y2, 1), (y2, 2), (y2, 3))
    end((pass1, 2))
    mid((pass1, 0))
    both((norm_grads, 0, y), (norm_grads, 1, y), (norm_grads, 2, y), (norm_grads, 3, y))
    mid((pass1, 1), (pass1, 2))
    both((ln_grads,), (down_grads,))
    both((wide_out, 1))
    both((end1,), (ln_out,), (pass2, 0))
    both((pass2, 1))
    both((down_out,))
    both((pass2, 2), (ln_arrive,), (end2,), (wide_arrive,))

    for off in offsets:
        w_copy(s, shifted(off, 1)).wait_send()
        a_copy(0, s, shifted(off, 1)).wait_send()
        a_copy(1, s, shifted(off, 1)).wait_send()
        v_copy(s, shifted(off, 1)).wait_send()
    for t in range(SEQ):
        x_copy(t, b).wait_send()
    tok_drain()
    g_drain()
    drain_core1()
    drain1()
    drain_core2()
    drain2()
    d_copy.wait_send()
    for copy in dx_copies:
        copy.wait_send()


def finish(
    tokens_h, cot_h, out_h, gn_sum_h, norm_gain_h, d_rows_h, arecv_h, ln_sums_h,
    out, d_tok, d_gain, d_shift, d_qkv, d_bqkv, d_out, d_up, d_bup, d_down, d_bout,
    tokens, cot, gn_sum, norm_gain, d_rows, arecv, ln_sums, sems,
):
    moves = [
        pltpu.make_async_copy(src, dst, sems.at[n])
        for n, (src, dst) in enumerate(
            [
                (gn_sum_h, gn_sum), (tokens_h, tokens), (norm_gain_h, norm_gain), (cot_h, cot),
                (arecv_h, arecv), (d_rows_h, d_rows), (ln_sums_h, ln_sums), (out_h, out),
            ]
        )
    ]
    for move in moves:
        move.start()
    for move in moves:
        move.wait()
    s = lax.axis_index("seq")
    b = lax.axis_index("batch")
    x = tokens[...].astype(F32)
    centered = x - jnp.mean(x, -1, keepdims=True)
    inv = lax.rsqrt(jnp.mean(centered * centered, -1, keepdims=True) + eps_norm)
    u = centered * inv
    gu = gn_sum[...] * norm_gain[0:1]
    d_tok[...] = cot[...].astype(F32) + inv * (
        gu - jnp.mean(gu, -1, keepdims=True) - u * jnp.mean(gu * u, -1, keepdims=True)
    )
    d_down[...] = d_rows[0:128]
    d_out[...] = d_rows[128:160]
    for t in range(0, SEQ, 2):
        even, odd = arecv[1, t].astype(F32), arecv[1, t + 1].astype(F32)
        d_up[:, UP * t : UP * (t + 1)] = arecv[0, t].astype(F32)
        d_up[:, UP * (t + 1) : UP * (t + 2)] = arecv[0, t + 1].astype(F32)
        for which in range(3):
            lo = HD * which
            d_qkv[:, MODEL * which + HD * t : MODEL * which + HD * (t + 2)] = jnp.concatenate(
                [even[:, lo : lo + HD], odd[:, lo : lo + HD]], 1
            )
    lane_of = lax.broadcasted_iota(jnp.int32, (32, 128), 1)

    def pick(block, lane):
        return jnp.sum(jnp.where(lane_of == lane, block, 0.0), 1, keepdims=True)

    mine = arecv[1, s][:, 128:256].astype(F32)
    picked = [mine[:, HD : HD + 1]]
    for i in range(4):
        picked.append(pick(mine, HD + 1 + 4 * b + i))
    for i in range(3):
        chunk = 3 * (2 * s + b) + i
        block = arecv[1, lax.rem(chunk, 32) // 2][:, 128:256].astype(F32)
        picked.append(pick(block, HD + 1 + 8 + 2 * (chunk // 32) + lax.rem(chunk, 2)))
    rows = jnp.concatenate(picked + [jnp.zeros((32, 120), F32)], 1).T
    d_bout[...] = rows[0:1]
    d_bup[...] = jnp.concatenate([rows[1 + i : 2 + i] for i in range(4)], 1)
    d_bqkv[...] = jnp.concatenate([rows[5 + i : 6 + i] for i in range(3)], 1)
    turned = pltpu.roll(ln_sums[...], lax.rem(128 - 32 * lax.rem(2 * s + b, 4), 128), 1)
    d_gain[...] = turned[0:1, 0:32]
    d_shift[...] = turned[1:2, 0:32]


def fast_local(
    tokens, ln_gain, ln_bias, w_qkv, b_qkv, w_out, w_up, b_up, w_down, b_out, cotangent
):
    length = SEQ * TOK
    frequency = rotary_base ** (-(2.0 * np.arange(8)) / 16.0)
    angles = frequency.astype(np.float32)[:, None] * np.arange(length, dtype=np.float32)[None]
    cost = jnp.asarray(np.cos(angles.astype(np.float64)).astype(np.float32))
    sint = jnp.asarray(np.sin(angles.astype(np.float64)).astype(np.float32))
    vm = pl.BlockSpec(memory_space=pltpu.VMEM)
    shape = jax.ShapeDtypeStruct
    dma = pltpu.SemaphoreType.DMA

    def reduce_buffers():
        return [
            pltpu.VMEM((CHIPS, TOK, MODEL), BF16),
            pltpu.VMEM((4, TOK, MODEL), BF16),
            pltpu.VMEM((4, TOK, MODEL), BF16),
            pltpu.VMEM((4, TOK, MODEL), BF16),
        ]

    reduce_sems = [dma((8,)), dma((8,))] + [dma((4,))] * 6
    results = pl.pallas_call(
        fused,
        out_shape=[
            shape((TOK, MODEL), BF16),
            shape((TOK, MODEL), F32),
            shape((8, MODEL), F32),
            shape((160, MODEL), F32),
            shape((2, SEQ, 32, 256), BF16),
            shape((8, 128), F32),
        ],
        in_specs=[vm] * 13,
        out_specs=[vm] * 6,
        scratch_shapes=[
            pltpu.VMEM((SEQ, TOK, MODEL), BF16),
            pltpu.VMEM((SEQ, TOK, MODEL), BF16),
            pltpu.VMEM((SEQ, 32, WIDE), BF16),
            pltpu.VMEM((2 * SEQ, 32, WIDE), BF16),
            pltpu.VMEM((WIDE, MODEL), BF16),
            pltpu.VMEM((UP + HD, MODEL), BF16),
            pltpu.VMEM((8, MODEL), F32),
            pltpu.VMEM((VEC, 1), F32),
            pltpu.VMEM((CHIPS, BT, MODEL), BF16),
            pltpu.VMEM((CHIPS, BT, MODEL), BF16),
            pltpu.VMEM((UP + HD, length), BF16),
            pltpu.VMEM((UP, length), F32),
            pltpu.VMEM((HD, length), BF16),
            pltpu.VMEM((HD, length), BF16),
            pltpu.VMEM((HD, length), BF16),
            pltpu.VMEM((CHIPS, BT, HD), BF16),
            pltpu.VMEM((CHIPS, BT, HD), BF16),
            pltpu.VMEM((CHIPS, BT, BT), F32),
            pltpu.VMEM((18, TOK, MODEL), BF16),
            pltpu.VMEM((1, length), F32),
            pltpu.VMEM((HD, length), F32),
            pltpu.VMEM((GRADS, length), BF16),
            pltpu.VMEM((HD, length), BF16),
            pltpu.VMEM((1, length), F32),
            pltpu.VMEM((HD, length), F32),
            pltpu.VMEM((HD, length), F32),
            pltpu.VMEM((SEQ, TOK, MODEL), BF16),
        ]
        + reduce_buffers()
        + reduce_buffers()
        + [
            pltpu.VMEM((TOK, MODEL), F32),
            pltpu.VMEM((8, MODEL), F32),
            pltpu.VMEM((8, MODEL), F32),
            pltpu.VMEM((8, MODEL), F32),
            pltpu.VMEM((WIDE, MODEL), F32),
            pltpu.VMEM((UP + HD, MODEL), F32),
            pltpu.VMEM((160, MODEL), BF16),
            pltpu.VMEM((160, MODEL), BF16),
            pltpu.VMEM((2, 2, SEQ, 32, 256), BF16),
            pltpu.VMEM((2, SEQ, 32, 256), BF16),
            pltpu.VMEM((8, MODEL), F32),
            pltpu.VMEM((8, MODEL), F32),
            pltpu.VMEM((SEQ, 8, 128), F32),
            dma((SEQ,)), dma((SEQ,)), dma((SEQ,)), dma((SEQ,)), dma((2,)), dma((2,)),
            dma((4, SEQ)), dma((SEQ,)), dma((4, SEQ)), dma((SEQ,)),
        ]
        + reduce_sems
        + reduce_sems
        + [dma, dma, dma((2,)), dma((2,)), dma((2, SEQ)), dma((2, SEQ)), dma, dma, dma((SEQ,)), dma((SEQ,))],
        compiler_params=pltpu.CompilerParams(
            collective_id=0, has_side_effects=True, vmem_limit_bytes=62 * 2**20
        ),
    )(
        tokens.reshape(TOK, MODEL), cotangent.reshape(TOK, MODEL),
        w_qkv, w_out, w_up, w_down,
        ln_gain.reshape(1, 32), ln_bias.reshape(1, 32), b_out.reshape(1, 32),
        b_up.reshape(1, 128), b_qkv.reshape(1, 96), cost, sint,
    )
    out, gn_sum, norm_gain, d_rows, arecv, ln_sums = results
    (out, d_tok, d_gain, d_shift, d_qkv, d_bqkv, d_out, d_up, d_bup, d_down, d_bout) = pl.pallas_call(
        finish,
        out_shape=[
            shape((TOK, MODEL), BF16),
            shape((TOK, MODEL), F32),
            shape((1, 32), F32),
            shape((1, 32), F32),
            shape((32, 3 * MODEL), F32),
            shape((1, 96), F32),
            shape((32, MODEL), F32),
            shape((32, 4 * MODEL), F32),
            shape((1, 128), F32),
            shape((128, MODEL), F32),
            shape((1, 32), F32),
        ],
        in_specs=[pl.BlockSpec(memory_space=pl.ANY)] * 8,
        out_specs=[vm] * 11,
        scratch_shapes=[
            pltpu.VMEM((TOK, MODEL), BF16),
            pltpu.VMEM((TOK, MODEL), BF16),
            pltpu.VMEM((TOK, MODEL), F32),
            pltpu.VMEM((8, MODEL), F32),
            pltpu.VMEM((160, MODEL), F32),
            pltpu.VMEM((2, SEQ, 32, 256), BF16),
            pltpu.VMEM((8, 128), F32),
            dma((8,)),
        ],
        compiler_params=pltpu.CompilerParams(vmem_limit_bytes=62 * 2**20),
    )(
        tokens.reshape(TOK, MODEL), cotangent.reshape(TOK, MODEL),
        out, gn_sum, norm_gain, d_rows, arecv, ln_sums,
    )
    return (
        out.reshape(tokens.shape),
        d_tok.reshape(tokens.shape),
        d_gain.reshape(32),
        d_shift.reshape(32),
        d_qkv,
        d_bqkv.reshape(96),
        d_out,
        d_up,
        d_bup.reshape(128),
        d_down,
        d_bout.reshape(32),
    )


def solution(mesh):
    in_specs = (
        P("batch", "seq", None),
        P(("seq", "batch")),
        P(("seq", "batch")),
        P(("seq", "batch"), None),
        P(("seq", "batch")),
        P(("seq", "batch"), None),
        P(("seq", "batch"), None),
        P(("seq", "batch")),
        P(("seq", "batch"), None),
        P(("seq", "batch")),
        P("batch", "seq", None),
    )
    out_specs = (
        P("batch", "seq", None),
        P("batch", "seq", None),
        P(("seq", "batch")),
        P(("seq", "batch")),
        P(("seq", "batch"), None),
        P(("seq", "batch")),
        P(("seq", "batch"), None),
        P(("seq", "batch"), None),
        P(("seq", "batch")),
        P(("seq", "batch"), None),
        P(("seq", "batch")),
    )
    fits = mesh.shape["seq"] == SEQ and mesh.shape["batch"] == 2
    body = fast_local if fits else local
    return jax.shard_map(body, mesh=mesh, in_specs=in_specs, out_specs=out_specs, check_vma=False)
```

```python
import math

import jax
import jax.numpy as jnp
import numpy as np
from jax import lax
from jax.experimental import pallas as pl
from jax.experimental.pallas import tpu as pltpu
from jax.sharding import PartitionSpec as P

HEADS = 16
ROTARY = 16


eps_norm = 1e-05
neg_big = -1e30
rotary_base = 10000.0


def rotary_tables(positions, half_width):
    frequency = rotary_base ** (
        -(2.0 * jnp.arange(half_width, dtype=jnp.float32)) / (2.0 * half_width)
    )
    angles = positions[:, None] * frequency[None, :]
    return (jnp.cos(angles)[:, None, :], jnp.sin(angles)[:, None, :])


def rotate(section, cosine_table, sine_table):
    half_width = cosine_table.shape[-1]
    first_half = section[..., :half_width]
    second_half = section[..., half_width : 2 * half_width]
    return jnp.concatenate(
        [
            first_half * cosine_table - second_half * sine_table,
            second_half * cosine_table + first_half * sine_table,
            section[..., 2 * half_width :],
        ],
        -1,
    )


def exact_gelu(values):
    return jax.nn.gelu(values, approximate=False)


def contract_rows(left, right):
    return lax.dot_general(
        left, right, (((0,), (0,)), ((), ())), preferred_element_type=jnp.float32
    )


def times_transposed(left, right):
    return lax.dot_general(
        left, right, (((1,), (1,)), ((), ())), preferred_element_type=jnp.float32
    )


def masked_scores(queries, key_rows, query_pos, key_pos, score_scale):
    scores = (
        jnp.einsum("qhd,khd->hqk", queries, key_rows, preferred_element_type=jnp.float32)
        * score_scale
    )
    allowed = key_pos[None, :] <= query_pos[:, None]
    return jnp.where(allowed[None], scores, neg_big)


def split_blocks(flat_rows, block_rows, head_count, head_dim):
    length = flat_rows.shape[0]
    return flat_rows.reshape(length // block_rows, block_rows, head_count, head_dim)


def attend(queries, key_all, value_all, query_pos, score_scale, block_rows):
    head_count, head_dim = (queries.shape[1], queries.shape[2])
    length = key_all.shape[0]
    key_blocks = split_blocks(key_all, block_rows, head_count, head_dim)
    value_blocks = split_blocks(value_all, block_rows, head_count, head_dim)
    position_blocks = jnp.arange(length, dtype=jnp.int32).reshape(length // block_rows, block_rows)

    def statistics(state_in, entry):
        running_max, running_sum = state_in
        key_rows, key_pos = entry
        scores = masked_scores(queries, key_rows, query_pos, key_pos, score_scale)
        new_max = jnp.maximum(running_max, jnp.max(scores, -1))
        running_sum = running_sum * jnp.exp(running_max - new_max) + jnp.sum(
            jnp.exp(scores - new_max[..., None]), -1
        )
        return ((new_max, running_sum), None)

    start_state = (
        jnp.full((head_count, queries.shape[0]), neg_big, jnp.float32),
        jnp.zeros((head_count, queries.shape[0]), jnp.float32),
    )
    (running_max, running_sum), _ = lax.scan(statistics, start_state, (key_blocks, position_blocks))
    log_total = running_max + jnp.log(running_sum)

    def attend_accumulate(mixed_heads, entry):
        key_rows, value_rows, key_pos = entry
        scores = masked_scores(queries, key_rows, query_pos, key_pos, score_scale)
        probs_low = jnp.exp(scores - log_total[..., None]).astype(jnp.bfloat16)
        return (
            mixed_heads
            + jnp.einsum("hqk,khd->qhd", probs_low, value_rows, preferred_element_type=jnp.float32),
            None,
        )

    mixed_heads, _ = lax.scan(
        attend_accumulate,
        jnp.zeros(queries.shape, jnp.float32),
        (key_blocks, value_blocks, position_blocks),
    )
    return (mixed_heads, log_total)


def query_grads(
    queries,
    grad_heads,
    key_all,
    value_all,
    log_total,
    delta_rows,
    query_pos,
    score_scale,
    block_rows,
):
    head_count, head_dim = (queries.shape[1], queries.shape[2])
    length = key_all.shape[0]
    key_blocks = split_blocks(key_all, block_rows, head_count, head_dim)
    value_blocks = split_blocks(value_all, block_rows, head_count, head_dim)
    position_blocks = jnp.arange(length, dtype=jnp.int32).reshape(length // block_rows, block_rows)

    def query_accumulate(grad_queries, entry):
        key_rows, value_rows, key_pos = entry
        scores = masked_scores(queries, key_rows, query_pos, key_pos, score_scale)
        probs = jnp.exp(scores - log_total[..., None])
        grad_probs = jnp.einsum(
            "qhd,khd->hqk", grad_heads, value_rows, preferred_element_type=jnp.float32
        )
        grad_scores = (probs * (grad_probs - delta_rows[..., None])).astype(jnp.bfloat16)
        return (
            grad_queries
            + jnp.einsum("hqk,khd->qhd", grad_scores, key_rows, preferred_element_type=jnp.float32),
            None,
        )

    grad_queries, _ = lax.scan(
        query_accumulate,
        jnp.zeros(queries.shape, jnp.float32),
        (key_blocks, value_blocks, position_blocks),
    )
    return grad_queries * score_scale


def key_terms(
    queries,
    grad_heads,
    log_total,
    delta_rows,
    query_pos,
    key_rows,
    value_rows,
    key_pos,
    score_scale,
):
    scores = masked_scores(queries, key_rows, query_pos, key_pos, score_scale)
    probs = jnp.exp(scores - log_total[..., None])
    grad_probs = jnp.einsum(
        "qhd,khd->hqk", grad_heads, value_rows, preferred_element_type=jnp.float32
    )
    grad_scores = (probs * (grad_probs - delta_rows[..., None])).astype(jnp.bfloat16)
    grad_keys = (
        jnp.einsum("hqk,qhd->khd", grad_scores, queries, preferred_element_type=jnp.float32)
        * score_scale
    )
    grad_values = jnp.einsum(
        "hqk,qhd->khd", probs.astype(jnp.bfloat16), grad_heads, preferred_element_type=jnp.float32
    )
    key_count = key_rows.shape[0]
    return jnp.concatenate(
        [grad_keys.reshape(key_count, -1), grad_values.reshape(key_count, -1)], -1
    )


def local(tokens, ln_gain, ln_bias, w_qkv, b_qkv, w_out, w_up, b_up, w_down, b_out, cotangent):
    seq_count, tok_rows, model_width = tokens.shape
    head_count = HEADS
    head_dim = model_width // head_count
    score_scale = head_dim ** (-0.5)
    length = tok_rows * lax.axis_size("seq")
    block_rows = math.gcd(length, 512)
    token_count = seq_count * tok_rows
    owned_shards = (ln_gain, ln_bias, w_qkv, b_qkv, w_out, w_up, b_up, w_down, b_out)
    norm_gain, norm_shift, wqkv, bqkv, wout, wup, bup, wdown, bout = (
        lax.all_gather(owned_shards[0], ("seq", "batch"), axis=0, tiled=True),
        lax.all_gather(owned_shards[1], ("seq", "batch"), axis=0, tiled=True),
        lax.all_gather(owned_shards[2], ("seq", "batch"), axis=0, tiled=True),
        lax.all_gather(owned_shards[3], ("seq", "batch"), axis=0, tiled=True),
        lax.all_gather(owned_shards[4], ("seq", "batch"), axis=0, tiled=True),
        lax.all_gather(owned_shards[5], ("seq", "batch"), axis=0, tiled=True),
        lax.all_gather(owned_shards[6], ("seq", "batch"), axis=0, tiled=True),
        lax.all_gather(owned_shards[7], ("seq", "batch"), axis=0, tiled=True),
        lax.all_gather(owned_shards[8], ("seq", "batch"), axis=0, tiled=True),
    )
    inputs = tokens.reshape(token_count, model_width).astype(jnp.float32)
    average = jnp.mean(inputs, -1, keepdims=True)
    centered = inputs - average
    inv_root = lax.rsqrt(jnp.mean(centered * centered, -1, keepdims=True) + eps_norm)
    unit_rows = centered * inv_root
    normed = (unit_rows * norm_gain.astype(jnp.float32) + norm_shift.astype(jnp.float32)).astype(
        jnp.bfloat16
    )
    joined_qkv = (
        jnp.dot(normed, wqkv, preferred_element_type=jnp.float32) + bqkv.astype(jnp.float32)
    ).reshape(seq_count, tok_rows, 3, head_count, head_dim)
    query_pos = lax.axis_index("seq") * tok_rows + jnp.arange(tok_rows, dtype=jnp.int32)
    cosine_table, sine_table = rotary_tables(query_pos.astype(jnp.float32), ROTARY // 2)
    queries = rotate(joined_qkv[:, :, 0], cosine_table, sine_table).astype(jnp.bfloat16)
    key_local = rotate(joined_qkv[:, :, 1], cosine_table, sine_table).astype(jnp.bfloat16)
    value_local = joined_qkv[:, :, 2].astype(jnp.bfloat16)
    key_all, value_all = (
        lax.all_gather(
            key_local.reshape(seq_count, tok_rows, model_width), "seq", axis=1, tiled=True
        ),
        lax.all_gather(
            value_local.reshape(seq_count, tok_rows, model_width), "seq", axis=1, tiled=True
        ),
    )

    def forward_sequence(entry):
        query_seq, key_seq, value_seq = entry
        return attend(query_seq, key_seq, value_seq, query_pos, score_scale, block_rows)

    mixed_heads, log_total = lax.map(forward_sequence, (queries, key_all, value_all))
    mixed_low = mixed_heads.reshape(token_count, model_width).astype(jnp.bfloat16)
    attn_out = jnp.dot(mixed_low, wout, preferred_element_type=jnp.float32)
    up_proj = jnp.dot(normed, wup, preferred_element_type=jnp.float32) + bup.astype(jnp.float32)
    activation = exact_gelu(up_proj).astype(jnp.bfloat16)
    mlp_out = jnp.dot(activation, wdown, preferred_element_type=jnp.float32)
    result = (inputs + attn_out + mlp_out + bout.astype(jnp.float32)).astype(jnp.bfloat16)
    norm_gain, norm_shift, wqkv, bqkv, wout, wup, bup, wdown, bout = (
        lax.all_gather(owned_shards[0], ("seq", "batch"), axis=0, tiled=True),
        lax.all_gather(owned_shards[1], ("seq", "batch"), axis=0, tiled=True),
        lax.all_gather(owned_shards[2], ("seq", "batch"), axis=0, tiled=True),
        lax.all_gather(owned_shards[3], ("seq", "batch"), axis=0, tiled=True),
        lax.all_gather(owned_shards[4], ("seq", "batch"), axis=0, tiled=True),
        lax.all_gather(owned_shards[5], ("seq", "batch"), axis=0, tiled=True),
        lax.all_gather(owned_shards[6], ("seq", "batch"), axis=0, tiled=True),
        lax.all_gather(owned_shards[7], ("seq", "batch"), axis=0, tiled=True),
        lax.all_gather(owned_shards[8], ("seq", "batch"), axis=0, tiled=True),
    )
    cotangent_rows = cotangent.reshape(token_count, model_width)
    cotangent_f = cotangent_rows.astype(jnp.float32)
    grad_bout = jnp.sum(cotangent_f, 0)
    grad_wout = contract_rows(mixed_low, cotangent_rows)
    grad_wdown = contract_rows(activation, cotangent_rows)
    grad_act = times_transposed(cotangent_rows, wdown)
    _, gelu_back = jax.vjp(exact_gelu, up_proj)
    grad_up = gelu_back(grad_act)[0].astype(jnp.bfloat16)
    grad_wup = contract_rows(normed, grad_up)
    grad_bup = jnp.sum(grad_up.astype(jnp.float32), 0)
    grad_heads = (
        times_transposed(cotangent_rows, wout)
        .astype(jnp.bfloat16)
        .reshape(seq_count, tok_rows, head_count, head_dim)
    )
    delta_rows = jnp.swapaxes(jnp.sum(grad_heads.astype(jnp.float32) * mixed_heads, -1), 1, 2)

    def backward_sequence(entry):
        query_seq, grad_seq, key_seq, value_seq, total_seq, delta_seq = entry
        return query_grads(
            query_seq,
            grad_seq,
            key_seq,
            value_seq,
            total_seq,
            delta_seq,
            query_pos,
            score_scale,
            block_rows,
        )

    grad_queries = lax.map(
        backward_sequence, (queries, grad_heads, key_all, value_all, log_total, delta_rows)
    )
    row_count = tok_rows * lax.axis_size("seq")
    sub_rows = math.gcd(row_count, 512)

    def one_block(block_index):
        first_key = block_index * sub_rows
        key_pos = first_key + jnp.arange(sub_rows, dtype=jnp.int32)

        def one_sequence(entry):
            query_seq, grad_seq, total_seq, delta_seq, key_seq, value_seq = entry
            key_rows = lax.dynamic_slice_in_dim(key_seq, first_key, sub_rows, 0).reshape(
                sub_rows, head_count, head_dim
            )
            value_rows = lax.dynamic_slice_in_dim(value_seq, first_key, sub_rows, 0).reshape(
                sub_rows, head_count, head_dim
            )
            return key_terms(
                query_seq,
                grad_seq,
                total_seq,
                delta_seq,
                query_pos,
                key_rows,
                value_rows,
                key_pos,
                score_scale,
            )

        per_sequence = lax.map(
            one_sequence, (queries, grad_heads, log_total, delta_rows, key_all, value_all)
        )
        return jnp.swapaxes(per_sequence, 0, 1)

    block_terms = lax.map(one_block, jnp.arange(row_count // sub_rows, dtype=jnp.int32))
    summed = lax.psum_scatter(
        block_terms.reshape(row_count, seq_count, 2 * model_width).astype(jnp.bfloat16),
        "seq",
        scatter_dimension=0,
        tiled=True,
    ).astype(jnp.float32)
    key_grads_all = jnp.swapaxes(summed, 0, 1)
    grad_keys = key_grads_all[..., :model_width].reshape(seq_count, tok_rows, head_count, head_dim)
    grad_values = key_grads_all[..., model_width:].reshape(
        seq_count, tok_rows, head_count, head_dim
    )
    grad_q_turned = rotate(grad_queries, cosine_table, -sine_table)
    grad_k_turned = rotate(grad_keys, cosine_table, -sine_table)
    grad_joined = (
        jnp.stack([grad_q_turned, grad_k_turned, grad_values], 2)
        .reshape(token_count, 3 * model_width)
        .astype(jnp.bfloat16)
    )
    grad_wqkv = contract_rows(normed, grad_joined)
    grad_bqkv = jnp.sum(grad_joined.astype(jnp.float32), 0)
    grad_normed = times_transposed(grad_joined, wqkv) + times_transposed(grad_up, wup)
    grad_gain = jnp.sum(grad_normed * unit_rows, 0)
    grad_shift = jnp.sum(grad_normed, 0)
    grad_unit = grad_normed * norm_gain.astype(jnp.float32)
    grad_inputs = cotangent_f + inv_root * (
        grad_unit
        - jnp.mean(grad_unit, -1, keepdims=True)
        - unit_rows * jnp.mean(grad_unit * unit_rows, -1, keepdims=True)
    )
    owner_grads = (
        lax.psum_scatter(grad_gain, ("seq", "batch"), scatter_dimension=0, tiled=True),
        lax.psum_scatter(grad_shift, ("seq", "batch"), scatter_dimension=0, tiled=True),
        lax.psum_scatter(grad_wqkv, ("seq", "batch"), scatter_dimension=0, tiled=True),
        lax.psum_scatter(grad_bqkv, ("seq", "batch"), scatter_dimension=0, tiled=True),
        lax.psum_scatter(grad_wout, ("seq", "batch"), scatter_dimension=0, tiled=True),
        lax.psum_scatter(grad_wup, ("seq", "batch"), scatter_dimension=0, tiled=True),
        lax.psum_scatter(grad_bup, ("seq", "batch"), scatter_dimension=0, tiled=True),
        lax.psum_scatter(grad_wdown, ("seq", "batch"), scatter_dimension=0, tiled=True),
        lax.psum_scatter(grad_bout, ("seq", "batch"), scatter_dimension=0, tiled=True),
    )
    return (
        result.reshape(seq_count, tok_rows, model_width),
        grad_inputs.reshape(seq_count, tok_rows, model_width),
        owner_grads[0],
        owner_grads[1],
        owner_grads[2],
        owner_grads[3],
        owner_grads[4],
        owner_grads[5],
        owner_grads[6],
        owner_grads[7],
        owner_grads[8],
    )


MESH = pl.DeviceIdType.MESH
F32, BF16 = jnp.float32, jnp.bfloat16
TOK = 128
BT = 256
MODEL = 1024
SEQ = 16
CHIPS = 8
UP = 256
HD = 64
WIDE = 512
VEC = 448
GRADS = 448


def dot(left, right):
    return jnp.dot(left, right, preferred_element_type=F32)


def dot_nt(left, right):
    return lax.dot_general(left, right, (((1,), (1,)), ((), ())), preferred_element_type=F32)


def lanes(block):
    if isinstance(block, int):
        return slice(block * BT, (block + 1) * BT)
    return pl.ds(pl.multiple_of(block * BT, BT), BT)


def turn(rows, cosine, sine):
    first, second = rows[0:8], rows[8:16]
    return jnp.concatenate(
        [first * cosine - second * sine, second * cosine + first * sine, rows[16:]], 0
    )


def remote(src, dst, send_sem, recv_sem, device):
    return pltpu.make_async_remote_copy(
        src_ref=src,
        dst_ref=dst,
        send_sem=send_sem,
        recv_sem=recv_sem,
        device_id=device,
        device_id_type=MESH,
    )


def fused(
    tokens_h, cot_h, w_qkv_h, w_out_h, w_up_h, w_down_h, gain, shift, bout, bup, bqkv, cost, sint,
    out_h, gn_sum_h, norm_gain_h, d_rows_h, arecv_h, ln_sums_h,
    out, d_rows, arecv, ln_sums, res_sems, w_qkv, w_up, in_sems, tok, g, wsend, wc, wct, wd, gv, bct, normed, unit, amt, dactt, qt, kt, vt, k, v, sbuf, e,
    linv, ot, gt, dost, delta, dkt, dvt, part1, rc1, ry1, rzl1, rzr1, rc2, ry2, rzl2, rzr2, tmp,
    dgain, dshift, dbout, dwct, dwd, dsend, drecv, dws, xrecv, vsend, vrecv, vparts,
    w_ss, w_rs, x_ss, x_rs, wd_ss, wd_rs, t_ss, t_rs, g_ss, g_rs,
    c1_ss, c1_rs, y1_ss, y1_rs, zp1_ss, zl1_rs, zm1_ss, zr1_rs,
    c2_ss, c2_rs, y2_ss, y2_rs, zp2_ss, zl2_rs, zm2_ss, zr2_rs,
    d_ss, d_rs, dx_ss, dx_rs, a_ss, a_rs, vx_ss, vx_rs, v_ss, v_rs,
):
    s = lax.axis_index("seq")
    b = lax.axis_index("batch")
    z, y, c = s // 4, (s // 2) % 2, s % 2
    oy, oc, ob = 1 - y, 1 - c, 1 - b
    sib = (s + 1 - 2 * c, b)
    yn = (s + 2 - 4 * y, b)
    zp = (lax.rem(s + 4, SEQ), b)
    zm = (lax.rem(s + SEQ - 4, SEQ), b)
    xn = (s, ob)
    offsets = [(dz, dy, dc) for dz in (0, 1, 3, 2) for dy in (0, 1) for dc in (0, 1)][1:]

    def shifted(offset, sign):
        dz, dy, dc = offset
        return (
            4 * lax.rem(z + 4 + sign * dz, 4)
            + 2 * lax.rem(y + 2 + sign * dy, 2)
            + lax.rem(c + 2 + sign * dc, 2)
        )

    high = z // 2
    zo = [z, z + 1 - 2 * lax.rem(z, 2), 2 - high, 3 - 3 * high]
    inner = jnp.logical_and(z > 0, z < 3)
    outer = jnp.logical_or(z == 0, z == 3)

    def mid(*steps):
        @pl.when(inner)
        def _():
            for step in steps:
                step[0](*step[1:])

    def end(*steps):
        @pl.when(outer)
        def _():
            for step in steps:
                step[0](*step[1:])

    def both(*steps):
        for step in steps:
            step[0](*step[1:])

    barrier = pltpu.get_barrier_semaphore()
    for off in offsets:
        pl.semaphore_signal(
            barrier, inc=1, device_id=(shifted(off, 1), b), device_id_type=MESH
        )
    pl.semaphore_signal(barrier, inc=1, device_id=xn, device_id_type=MESH)

    down_own = pl.ds(pl.multiple_of(128 * b, 128), 128)
    down_other = pl.ds(pl.multiple_of(128 * ob, 128), 128)
    out_own = pl.ds(pl.multiple_of(UP + 32 * b, 32), 32)
    out_other = pl.ds(pl.multiple_of(UP + 32 * ob, 32), 32)
    loads = [
        pltpu.make_async_copy(src, dst, in_sems.at[n])
        for n, (src, dst) in enumerate(
            [
                (w_up_h, w_up), (w_qkv_h, w_qkv), (tokens_h, tok.at[s]), (cot_h, g.at[s]),
                (w_down_h, wd.at[down_own]), (w_out_h, wd.at[out_own]),
            ]
        )
    ]
    for load in loads:
        load.start()

    vectors = [gain[...], shift[...], bout[...]]
    vectors += [bup[:, 32 * i : 32 * (i + 1)] for i in range(4)]
    vectors += [bqkv[:, 32 * i : 32 * (i + 1)] for i in range(3)]
    vec = jnp.concatenate([w.astype(F32) for w in vectors] + [jnp.zeros((6, 32), F32)], 0).T
    vec = jnp.concatenate([vec, jnp.zeros((32, HD - 16), F32)], 1).astype(BF16)
    loads[0].wait()
    loads[1].wait()
    for t in range(SEQ):
        wsend[t] = jnp.concatenate(
            [
                w_up[:, UP * t : UP * (t + 1)],
                w_qkv[:, HD * t : HD * (t + 1)],
                w_qkv[:, MODEL + HD * t : MODEL + HD * (t + 1)],
                w_qkv[:, 2 * MODEL + HD * t : 2 * MODEL + HD * (t + 1)],
                vec,
            ],
            1,
        )
    wc[2 * s + b] = wsend[s]
    for load in loads[2:6]:
        load.wait()
    pl.semaphore_wait(barrier, SEQ)

    def w_copy(source, target):
        return remote(
            wsend.at[target], wc.at[2 * source + b], w_ss.at[target], w_rs.at[source], (target, b)
        )

    def x_copy(source, plane):
        return remote(
            wc.at[2 * source + plane], wc.at[2 * source + plane],
            x_ss.at[source], x_rs.at[source], xn,
        )

    wd_copies = [
        remote(wd.at[down_own], wd.at[down_own], wd_ss.at[0], wd_rs.at[0], xn),
        remote(wd.at[out_own], wd.at[out_own], wd_ss.at[1], wd_rs.at[1], xn),
    ]

    def gather(buf, ss, rs):
        def send(shard, way, device):
            return remote(buf.at[shard], buf.at[shard], ss.at[way, shard], rs.at[shard], device)

        def arrived(shard):
            send(shard, 0, sib).wait_recv()

        def on_own_z(act):
            @pl.when(z < 3)
            def _():
                act(send(s, 0, zp))

            @pl.when(z > 0)
            def _():
                act(send(s, 1, zm))

        def on_own_y(act):
            act(send(s, 2, yn))
            act(send(s, 3, sib))

        def own_z():
            on_own_z(start)

        def own_y():
            on_own_y(start)

        def on_z(t, act):
            shard = 4 * zo[t] + 2 * y + c

            @pl.when(jnp.logical_and(zo[t] < z, z < 3))
            def _():
                act(send(shard, 0, zp))

            @pl.when(jnp.logical_and(zo[t] > z, z > 0))
            def _():
                act(send(shard, 1, zm))

            act(send(shard, 2, yn))
            act(send(shard, 3, sib))

        def on_y(t, act):
            act(send(4 * zo[t] + 2 * oy + c, 3, sib))

        start = lambda copy: copy.start()
        finish = lambda copy: copy.wait_send()

        def step_z(t):
            arrived(4 * zo[t] + 2 * y + c)
            on_z(t, start)

        def step_y(t):
            arrived(4 * zo[t] + 2 * oy + c)
            on_y(t, start)

        def step_core(t, row):
            arrived(4 * zo[t] + 2 * row + oc)

        def drain():
            on_own_z(finish)
            on_own_y(finish)
            for t in range(1, 4):
                on_z(t, finish)
            for t in range(4):
                on_y(t, finish)

        return own_z, own_y, step_z, step_y, step_core, drain

    tok_oz, tok_oy, tok_z, tok_y, tok_core, tok_drain = gather(tok, t_ss, t_rs)
    g_oz, g_oy, g_z, g_y, g_core, g_drain = gather(g, g_ss, g_rs)

    def w_send(lo, hi):
        for off in offsets[lo:hi]:
            w_copy(s, shifted(off, 1)).start()

    def w_arrive(lo, hi):
        for off in offsets[lo:hi]:
            source = shifted(off, -1)
            w_copy(source, s).wait_recv()
            x_copy(source, b).start()

    both((tok_oz,), (tok_oy,))
    for off in offsets: w_copy(s, shifted(off, 1)).start()
    x_copy(s, b).start()
    mid((tok_z, 1), (tok_z, 2), (tok_y, 0))
    end((tok_z, 1), (tok_y, 0))
    both((g_oy,))
    end((g_oz,))
    both((w_arrive, 0, 7))
    both((w_arrive, 7, 15))
    mid((tok_z, 3), (tok_y, 1))
    end((tok_z, 2), (tok_y, 1))
    for copy in wd_copies: copy.start()
    for t in range(SEQ): x_copy(t, ob).wait_recv()
    wct[...] = wc[...].reshape(MODEL, WIDE).T
    rows = wct[VEC : VEC + 16, :].astype(F32)
    gv[...] = jnp.zeros_like(gv)
    gv[0:1] = rows[0:1]
    gv[1:2] = rows[1:2]
    gv[2:3] = rows[2:3]
    cols = []
    for half in range(2):
        tail = wc[2 * s + half][:, VEC - HD :].astype(F32)
        for i in range(4):
            cols.append(tail[:, HD + 3 + i : HD + 4 + i])
    lane_of = lax.broadcasted_iota(jnp.int32, (32, 128), 1)
    for which in range(3):
        for half in range(2):
            chunk = 32 * which + 2 * s + half
            tail = wc[chunk // 3][:, VEC - HD :].astype(F32)
            cols.append(
                jnp.sum(jnp.where(lane_of == HD + 7 + lax.rem(chunk, 3), tail, 0.0), 1, keepdims=True)
            )
    bct[...] = jnp.concatenate(cols, 0)

    def project(i):
        x = tok[pl.ds(2 * i, 2)].reshape(BT, MODEL).astype(F32)
        centered = x - jnp.mean(x, -1, keepdims=True)
        inv = lax.rsqrt(jnp.mean(centered * centered, -1, keepdims=True) + eps_norm)
        u = centered * inv
        n = (u * gv[0:1] + gv[1:2]).astype(BF16)
        normed[i] = n
        unit[i] = u.astype(BF16)
        jt = dot_nt(wct[0:VEC], n) + bct[...]
        up = jt[0:UP]
        half = 0.5 + 0.5 * lax.erf(up * 0.7071067811865476)
        at = lanes(i)
        amt[0:UP, at] = (up * half).astype(BF16)
        dactt[:, at] = half + up * (jnp.exp(-0.5 * up * up) * 0.3989422804014327)
        cs, sn = cost[:, at], sint[:, at]
        qt[:, at] = (turn(jt[256:320], cs, sn) * 0.125).astype(BF16)
        keys = turn(jt[320:384], cs, sn)
        kt[:, at] = keys.astype(BF16)
        vt[:, at] = jt[384:448].astype(BF16)
        k[i] = keys.T.astype(BF16)
        v[i] = jt[384:448].T.astype(BF16)

    def chip_of(t, row):
        return 2 * zo[t] + row

    def proj(t, row):
        tok_core(t, row)
        project(chip_of(t, row))

    both((proj, 0, y))
    mid((g_oz,))
    both((proj, 0, oy), (proj, 1, y))
    both((proj, 1, oy))
    end((tok_z, 3), (g_y, 0))
    mid((g_z, 1), (g_y, 0), (tok_y, 2))
    both((proj, 2, y))
    mid((g_z, 2))
    end((tok_y, 2))
    both((proj, 2, oy))
    both((proj, 3, y))
    end((g_z, 1))
    both((tok_y, 3), (proj, 3, oy))
    mid((g_z, 3))

    def e_put(n, block):
        m, at = 2 * (n // 4), 256 * (n % 4)
        e[m : m + 2, :, at : at + 256] = block.reshape(2, TOK, BT)

    def e_get(n):
        m, at = 2 * (n // 4), 256 * (n % 4)
        return e[m : m + 2, :, at : at + 256].reshape(BT, BT)

    def attend_fwd(qb):
        at = lanes(qb)
        base = qb * (qb + 1) // 2
        q = qt[:, at]
        top = None
        for kb in range(qb + 1):
            st = dot(k[kb], q)
            if kb == qb:
                key_at = lax.broadcasted_iota(jnp.int32, (BT, BT), 0)
                query_at = lax.broadcasted_iota(jnp.int32, (BT, BT), 1)
                st = jnp.where(key_at <= query_at, st, neg_big)
            sbuf[kb] = st
            here = jnp.max(st, 0, keepdims=True)
            top = here if top is None else jnp.maximum(top, here)
        total = jnp.zeros((1, BT), F32)
        o = jnp.zeros((HD, BT), F32)
        for kb in range(qb + 1):
            ee = jnp.exp(sbuf[kb] - top)
            total = total + jnp.sum(ee, 0, keepdims=True)
            eb = ee.astype(BF16)
            e_put(base + kb, eb)
            o = o + dot(vt[:, lanes(kb)], eb)
        li = 1.0 / total
        linv[:, at] = li
        o = o * li
        ot[:, at] = o
        amt[UP : UP + HD, at] = o.astype(BF16)

    def reducer(part, rc, ry, rzl, rzr, c_ss, c_rs, y_ss, y_rs, zp_ss, zl_rs, zm_ss, zr_rs):
        order = [zo[3], zo[2], zo[1], zo[0]]

        def core_copy(t, row, color):
            chip = 2 * order[t] + row
            return remote(
                part.at[2 * chip + color], rc.at[chip], c_ss.at[chip], c_rs.at[chip], sib
            )

        def y_copy(t, row):
            return remote(
                rc.at[2 * order[t] + row], ry.at[order[t]], y_ss.at[order[t]], y_rs.at[order[t]], yn
            )

        def zp_copy(t):
            at = order[t]
            return remote(rc.at[2 * at + y], rzl.at[at], zp_ss.at[at], zl_rs.at[at], zp)

        def zm_copy(t):
            at = order[t]
            return remote(rc.at[2 * at + y], rzr.at[at], zm_ss.at[at], zr_rs.at[at], zm)

        def send_core(t, row):
            core_copy(t, row, oc).start()

        def send_y(t):
            chip = 2 * order[t] + oy
            core_copy(t, oy, oc).wait_recv()
            rc[chip] = (rc[chip].astype(F32) + part[2 * chip + c].astype(F32)).astype(BF16)
            y_copy(t, oy).start()

        def sum_here(t):
            chip = 2 * order[t] + y
            core_copy(t, y, oc).wait_recv()
            y_copy(t, y).wait_recv()
            tmp[...] = (
                rc[chip].astype(F32) + part[2 * chip + c].astype(F32) + ry[order[t]].astype(F32)
            )

        def add_left(t):
            zp_copy(t).wait_recv()
            tmp[...] += rzl[order[t]].astype(F32)

        def add_right(t):
            zm_copy(t).wait_recv()
            tmp[...] += rzr[order[t]].astype(F32)

        def pass_on(t):
            at = order[t]
            sum_here(t)

            @pl.when(jnp.logical_and(at > z, z > 0))
            def _():
                add_left(t)

            @pl.when(jnp.logical_and(at < z, z < 3))
            def _():
                add_right(t)

            rc[2 * at + y] = tmp[...].astype(BF16)

            @pl.when(at > z)
            def _():
                zp_copy(t).start()

            @pl.when(at < z)
            def _():
                zm_copy(t).start()

        def last():
            sum_here(3)

            @pl.when(z > 0)
            def _():
                add_left(3)

            @pl.when(z < 3)
            def _():
                add_right(3)

        def drain_core():
            for t in range(4):
                for row in (oy, y):
                    core_copy(t, row, oc).wait_send()

        def drain():
            for t in range(4):
                y_copy(t, oy).wait_send()
            for t in range(3):
                at = order[t]

                @pl.when(at > z)
                def _():
                    zp_copy(t).wait_send()

                @pl.when(at < z)
                def _():
                    zm_copy(t).wait_send()

        return order, send_core, send_y, pass_on, last, drain_core, drain

    order, core1, y1, pass1, last1, drain_core1, drain1 = reducer(
        part1, rc1, ry1, rzl1, rzr1, c1_ss, c1_rs, y1_ss, y1_rs, zp1_ss, zl1_rs, zm1_ss, zr1_rs
    )
    _, core2, y2, pass2, last2, drain_core2, drain2 = reducer(
        e, rc2, ry2, rzl2, rzr2, c2_ss, c2_rs, y2_ss, y2_rs, zp2_ss, zl2_rs, zm2_ss, zr2_rs
    )

    def out_block(t, row):
        i = 2 * order[t] + row
        part1[pl.ds(2 * i, 2)] = (
            dot(amt[:, lanes(i)].T, wd[...]).astype(BF16).reshape(2, TOK, MODEL)
        )
        core1(t, row)

    def grads_at(i):
        gb = g[pl.ds(2 * i, 2)].reshape(BT, MODEL)
        at = lanes(i)
        r = dot_nt(wd[...], gb)
        gt[0:UP, at] = (r[0:UP] * dactt[:, at]).astype(BF16)
        li = linv[:, at]
        gm = r[UP : UP + HD]
        dost[:, at] = (gm * li).astype(BF16)
        delta[:, at] = jnp.sum(gm * ot[:, at], 0, keepdims=True) * li
        dbout[...] += jnp.sum(gb.astype(F32).reshape(BT // 8, 8, MODEL), 0)

    def attend_bwd(qb):
        at = lanes(qb)
        base = qb * (qb + 1) // 2
        do, q, de = dost[:, at], qt[:, at], delta[:, at]
        dq = jnp.zeros((HD, BT), F32)
        for kb in range(qb + 1):
            ks = lanes(kb)
            eb = e_get(base + kb)
            dp = dot(v[kb], do)
            ds = (eb.astype(F32) * (dp - de)).astype(BF16)
            dv = dot_nt(do, eb)
            dk = dot_nt(q, ds)
            if kb == qb:
                dvt[:, ks] = dv
                dkt[:, ks] = dk
            else:
                dvt[:, ks] += dv
                dkt[:, ks] += dk
            dq = dq + dot(kt[:, ks], ds)
        gt[256:320, at] = turn(dq * 0.125, cost[:, at], -sint[:, at]).astype(BF16)

    def norm_grads(t, row):
        i = 2 * order[t] + row
        gn = dot(gt[:, lanes(i)].T, wct[0:GRADS])
        e[pl.ds(2 * i, 2)] = gn.astype(BF16).reshape(2, TOK, MODEL)
        core2(t, row)
        dshift[...] += jnp.sum(gn.reshape(BT // 8, 8, MODEL), 0)
        dgain[...] += jnp.sum((gn * unit[i].astype(F32)).reshape(BT // 8, 8, MODEL), 0)

    dgain[...] = jnp.zeros_like(dgain)
    dshift[...] = jnp.zeros_like(dshift)
    dbout[...] = jnp.zeros_like(dbout)

    def wd_arrive():
        for copy in wd_copies:
            copy.wait_send()
        remote(wd.at[down_other], wd.at[down_other], wd_ss.at[0], wd_rs.at[0], xn).wait_recv()
        remote(wd.at[out_other], wd.at[out_other], wd_ss.at[1], wd_rs.at[1], xn).wait_recv()

    def fwd(lo, hi):
        for qb in range(lo, hi):
            attend_fwd(qb)

    def grads(t, row):
        g_core(t, row)
        grads_at(chip_of(t, row))

    def bwd(lo, hi):
        for qb in range(lo, hi):
            attend_bwd(qb)

    def bwd_keys():
        gt[320:384, :] = turn(dkt[...], cost[...], -sint[...]).astype(BF16)
        gt[384:448, :] = dvt[...].astype(BF16)

    dx_copies = [remote(dws.at[p, ob], xrecv.at[p], dx_ss.at[p], dx_rs.at[p], xn) for p in range(2)]

    def turn_out(p, extra):
        for j in range(2 * SEQ // 4):
            turned = dwct[256 * p : 256 * (p + 1), 128 * j : 128 * (j + 1)].T
            for i in range(4):
                piece = turned[32 * i : 32 * (i + 1)]
                dev = 4 * j + i
                at = dws.at[p, dev % 2, dev // 2]
                if extra is None:
                    at[...] = piece.astype(BF16)
                else:
                    at[:, 0:128] = piece[:, 0:128].astype(BF16)
                    at[:, 128:256] = (piece[:, 128:256] + extra).astype(BF16)
        dx_copies[p].start()

    def up_grads():
        nn = normed.reshape(SEQ * TOK, MODEL)
        for n in range(4):
            dwct[0:256, lanes(n)] = dot(gt[0:256], nn[:, lanes(n)])
        turn_out(0, None)

    def qkv_grads():
        nn = normed.reshape(SEQ * TOK, MODEL)
        for n in range(4):
            dwct[256:GRADS, lanes(n)] = dot(gt[256:GRADS], nn[:, lanes(n)])
        dwct[GRADS:WIDE] = jnp.zeros((WIDE - GRADS, MODEL), F32)
        dwct[VEC : VEC + 1] = jnp.sum(dbout[...], 0, keepdims=True)
        bias_col = jnp.sum(gt[...].astype(F32), 1, keepdims=True)
        turn_out(
            1,
            jnp.concatenate(
                [jnp.zeros((32, HD + 1), F32)]
                + [bias_col[32 * n : 32 * (n + 1)] for n in range(14)]
                + [jnp.zeros((32, 128 - HD - 15), F32)],
                1,
            ),
        )

    vx_copy = remote(vsend, vrecv, vx_ss, vx_rs, xn)

    def ln_grads():
        vsend[0:1] = jnp.sum(dgain[...], 0, keepdims=True)
        vsend[1:2] = jnp.sum(dshift[...], 0, keepdims=True)
        vsend[2:8] = jnp.zeros((6, MODEL), F32)
        vx_copy.start()

    d_copy = remote(dsend, drecv, d_ss, d_rs, xn)

    def down_grads():
        gg = g.reshape(SEQ * TOK, MODEL)
        for n in range(4):
            dwd[:, lanes(n)] = dot(amt[...], gg[:, lanes(n)])
        dsend[0:128] = dwd[down_other].astype(BF16)
        dsend[128:160] = dwd[out_other].astype(BF16)
        d_copy.start()

    def a_copy(p, source, target):
        return remote(
            dws.at[p, b, target], arecv.at[p, source], a_ss.at[p, target], a_rs.at[p, source],
            (target, b),
        )

    def wide_out(p):
        dx_copies[p].wait_recv()
        dws[p, b] = (dws[p, b].astype(F32) + xrecv[p].astype(F32)).astype(BF16)
        for off in offsets:
            a_copy(p, s, shifted(off, 1)).start()
        arecv[p, s] = dws[p, b, s]

    res_copies = [
        pltpu.make_async_copy(src, dst, res_sems.at[n])
        for n, (src, dst) in enumerate(
            [
                (out, out_h), (tmp, gn_sum_h), (gv, norm_gain_h), (d_rows, d_rows_h),
                (arecv, arecv_h), (ln_sums, ln_sums_h),
            ]
        )
    ]

    def end1():
        last1()
        out[...] = (tmp[...] + tok[s].astype(F32) + gv[2:3]).astype(BF16)
        res_copies[0].start()

    def v_copy(source, target):
        piece = pl.ds(pl.multiple_of(128 * (target // 2), 128), 128)
        return remote(
            vrecv.at[:, piece], vparts.at[source], v_ss.at[target], v_rs.at[source], (target, b)
        )

    def ln_out():
        vx_copy.wait()
        vrecv[...] += vsend[...]
        for off in offsets:
            v_copy(s, shifted(off, 1)).start()
        vparts[s] = vrecv[:, pl.ds(pl.multiple_of(128 * (s // 2), 128), 128)]

    def down_out():
        d_copy.wait_recv()
        d_rows[0:128] = dwd[down_own] + drecv[0:128].astype(F32)
        d_rows[128:160] = dwd[out_own] + drecv[128:160].astype(F32)
        res_copies[2].start()
        res_copies[3].start()

    def ln_arrive():
        for off in offsets:
            v_copy(shifted(off, -1), s).wait_recv()
        ln_sums[...] = jnp.sum(vparts[...], 0)
        res_copies[5].start()

    def end2():
        last2()
        res_copies[1].start()

    def wide_arrive():
        for off in offsets:
            a_copy(0, shifted(off, -1), s).wait_recv()
            a_copy(1, shifted(off, -1), s).wait_recv()
        res_copies[4].start()

    both((wd_arrive,), (fwd, 0, 5))
    mid((g_y, 1))
    end((g_z, 2))
    both((fwd, 5, 8))
    end((g_y, 1))
    both((grads, 0, y), (out_block, 0, oy), (out_block, 1, oy), (out_block, 2, oy), (out_block, 3, oy))
    end((g_z, 3))
    both((y1, 0), (y1, 1), (y1, 2), (y1, 3))
    both((out_block, 0, y), (out_block, 1, y), (out_block, 2, y), (out_block, 3, y))
    both((grads, 0, oy), (grads, 1, y), (grads, 1, oy), (grads, 2, y), (g_y, 2), (grads, 2, oy), (grads, 3, y))
    both((g_y, 3), (grads, 3, oy))
    both((up_grads,))
    end((pass1, 0))
    both((bwd, 0, 8), (bwd_keys,))
    end((pass1, 1))
    both((qkv_grads,))
    both((wide_out, 0))
    both((norm_grads, 0, oy), (norm_grads, 1, oy), (norm_grads, 2, oy), (norm_grads, 3, oy))
    both((y2, 0), (y2, 1), (y2, 2), (y2, 3))
    end((pass1, 2))
    mid((pass1, 0))
    both((norm_grads, 0, y), (norm_grads, 1, y), (norm_grads, 2, y), (norm_grads, 3, y))
    mid((pass1, 1), (pass1, 2))
    both((ln_grads,), (down_grads,))
    both((wide_out, 1))
    end((end1,), (pass2, 0), (ln_out,))
    mid((ln_out,), (end1,), (pass2, 0))
    both((pass2, 1))
    both((down_out,))
    both((pass2, 2), (ln_arrive,), (wide_arrive,), (end2,))

    for off in offsets:
        w_copy(s, shifted(off, 1)).wait_send()
        a_copy(0, s, shifted(off, 1)).wait_send()
        a_copy(1, s, shifted(off, 1)).wait_send()
        v_copy(s, shifted(off, 1)).wait_send()
    for t in range(SEQ):
        x_copy(t, b).wait_send()
    tok_drain()
    g_drain()
    drain_core1()
    drain1()
    drain_core2()
    drain2()
    d_copy.wait_send()
    for copy in dx_copies:
        copy.wait_send()
    for copy in res_copies:
        copy.wait()


def finish(
    tokens_h, cot_h, out_h, gn_sum_h, norm_gain_h, d_rows_h, arecv_h, ln_sums_h,
    out, d_tok_h, d_gain, d_shift, d_qkv_h, d_bqkv, d_out, d_up_h, d_bup, d_down, d_bout,
    tokens, cot, gn_sum, norm_gain, arecv, ln_sums, d_tok, d_qkv, d_up, kept, rows, sems, out_sems,
):
    loads = [
        pltpu.make_async_copy(src, dst, sems.at[n])
        for n, (src, dst) in enumerate(
            [
                (arecv_h.at[0], arecv.at[0]), (arecv_h.at[1], arecv.at[1]),
                (gn_sum_h, gn_sum), (tokens_h, tokens), (norm_gain_h, norm_gain), (cot_h, cot),
                (ln_sums_h, ln_sums), (out_h, kept), (d_rows_h, rows),
            ]
        )
    ]
    stores = [
        pltpu.make_async_copy(src, dst, out_sems.at[n])
        for n, (src, dst) in enumerate(
            [
                (kept, out), (rows.at[0:128], d_down), (rows.at[128:160], d_out),
                (d_up, d_up_h), (d_qkv, d_qkv_h), (d_tok, d_tok_h),
            ]
        )
    ]
    for move in loads:
        move.start()
    s = lax.axis_index("seq")
    b = lax.axis_index("batch")
    loads[0].wait()
    for t in range(SEQ):
        d_up[:, UP * t : UP * (t + 1)] = arecv[0, t].astype(F32)
    stores[3].start()
    loads[7].wait()
    loads[8].wait()
    for move in stores[0:3]:
        move.start()
    loads[1].wait()
    for t in range(0, SEQ, 2):
        even, odd = arecv[1, t].astype(F32), arecv[1, t + 1].astype(F32)
        for which in range(3):
            lo = HD * which
            d_qkv[:, MODEL * which + HD * t : MODEL * which + HD * (t + 2)] = jnp.concatenate(
                [even[:, lo : lo + HD], odd[:, lo : lo + HD]], 1
            )
    stores[4].start()
    for move in loads[2:7]:
        move.wait()
    x = tokens[...].astype(F32)
    centered = x - jnp.mean(x, -1, keepdims=True)
    inv = lax.rsqrt(jnp.mean(centered * centered, -1, keepdims=True) + eps_norm)
    u = centered * inv
    gu = gn_sum[...] * norm_gain[0:1]
    d_tok[...] = cot[...].astype(F32) + inv * (
        gu - jnp.mean(gu, -1, keepdims=True) - u * jnp.mean(gu * u, -1, keepdims=True)
    )
    stores[5].start()
    lane_of = lax.broadcasted_iota(jnp.int32, (32, 128), 1)

    def pick(block, lane):
        return jnp.sum(jnp.where(lane_of == lane, block, 0.0), 1, keepdims=True)

    mine = arecv[1, s][:, 128:256].astype(F32)
    picked = [mine[:, HD : HD + 1]]
    for i in range(4):
        picked.append(pick(mine, HD + 1 + 4 * b + i))
    for i in range(3):
        chunk = 3 * (2 * s + b) + i
        block = arecv[1, lax.rem(chunk, 32) // 2][:, 128:256].astype(F32)
        picked.append(pick(block, HD + 1 + 8 + 2 * (chunk // 32) + lax.rem(chunk, 2)))
    rows = jnp.concatenate(picked + [jnp.zeros((32, 120), F32)], 1).T
    d_bout[...] = rows[0:1]
    d_bup[...] = jnp.concatenate([rows[1 + i : 2 + i] for i in range(4)], 1)
    d_bqkv[...] = jnp.concatenate([rows[5 + i : 6 + i] for i in range(3)], 1)
    turned = pltpu.roll(ln_sums[...], lax.rem(128 - 32 * lax.rem(2 * s + b, 4), 128), 1)
    d_gain[...] = turned[0:1, 0:32]
    d_shift[...] = turned[1:2, 0:32]
    for move in stores:
        move.wait()


def fast_local(
    tokens, ln_gain, ln_bias, w_qkv, b_qkv, w_out, w_up, b_up, w_down, b_out, cotangent
):
    length = SEQ * TOK
    frequency = rotary_base ** (-(2.0 * np.arange(8)) / 16.0)
    angles = frequency.astype(np.float32)[:, None] * np.arange(length, dtype=np.float32)[None]
    cost = jnp.asarray(np.cos(angles.astype(np.float64)).astype(np.float32))
    sint = jnp.asarray(np.sin(angles.astype(np.float64)).astype(np.float32))
    vm = pl.BlockSpec(memory_space=pltpu.VMEM)
    far = pl.BlockSpec(memory_space=pl.ANY)
    shape = jax.ShapeDtypeStruct
    dma = pltpu.SemaphoreType.DMA

    def reduce_buffers():
        return [
            pltpu.VMEM((CHIPS, TOK, MODEL), BF16),
            pltpu.VMEM((4, TOK, MODEL), BF16),
            pltpu.VMEM((4, TOK, MODEL), BF16),
            pltpu.VMEM((4, TOK, MODEL), BF16),
        ]

    reduce_sems = [dma((8,)), dma((8,))] + [dma((4,))] * 6
    results = pl.pallas_call(
        fused,
        out_shape=[
            shape((TOK, MODEL), BF16),
            shape((TOK, MODEL), F32),
            shape((8, MODEL), F32),
            shape((160, MODEL), F32),
            shape((2, SEQ, 32, 256), BF16),
            shape((8, 128), F32),
        ],
        in_specs=[far] * 6 + [vm] * 7,
        out_specs=[far] * 6,
        scratch_shapes=[
            pltpu.VMEM((TOK, MODEL), BF16),
            pltpu.VMEM((160, MODEL), F32),
            pltpu.VMEM((2, SEQ, 32, 256), BF16),
            pltpu.VMEM((8, 128), F32),
            dma((6,)),
            pltpu.VMEM((32, 3 * MODEL), BF16),
            pltpu.VMEM((32, 4 * MODEL), BF16),
            dma((6,)),
            pltpu.VMEM((SEQ, TOK, MODEL), BF16),
            pltpu.VMEM((SEQ, TOK, MODEL), BF16),
            pltpu.VMEM((SEQ, 32, WIDE), BF16),
            pltpu.VMEM((2 * SEQ, 32, WIDE), BF16),
            pltpu.VMEM((WIDE, MODEL), BF16),
            pltpu.VMEM((UP + HD, MODEL), BF16),
            pltpu.VMEM((8, MODEL), F32),
            pltpu.VMEM((VEC, 1), F32),
            pltpu.VMEM((CHIPS, BT, MODEL), BF16),
            pltpu.VMEM((CHIPS, BT, MODEL), BF16),
            pltpu.VMEM((UP + HD, length), BF16),
            pltpu.VMEM((UP, length), F32),
            pltpu.VMEM((HD, length), BF16),
            pltpu.VMEM((HD, length), BF16),
            pltpu.VMEM((HD, length), BF16),
            pltpu.VMEM((CHIPS, BT, HD), BF16),
            pltpu.VMEM((CHIPS, BT, HD), BF16),
            pltpu.VMEM((CHIPS, BT, BT), F32),
            pltpu.VMEM((18, TOK, MODEL), BF16),
            pltpu.VMEM((1, length), F32),
            pltpu.VMEM((HD, length), F32),
            pltpu.VMEM((GRADS, length), BF16),
            pltpu.VMEM((HD, length), BF16),
            pltpu.VMEM((1, length), F32),
            pltpu.VMEM((HD, length), F32),
            pltpu.VMEM((HD, length), F32),
            pltpu.VMEM((SEQ, TOK, MODEL), BF16),
        ]
        + reduce_buffers()
        + reduce_buffers()
        + [
            pltpu.VMEM((TOK, MODEL), F32),
            pltpu.VMEM((8, MODEL), F32),
            pltpu.VMEM((8, MODEL), F32),
            pltpu.VMEM((8, MODEL), F32),
            pltpu.VMEM((WIDE, MODEL), F32),
            pltpu.VMEM((UP + HD, MODEL), F32),
            pltpu.VMEM((160, MODEL), BF16),
            pltpu.VMEM((160, MODEL), BF16),
            pltpu.VMEM((2, 2, SEQ, 32, 256), BF16),
            pltpu.VMEM((2, SEQ, 32, 256), BF16),
            pltpu.VMEM((8, MODEL), F32),
            pltpu.VMEM((8, MODEL), F32),
            pltpu.VMEM((SEQ, 8, 128), F32),
            dma((SEQ,)), dma((SEQ,)), dma((SEQ,)), dma((SEQ,)), dma((2,)), dma((2,)),
            dma((4, SEQ)), dma((SEQ,)), dma((4, SEQ)), dma((SEQ,)),
        ]
        + reduce_sems
        + reduce_sems
        + [dma, dma, dma((2,)), dma((2,)), dma((2, SEQ)), dma((2, SEQ)), dma, dma, dma((SEQ,)), dma((SEQ,))],
        compiler_params=pltpu.CompilerParams(
            collective_id=0, has_side_effects=True, vmem_limit_bytes=62 * 2**20
        ),
    )(
        tokens.reshape(TOK, MODEL), cotangent.reshape(TOK, MODEL),
        w_qkv, w_out, w_up, w_down,
        ln_gain.reshape(1, 32), ln_bias.reshape(1, 32), b_out.reshape(1, 32),
        b_up.reshape(1, 128), b_qkv.reshape(1, 96), cost, sint,
    )
    out, gn_sum, norm_gain, d_rows, arecv, ln_sums = results
    (out, d_tok, d_gain, d_shift, d_qkv, d_bqkv, d_out, d_up, d_bup, d_down, d_bout) = pl.pallas_call(
        finish,
        out_shape=[
            shape((TOK, MODEL), BF16),
            shape((TOK, MODEL), F32),
            shape((1, 32), F32),
            shape((1, 32), F32),
            shape((32, 3 * MODEL), F32),
            shape((1, 96), F32),
            shape((32, MODEL), F32),
            shape((32, 4 * MODEL), F32),
            shape((1, 128), F32),
            shape((128, MODEL), F32),
            shape((1, 32), F32),
        ],
        in_specs=[far] * 8,
        out_specs=[far, far, vm, vm, far, vm, far, far, vm, far, vm],
        scratch_shapes=[
            pltpu.VMEM((TOK, MODEL), BF16),
            pltpu.VMEM((TOK, MODEL), BF16),
            pltpu.VMEM((TOK, MODEL), F32),
            pltpu.VMEM((8, MODEL), F32),
            pltpu.VMEM((2, SEQ, 32, 256), BF16),
            pltpu.VMEM((8, 128), F32),
            pltpu.VMEM((TOK, MODEL), F32),
            pltpu.VMEM((32, 3 * MODEL), F32),
            pltpu.VMEM((32, 4 * MODEL), F32),
            pltpu.VMEM((TOK, MODEL), BF16),
            pltpu.VMEM((160, MODEL), F32),
            dma((9,)),
            dma((6,)),
        ],
        compiler_params=pltpu.CompilerParams(vmem_limit_bytes=62 * 2**20),
    )(
        tokens.reshape(TOK, MODEL), cotangent.reshape(TOK, MODEL),
        out, gn_sum, norm_gain, d_rows, arecv, ln_sums,
    )
    return (
        out.reshape(tokens.shape),
        d_tok.reshape(tokens.shape),
        d_gain.reshape(32),
        d_shift.reshape(32),
        d_qkv,
        d_bqkv.reshape(96),
        d_out,
        d_up,
        d_bup.reshape(128),
        d_down,
        d_bout.reshape(32),
    )


def solution(mesh):
    in_specs = (
        P("batch", "seq", None),
        P(("seq", "batch")),
        P(("seq", "batch")),
        P(("seq", "batch"), None),
        P(("seq", "batch")),
        P(("seq", "batch"), None),
        P(("seq", "batch"), None),
        P(("seq", "batch")),
        P(("seq", "batch"), None),
        P(("seq", "batch")),
        P("batch", "seq", None),
    )
    out_specs = (
        P("batch", "seq", None),
        P("batch", "seq", None),
        P(("seq", "batch")),
        P(("seq", "batch")),
        P(("seq", "batch"), None),
        P(("seq", "batch")),
        P(("seq", "batch"), None),
        P(("seq", "batch"), None),
        P(("seq", "batch")),
        P(("seq", "batch"), None),
        P(("seq", "batch")),
    )
    fits = mesh.shape["seq"] == SEQ and mesh.shape["batch"] == 2
    body = fast_local if fits else local
    return jax.shard_map(body, mesh=mesh, in_specs=in_specs, out_specs=out_specs, check_vma=False)
```

```python
import math

import jax
import jax.numpy as jnp
import numpy as np
from jax import lax
from jax.experimental import pallas as pl
from jax.experimental.pallas import tpu as pltpu
from jax.sharding import PartitionSpec as P

HEADS = 16
ROTARY = 16


eps_norm = 1e-05
neg_big = -1e30
rotary_base = 10000.0


def rotary_tables(positions, half_width):
    frequency = rotary_base ** (
        -(2.0 * jnp.arange(half_width, dtype=jnp.float32)) / (2.0 * half_width)
    )
    angles = positions[:, None] * frequency[None, :]
    return (jnp.cos(angles)[:, None, :], jnp.sin(angles)[:, None, :])


def rotate(section, cosine_table, sine_table):
    half_width = cosine_table.shape[-1]
    first_half = section[..., :half_width]
    second_half = section[..., half_width : 2 * half_width]
    return jnp.concatenate(
        [
            first_half * cosine_table - second_half * sine_table,
            second_half * cosine_table + first_half * sine_table,
            section[..., 2 * half_width :],
        ],
        -1,
    )


def exact_gelu(values):
    return jax.nn.gelu(values, approximate=False)


def contract_rows(left, right):
    return lax.dot_general(
        left, right, (((0,), (0,)), ((), ())), preferred_element_type=jnp.float32
    )


def times_transposed(left, right):
    return lax.dot_general(
        left, right, (((1,), (1,)), ((), ())), preferred_element_type=jnp.float32
    )


def masked_scores(queries, key_rows, query_pos, key_pos, score_scale):
    scores = (
        jnp.einsum("qhd,khd->hqk", queries, key_rows, preferred_element_type=jnp.float32)
        * score_scale
    )
    allowed = key_pos[None, :] <= query_pos[:, None]
    return jnp.where(allowed[None], scores, neg_big)


def split_blocks(flat_rows, block_rows, head_count, head_dim):
    length = flat_rows.shape[0]
    return flat_rows.reshape(length // block_rows, block_rows, head_count, head_dim)


def attend(queries, key_all, value_all, query_pos, score_scale, block_rows):
    head_count, head_dim = (queries.shape[1], queries.shape[2])
    length = key_all.shape[0]
    key_blocks = split_blocks(key_all, block_rows, head_count, head_dim)
    value_blocks = split_blocks(value_all, block_rows, head_count, head_dim)
    position_blocks = jnp.arange(length, dtype=jnp.int32).reshape(length // block_rows, block_rows)

    def statistics(state_in, entry):
        running_max, running_sum = state_in
        key_rows, key_pos = entry
        scores = masked_scores(queries, key_rows, query_pos, key_pos, score_scale)
        new_max = jnp.maximum(running_max, jnp.max(scores, -1))
        running_sum = running_sum * jnp.exp(running_max - new_max) + jnp.sum(
            jnp.exp(scores - new_max[..., None]), -1
        )
        return ((new_max, running_sum), None)

    start_state = (
        jnp.full((head_count, queries.shape[0]), neg_big, jnp.float32),
        jnp.zeros((head_count, queries.shape[0]), jnp.float32),
    )
    (running_max, running_sum), _ = lax.scan(statistics, start_state, (key_blocks, position_blocks))
    log_total = running_max + jnp.log(running_sum)

    def attend_accumulate(mixed_heads, entry):
        key_rows, value_rows, key_pos = entry
        scores = masked_scores(queries, key_rows, query_pos, key_pos, score_scale)
        probs_low = jnp.exp(scores - log_total[..., None]).astype(jnp.bfloat16)
        return (
            mixed_heads
            + jnp.einsum("hqk,khd->qhd", probs_low, value_rows, preferred_element_type=jnp.float32),
            None,
        )

    mixed_heads, _ = lax.scan(
        attend_accumulate,
        jnp.zeros(queries.shape, jnp.float32),
        (key_blocks, value_blocks, position_blocks),
    )
    return (mixed_heads, log_total)


def query_grads(
    queries,
    grad_heads,
    key_all,
    value_all,
    log_total,
    delta_rows,
    query_pos,
    score_scale,
    block_rows,
):
    head_count, head_dim = (queries.shape[1], queries.shape[2])
    length = key_all.shape[0]
    key_blocks = split_blocks(key_all, block_rows, head_count, head_dim)
    value_blocks = split_blocks(value_all, block_rows, head_count, head_dim)
    position_blocks = jnp.arange(length, dtype=jnp.int32).reshape(length // block_rows, block_rows)

    def query_accumulate(grad_queries, entry):
        key_rows, value_rows, key_pos = entry
        scores = masked_scores(queries, key_rows, query_pos, key_pos, score_scale)
        probs = jnp.exp(scores - log_total[..., None])
        grad_probs = jnp.einsum(
            "qhd,khd->hqk", grad_heads, value_rows, preferred_element_type=jnp.float32
        )
        grad_scores = (probs * (grad_probs - delta_rows[..., None])).astype(jnp.bfloat16)
        return (
            grad_queries
            + jnp.einsum("hqk,khd->qhd", grad_scores, key_rows, preferred_element_type=jnp.float32),
            None,
        )

    grad_queries, _ = lax.scan(
        query_accumulate,
        jnp.zeros(queries.shape, jnp.float32),
        (key_blocks, value_blocks, position_blocks),
    )
    return grad_queries * score_scale


def key_terms(
    queries,
    grad_heads,
    log_total,
    delta_rows,
    query_pos,
    key_rows,
    value_rows,
    key_pos,
    score_scale,
):
    scores = masked_scores(queries, key_rows, query_pos, key_pos, score_scale)
    probs = jnp.exp(scores - log_total[..., None])
    grad_probs = jnp.einsum(
        "qhd,khd->hqk", grad_heads, value_rows, preferred_element_type=jnp.float32
    )
    grad_scores = (probs * (grad_probs - delta_rows[..., None])).astype(jnp.bfloat16)
    grad_keys = (
        jnp.einsum("hqk,qhd->khd", grad_scores, queries, preferred_element_type=jnp.float32)
        * score_scale
    )
    grad_values = jnp.einsum(
        "hqk,qhd->khd", probs.astype(jnp.bfloat16), grad_heads, preferred_element_type=jnp.float32
    )
    key_count = key_rows.shape[0]
    return jnp.concatenate(
        [grad_keys.reshape(key_count, -1), grad_values.reshape(key_count, -1)], -1
    )


def local(tokens, ln_gain, ln_bias, w_qkv, b_qkv, w_out, w_up, b_up, w_down, b_out, cotangent):
    seq_count, tok_rows, model_width = tokens.shape
    head_count = HEADS
    head_dim = model_width // head_count
    score_scale = head_dim ** (-0.5)
    length = tok_rows * lax.axis_size("seq")
    block_rows = math.gcd(length, 512)
    token_count = seq_count * tok_rows
    owned_shards = (ln_gain, ln_bias, w_qkv, b_qkv, w_out, w_up, b_up, w_down, b_out)
    norm_gain, norm_shift, wqkv, bqkv, wout, wup, bup, wdown, bout = (
        lax.all_gather(owned_shards[0], ("seq", "batch"), axis=0, tiled=True),
        lax.all_gather(owned_shards[1], ("seq", "batch"), axis=0, tiled=True),
        lax.all_gather(owned_shards[2], ("seq", "batch"), axis=0, tiled=True),
        lax.all_gather(owned_shards[3], ("seq", "batch"), axis=0, tiled=True),
        lax.all_gather(owned_shards[4], ("seq", "batch"), axis=0, tiled=True),
        lax.all_gather(owned_shards[5], ("seq", "batch"), axis=0, tiled=True),
        lax.all_gather(owned_shards[6], ("seq", "batch"), axis=0, tiled=True),
        lax.all_gather(owned_shards[7], ("seq", "batch"), axis=0, tiled=True),
        lax.all_gather(owned_shards[8], ("seq", "batch"), axis=0, tiled=True),
    )
    inputs = tokens.reshape(token_count, model_width).astype(jnp.float32)
    average = jnp.mean(inputs, -1, keepdims=True)
    centered = inputs - average
    inv_root = lax.rsqrt(jnp.mean(centered * centered, -1, keepdims=True) + eps_norm)
    unit_rows = centered * inv_root
    normed = (unit_rows * norm_gain.astype(jnp.float32) + norm_shift.astype(jnp.float32)).astype(
        jnp.bfloat16
    )
    joined_qkv = (
        jnp.dot(normed, wqkv, preferred_element_type=jnp.float32) + bqkv.astype(jnp.float32)
    ).reshape(seq_count, tok_rows, 3, head_count, head_dim)
    query_pos = lax.axis_index("seq") * tok_rows + jnp.arange(tok_rows, dtype=jnp.int32)
    cosine_table, sine_table = rotary_tables(query_pos.astype(jnp.float32), ROTARY // 2)
    queries = rotate(joined_qkv[:, :, 0], cosine_table, sine_table).astype(jnp.bfloat16)
    key_local = rotate(joined_qkv[:, :, 1], cosine_table, sine_table).astype(jnp.bfloat16)
    value_local = joined_qkv[:, :, 2].astype(jnp.bfloat16)
    key_all, value_all = (
        lax.all_gather(
            key_local.reshape(seq_count, tok_rows, model_width), "seq", axis=1, tiled=True
        ),
        lax.all_gather(
            value_local.reshape(seq_count, tok_rows, model_width), "seq", axis=1, tiled=True
        ),
    )

    def forward_sequence(entry):
        query_seq, key_seq, value_seq = entry
        return attend(query_seq, key_seq, value_seq, query_pos, score_scale, block_rows)

    mixed_heads, log_total = lax.map(forward_sequence, (queries, key_all, value_all))
    mixed_low = mixed_heads.reshape(token_count, model_width).astype(jnp.bfloat16)
    attn_out = jnp.dot(mixed_low, wout, preferred_element_type=jnp.float32)
    up_proj = jnp.dot(normed, wup, preferred_element_type=jnp.float32) + bup.astype(jnp.float32)
    activation = exact_gelu(up_proj).astype(jnp.bfloat16)
    mlp_out = jnp.dot(activation, wdown, preferred_element_type=jnp.float32)
    result = (inputs + attn_out + mlp_out + bout.astype(jnp.float32)).astype(jnp.bfloat16)
    norm_gain, norm_shift, wqkv, bqkv, wout, wup, bup, wdown, bout = (
        lax.all_gather(owned_shards[0], ("seq", "batch"), axis=0, tiled=True),
        lax.all_gather(owned_shards[1], ("seq", "batch"), axis=0, tiled=True),
        lax.all_gather(owned_shards[2], ("seq", "batch"), axis=0, tiled=True),
        lax.all_gather(owned_shards[3], ("seq", "batch"), axis=0, tiled=True),
        lax.all_gather(owned_shards[4], ("seq", "batch"), axis=0, tiled=True),
        lax.all_gather(owned_shards[5], ("seq", "batch"), axis=0, tiled=True),
        lax.all_gather(owned_shards[6], ("seq", "batch"), axis=0, tiled=True),
        lax.all_gather(owned_shards[7], ("seq", "batch"), axis=0, tiled=True),
        lax.all_gather(owned_shards[8], ("seq", "batch"), axis=0, tiled=True),
    )
    cotangent_rows = cotangent.reshape(token_count, model_width)
    cotangent_f = cotangent_rows.astype(jnp.float32)
    grad_bout = jnp.sum(cotangent_f, 0)
    grad_wout = contract_rows(mixed_low, cotangent_rows)
    grad_wdown = contract_rows(activation, cotangent_rows)
    grad_act = times_transposed(cotangent_rows, wdown)
    _, gelu_back = jax.vjp(exact_gelu, up_proj)
    grad_up = gelu_back(grad_act)[0].astype(jnp.bfloat16)
    grad_wup = contract_rows(normed, grad_up)
    grad_bup = jnp.sum(grad_up.astype(jnp.float32), 0)
    grad_heads = (
        times_transposed(cotangent_rows, wout)
        .astype(jnp.bfloat16)
        .reshape(seq_count, tok_rows, head_count, head_dim)
    )
    delta_rows = jnp.swapaxes(jnp.sum(grad_heads.astype(jnp.float32) * mixed_heads, -1), 1, 2)

    def backward_sequence(entry):
        query_seq, grad_seq, key_seq, value_seq, total_seq, delta_seq = entry
        return query_grads(
            query_seq,
            grad_seq,
            key_seq,
            value_seq,
            total_seq,
            delta_seq,
            query_pos,
            score_scale,
            block_rows,
        )

    grad_queries = lax.map(
        backward_sequence, (queries, grad_heads, key_all, value_all, log_total, delta_rows)
    )
    row_count = tok_rows * lax.axis_size("seq")
    sub_rows = math.gcd(row_count, 512)

    def one_block(block_index):
        first_key = block_index * sub_rows
        key_pos = first_key + jnp.arange(sub_rows, dtype=jnp.int32)

        def one_sequence(entry):
            query_seq, grad_seq, total_seq, delta_seq, key_seq, value_seq = entry
            key_rows = lax.dynamic_slice_in_dim(key_seq, first_key, sub_rows, 0).reshape(
                sub_rows, head_count, head_dim
            )
            value_rows = lax.dynamic_slice_in_dim(value_seq, first_key, sub_rows, 0).reshape(
                sub_rows, head_count, head_dim
            )
            return key_terms(
                query_seq,
                grad_seq,
                total_seq,
                delta_seq,
                query_pos,
                key_rows,
                value_rows,
                key_pos,
                score_scale,
            )

        per_sequence = lax.map(
            one_sequence, (queries, grad_heads, log_total, delta_rows, key_all, value_all)
        )
        return jnp.swapaxes(per_sequence, 0, 1)

    block_terms = lax.map(one_block, jnp.arange(row_count // sub_rows, dtype=jnp.int32))
    summed = lax.psum_scatter(
        block_terms.reshape(row_count, seq_count, 2 * model_width).astype(jnp.bfloat16),
        "seq",
        scatter_dimension=0,
        tiled=True,
    ).astype(jnp.float32)
    key_grads_all = jnp.swapaxes(summed, 0, 1)
    grad_keys = key_grads_all[..., :model_width].reshape(seq_count, tok_rows, head_count, head_dim)
    grad_values = key_grads_all[..., model_width:].reshape(
        seq_count, tok_rows, head_count, head_dim
    )
    grad_q_turned = rotate(grad_queries, cosine_table, -sine_table)
    grad_k_turned = rotate(grad_keys, cosine_table, -sine_table)
    grad_joined = (
        jnp.stack([grad_q_turned, grad_k_turned, grad_values], 2)
        .reshape(token_count, 3 * model_width)
        .astype(jnp.bfloat16)
    )
    grad_wqkv = contract_rows(normed, grad_joined)
    grad_bqkv = jnp.sum(grad_joined.astype(jnp.float32), 0)
    grad_normed = times_transposed(grad_joined, wqkv) + times_transposed(grad_up, wup)
    grad_gain = jnp.sum(grad_normed * unit_rows, 0)
    grad_shift = jnp.sum(grad_normed, 0)
    grad_unit = grad_normed * norm_gain.astype(jnp.float32)
    grad_inputs = cotangent_f + inv_root * (
        grad_unit
        - jnp.mean(grad_unit, -1, keepdims=True)
        - unit_rows * jnp.mean(grad_unit * unit_rows, -1, keepdims=True)
    )
    owner_grads = (
        lax.psum_scatter(grad_gain, ("seq", "batch"), scatter_dimension=0, tiled=True),
        lax.psum_scatter(grad_shift, ("seq", "batch"), scatter_dimension=0, tiled=True),
        lax.psum_scatter(grad_wqkv, ("seq", "batch"), scatter_dimension=0, tiled=True),
        lax.psum_scatter(grad_bqkv, ("seq", "batch"), scatter_dimension=0, tiled=True),
        lax.psum_scatter(grad_wout, ("seq", "batch"), scatter_dimension=0, tiled=True),
        lax.psum_scatter(grad_wup, ("seq", "batch"), scatter_dimension=0, tiled=True),
        lax.psum_scatter(grad_bup, ("seq", "batch"), scatter_dimension=0, tiled=True),
        lax.psum_scatter(grad_wdown, ("seq", "batch"), scatter_dimension=0, tiled=True),
        lax.psum_scatter(grad_bout, ("seq", "batch"), scatter_dimension=0, tiled=True),
    )
    return (
        result.reshape(seq_count, tok_rows, model_width),
        grad_inputs.reshape(seq_count, tok_rows, model_width),
        owner_grads[0],
        owner_grads[1],
        owner_grads[2],
        owner_grads[3],
        owner_grads[4],
        owner_grads[5],
        owner_grads[6],
        owner_grads[7],
        owner_grads[8],
    )


MESH = pl.DeviceIdType.MESH
F32, BF16 = jnp.float32, jnp.bfloat16
TOK = 128
BT = 256
MODEL = 1024
SEQ = 16
CHIPS = 8
UP = 256
HD = 64
WIDE = 512
VEC = 448
GRADS = 448


def dot(left, right):
    return jnp.dot(left, right, preferred_element_type=F32)


def dot_nt(left, right):
    return lax.dot_general(left, right, (((1,), (1,)), ((), ())), preferred_element_type=F32)


def lanes(block):
    if isinstance(block, int):
        return slice(block * BT, (block + 1) * BT)
    return pl.ds(pl.multiple_of(block * BT, BT), BT)


def turn(rows, cosine, sine):
    first, second = rows[0:8], rows[8:16]
    return jnp.concatenate(
        [first * cosine - second * sine, second * cosine + first * sine, rows[16:]], 0
    )


def remote(src, dst, send_sem, recv_sem, device):
    return pltpu.make_async_remote_copy(
        src_ref=src,
        dst_ref=dst,
        send_sem=send_sem,
        recv_sem=recv_sem,
        device_id=device,
        device_id_type=MESH,
    )


def fused(
    tokens_h, cot_h, w_qkv_h, w_out_h, w_up_h, w_down_h, gain, shift, bout, bup, bqkv, cost, sint,
    out_h, gn_sum_h, norm_gain_h, d_rows_h, arecv_h, ln_sums_h,
    out, d_rows, arecv, ln_sums, res_sems, w_qkv, w_up, in_sems, tok, g, wsend, wc, wct, wd, gv, bct, normed, unit, amt, dactt, qt, kt, vt, k, v, sbuf, e,
    linv, ot, gt, dost, delta, dkt, dvt, part1, rc1, ry1, rzl1, rzr1, rc2, ry2, rzl2, rzr2, tmp,
    dgain, dshift, dbout, dwct, dwd, dsend, drecv, dws, xrecv, vsend, vrecv, vparts,
    w_ss, w_rs, x_ss, x_rs, wd_ss, wd_rs, t_ss, t_rs, g_ss, g_rs,
    c1_ss, c1_rs, y1_ss, y1_rs, zp1_ss, zl1_rs, zm1_ss, zr1_rs,
    c2_ss, c2_rs, y2_ss, y2_rs, zp2_ss, zl2_rs, zm2_ss, zr2_rs,
    d_ss, d_rs, dx_ss, dx_rs, a_ss, a_rs, vx_ss, vx_rs, v_ss, v_rs,
):
    s = lax.axis_index("seq")
    b = lax.axis_index("batch")
    z, y, c = s // 4, (s // 2) % 2, s % 2
    oy, oc, ob = 1 - y, 1 - c, 1 - b
    sib = (s + 1 - 2 * c, b)
    yn = (s + 2 - 4 * y, b)
    zp = (lax.rem(s + 4, SEQ), b)
    zm = (lax.rem(s + SEQ - 4, SEQ), b)
    xn = (s, ob)
    offsets = [(dz, dy, dc) for dz in (0, 1, 3, 2) for dy in (0, 1) for dc in (0, 1)][1:]

    def shifted(offset, sign):
        dz, dy, dc = offset
        return (
            4 * lax.rem(z + 4 + sign * dz, 4)
            + 2 * lax.rem(y + 2 + sign * dy, 2)
            + lax.rem(c + 2 + sign * dc, 2)
        )

    high = z // 2
    zo = [z, z + 1 - 2 * lax.rem(z, 2), 2 - high, 3 - 3 * high]
    inner = jnp.logical_and(z > 0, z < 3)
    outer = jnp.logical_or(z == 0, z == 3)

    def mid(*steps):
        @pl.when(inner)
        def _():
            for step in steps:
                step[0](*step[1:])

    def end(*steps):
        @pl.when(outer)
        def _():
            for step in steps:
                step[0](*step[1:])

    def both(*steps):
        for step in steps:
            step[0](*step[1:])

    barrier = pltpu.get_barrier_semaphore()
    for off in offsets:
        pl.semaphore_signal(
            barrier, inc=1, device_id=(shifted(off, 1), b), device_id_type=MESH
        )
    pl.semaphore_signal(barrier, inc=1, device_id=xn, device_id_type=MESH)

    down_own = pl.ds(pl.multiple_of(128 * b, 128), 128)
    down_other = pl.ds(pl.multiple_of(128 * ob, 128), 128)
    out_own = pl.ds(pl.multiple_of(UP + 32 * b, 32), 32)
    out_other = pl.ds(pl.multiple_of(UP + 32 * ob, 32), 32)
    loads = [
        pltpu.make_async_copy(src, dst, in_sems.at[n])
        for n, (src, dst) in enumerate(
            [
                (w_up_h, w_up), (w_qkv_h, w_qkv), (tokens_h, tok.at[s]), (cot_h, g.at[s]),
                (w_down_h, wd.at[down_own]), (w_out_h, wd.at[out_own]),
            ]
        )
    ]
    for load in loads:
        load.start()

    vectors = [gain[...], shift[...], bout[...]]
    vectors += [bup[:, 32 * i : 32 * (i + 1)] for i in range(4)]
    vectors += [bqkv[:, 32 * i : 32 * (i + 1)] for i in range(3)]
    vec = jnp.concatenate([w.astype(F32) for w in vectors] + [jnp.zeros((6, 32), F32)], 0).T
    vec = jnp.concatenate([vec, jnp.zeros((32, HD - 16), F32)], 1).astype(BF16)
    loads[0].wait()
    loads[1].wait()
    for t in range(SEQ):
        wsend[t] = jnp.concatenate(
            [
                w_up[:, UP * t : UP * (t + 1)],
                w_qkv[:, HD * t : HD * (t + 1)],
                w_qkv[:, MODEL + HD * t : MODEL + HD * (t + 1)],
                w_qkv[:, 2 * MODEL + HD * t : 2 * MODEL + HD * (t + 1)],
                vec,
            ],
            1,
        )
    wc[2 * s + b] = wsend[s]
    for load in loads[2:6]:
        load.wait()
    pl.semaphore_wait(barrier, SEQ)

    def w_copy(source, target):
        return remote(
            wsend.at[target], wc.at[2 * source + b], w_ss.at[target], w_rs.at[source], (target, b)
        )

    def x_copy(source, plane):
        return remote(
            wc.at[2 * source + plane], wc.at[2 * source + plane],
            x_ss.at[source], x_rs.at[source], xn,
        )

    wd_copies = [
        remote(wd.at[down_own], wd.at[down_own], wd_ss.at[0], wd_rs.at[0], xn),
        remote(wd.at[out_own], wd.at[out_own], wd_ss.at[1], wd_rs.at[1], xn),
    ]

    def gather(buf, ss, rs):
        def send(shard, way, device):
            return remote(buf.at[shard], buf.at[shard], ss.at[way, shard], rs.at[shard], device)

        def arrived(shard):
            send(shard, 0, sib).wait_recv()

        def on_own_z(act):
            @pl.when(z < 3)
            def _():
                act(send(s, 0, zp))

            @pl.when(z > 0)
            def _():
                act(send(s, 1, zm))

        def on_own_y(act):
            act(send(s, 2, yn))
            act(send(s, 3, sib))

        def own_z():
            on_own_z(start)

        def own_y():
            on_own_y(start)

        def on_z(t, act):
            shard = 4 * zo[t] + 2 * y + c

            @pl.when(jnp.logical_and(zo[t] < z, z < 3))
            def _():
                act(send(shard, 0, zp))

            @pl.when(jnp.logical_and(zo[t] > z, z > 0))
            def _():
                act(send(shard, 1, zm))

            act(send(shard, 2, yn))
            act(send(shard, 3, sib))

        def on_y(t, act):
            act(send(4 * zo[t] + 2 * oy + c, 3, sib))

        start = lambda copy: copy.start()
        finish = lambda copy: copy.wait_send()

        def step_z(t):
            arrived(4 * zo[t] + 2 * y + c)
            on_z(t, start)

        def step_y(t):
            arrived(4 * zo[t] + 2 * oy + c)
            on_y(t, start)

        def step_core(t, row):
            arrived(4 * zo[t] + 2 * row + oc)

        def drain():
            on_own_z(finish)
            on_own_y(finish)
            for t in range(1, 4):
                on_z(t, finish)
            for t in range(4):
                on_y(t, finish)

        return own_z, own_y, step_z, step_y, step_core, drain

    tok_oz, tok_oy, tok_z, tok_y, tok_core, tok_drain = gather(tok, t_ss, t_rs)
    g_oz, g_oy, g_z, g_y, g_core, g_drain = gather(g, g_ss, g_rs)

    def w_send(lo, hi):
        for off in offsets[lo:hi]:
            w_copy(s, shifted(off, 1)).start()

    def w_arrive(lo, hi):
        for off in offsets[lo:hi]:
            source = shifted(off, -1)
            w_copy(source, s).wait_recv()
            x_copy(source, b).start()

    both((tok_oz,), (tok_oy,))
    for off in offsets: w_copy(s, shifted(off, 1)).start()
    x_copy(s, b).start()
    mid((tok_z, 1), (tok_z, 2), (tok_y, 0))
    end((tok_z, 1), (tok_y, 0))
    both((g_oy,))
    end((g_oz,))
    both((w_arrive, 0, 7))
    both((w_arrive, 7, 15))
    mid((tok_z, 3), (tok_y, 1))
    end((tok_z, 2), (tok_y, 1))
    for copy in wd_copies: copy.start()
    for t in range(SEQ): x_copy(t, ob).wait_recv()
    wct[...] = wc[...].reshape(MODEL, WIDE).T
    rows = wct[VEC : VEC + 16, :].astype(F32)
    gv[...] = jnp.zeros_like(gv)
    gv[0:1] = rows[0:1]
    gv[1:2] = rows[1:2]
    gv[2:3] = rows[2:3]
    cols = []
    for half in range(2):
        tail = wc[2 * s + half][:, VEC - HD :].astype(F32)
        for i in range(4):
            cols.append(tail[:, HD + 3 + i : HD + 4 + i])
    lane_of = lax.broadcasted_iota(jnp.int32, (32, 128), 1)
    for which in range(3):
        for half in range(2):
            chunk = 32 * which + 2 * s + half
            tail = wc[chunk // 3][:, VEC - HD :].astype(F32)
            cols.append(
                jnp.sum(jnp.where(lane_of == HD + 7 + lax.rem(chunk, 3), tail, 0.0), 1, keepdims=True)
            )
    bct[...] = jnp.concatenate(cols, 0)

    def project(i):
        x = tok[pl.ds(2 * i, 2)].reshape(BT, MODEL).astype(F32)
        centered = x - jnp.mean(x, -1, keepdims=True)
        inv = lax.rsqrt(jnp.mean(centered * centered, -1, keepdims=True) + eps_norm)
        u = centered * inv
        n = (u * gv[0:1] + gv[1:2]).astype(BF16)
        normed[i] = n
        unit[i] = u.astype(BF16)
        jt = dot_nt(wct[0:VEC], n) + bct[...]
        up = jt[0:UP]
        half = 0.5 + 0.5 * lax.erf(up * 0.7071067811865476)
        at = lanes(i)
        amt[0:UP, at] = (up * half).astype(BF16)
        dactt[:, at] = half + up * (jnp.exp(-0.5 * up * up) * 0.3989422804014327)
        cs, sn = cost[:, at], sint[:, at]
        qt[:, at] = (turn(jt[256:320], cs, sn) * 0.125).astype(BF16)
        keys = turn(jt[320:384], cs, sn)
        kt[:, at] = keys.astype(BF16)
        vt[:, at] = jt[384:448].astype(BF16)
        k[i] = keys.T.astype(BF16)
        v[i] = jt[384:448].T.astype(BF16)

    def chip_of(t, row):
        return 2 * zo[t] + row

    def proj(t, row):
        tok_core(t, row)
        project(chip_of(t, row))

    both((proj, 0, y))
    mid((g_oz,))
    both((proj, 0, oy), (proj, 1, y))
    both((proj, 1, oy))
    end((tok_z, 3), (g_y, 0))
    mid((g_z, 1), (g_y, 0), (tok_y, 2))
    both((proj, 2, y))
    mid((g_z, 2))
    end((tok_y, 2))
    both((proj, 2, oy))
    both((proj, 3, y))
    end((g_z, 1))
    both((tok_y, 3), (proj, 3, oy))
    mid((g_z, 3))

    def e_put(n, block):
        m, at = 2 * (n // 4), 256 * (n % 4)
        e[m : m + 2, :, at : at + 256] = block.reshape(2, TOK, BT)

    def e_get(n):
        m, at = 2 * (n // 4), 256 * (n % 4)
        return e[m : m + 2, :, at : at + 256].reshape(BT, BT)

    def attend_fwd(qb):
        at = lanes(qb)
        base = qb * (qb + 1) // 2
        q = qt[:, at]
        top = None
        for kb in range(qb + 1):
            st = dot(k[kb], q)
            if kb == qb:
                key_at = lax.broadcasted_iota(jnp.int32, (BT, BT), 0)
                query_at = lax.broadcasted_iota(jnp.int32, (BT, BT), 1)
                st = jnp.where(key_at <= query_at, st, neg_big)
            sbuf[kb] = st
            here = jnp.max(st, 0, keepdims=True)
            top = here if top is None else jnp.maximum(top, here)
        total = jnp.zeros((1, BT), F32)
        o = jnp.zeros((HD, BT), F32)
        for kb in range(qb + 1):
            ee = jnp.exp(sbuf[kb] - top)
            total = total + jnp.sum(ee, 0, keepdims=True)
            eb = ee.astype(BF16)
            e_put(base + kb, eb)
            o = o + dot(vt[:, lanes(kb)], eb)
        li = 1.0 / total
        linv[:, at] = li
        o = o * li
        ot[:, at] = o
        amt[UP : UP + HD, at] = o.astype(BF16)

    def reducer(part, rc, ry, rzl, rzr, c_ss, c_rs, y_ss, y_rs, zp_ss, zl_rs, zm_ss, zr_rs):
        order = [zo[3], zo[2], zo[1], zo[0]]

        def core_copy(t, row, color):
            chip = 2 * order[t] + row
            return remote(
                part.at[2 * chip + color], rc.at[chip], c_ss.at[chip], c_rs.at[chip], sib
            )

        def y_copy(t, row):
            return remote(
                rc.at[2 * order[t] + row], ry.at[order[t]], y_ss.at[order[t]], y_rs.at[order[t]], yn
            )

        def zp_copy(t):
            at = order[t]
            return remote(rc.at[2 * at + y], rzl.at[at], zp_ss.at[at], zl_rs.at[at], zp)

        def zm_copy(t):
            at = order[t]
            return remote(rc.at[2 * at + y], rzr.at[at], zm_ss.at[at], zr_rs.at[at], zm)

        def send_core(t, row):
            core_copy(t, row, oc).start()

        def send_y(t):
            chip = 2 * order[t] + oy
            core_copy(t, oy, oc).wait_recv()
            rc[chip] = (rc[chip].astype(F32) + part[2 * chip + c].astype(F32)).astype(BF16)
            y_copy(t, oy).start()

        def sum_here(t):
            chip = 2 * order[t] + y
            core_copy(t, y, oc).wait_recv()
            y_copy(t, y).wait_recv()
            tmp[...] = (
                rc[chip].astype(F32) + part[2 * chip + c].astype(F32) + ry[order[t]].astype(F32)
            )

        def add_left(t):
            zp_copy(t).wait_recv()
            tmp[...] += rzl[order[t]].astype(F32)

        def add_right(t):
            zm_copy(t).wait_recv()
            tmp[...] += rzr[order[t]].astype(F32)

        def pass_on(t):
            at = order[t]
            sum_here(t)

            @pl.when(jnp.logical_and(at > z, z > 0))
            def _():
                add_left(t)

            @pl.when(jnp.logical_and(at < z, z < 3))
            def _():
                add_right(t)

            rc[2 * at + y] = tmp[...].astype(BF16)

            @pl.when(at > z)
            def _():
                zp_copy(t).start()

            @pl.when(at < z)
            def _():
                zm_copy(t).start()

        def last():
            sum_here(3)

            @pl.when(z > 0)
            def _():
                add_left(3)

            @pl.when(z < 3)
            def _():
                add_right(3)

        def drain_core():
            for t in range(4):
                for row in (oy, y):
                    core_copy(t, row, oc).wait_send()

        def drain():
            for t in range(4):
                y_copy(t, oy).wait_send()
            for t in range(3):
                at = order[t]

                @pl.when(at > z)
                def _():
                    zp_copy(t).wait_send()

                @pl.when(at < z)
                def _():
                    zm_copy(t).wait_send()

        return order, send_core, send_y, pass_on, last, drain_core, drain

    order, core1, y1, pass1, last1, drain_core1, drain1 = reducer(
        part1, rc1, ry1, rzl1, rzr1, c1_ss, c1_rs, y1_ss, y1_rs, zp1_ss, zl1_rs, zm1_ss, zr1_rs
    )
    _, core2, y2, pass2, last2, drain_core2, drain2 = reducer(
        e, rc2, ry2, rzl2, rzr2, c2_ss, c2_rs, y2_ss, y2_rs, zp2_ss, zl2_rs, zm2_ss, zr2_rs
    )

    def out_block(t, row):
        i = 2 * order[t] + row
        part1[pl.ds(2 * i, 2)] = (
            dot(amt[:, lanes(i)].T, wd[...]).astype(BF16).reshape(2, TOK, MODEL)
        )
        core1(t, row)

    def grads_at(i):
        gb = g[pl.ds(2 * i, 2)].reshape(BT, MODEL)
        at = lanes(i)
        r = dot_nt(wd[...], gb)
        gt[0:UP, at] = (r[0:UP] * dactt[:, at]).astype(BF16)
        li = linv[:, at]
        gm = r[UP : UP + HD]
        dost[:, at] = (gm * li).astype(BF16)
        delta[:, at] = jnp.sum(gm * ot[:, at], 0, keepdims=True) * li
        dbout[...] += jnp.sum(gb.astype(F32).reshape(BT // 8, 8, MODEL), 0)

    def attend_bwd(qb):
        at = lanes(qb)
        base = qb * (qb + 1) // 2
        do, q, de = dost[:, at], qt[:, at], delta[:, at]
        dq = jnp.zeros((HD, BT), F32)
        for kb in range(qb + 1):
            ks = lanes(kb)
            eb = e_get(base + kb)
            dp = dot(v[kb], do)
            ds = (eb.astype(F32) * (dp - de)).astype(BF16)
            dv = dot_nt(do, eb)
            dk = dot_nt(q, ds)
            if kb == qb:
                dvt[:, ks] = dv
                dkt[:, ks] = dk
            else:
                dvt[:, ks] += dv
                dkt[:, ks] += dk
            dq = dq + dot(kt[:, ks], ds)
        gt[256:320, at] = turn(dq * 0.125, cost[:, at], -sint[:, at]).astype(BF16)

    def norm_grads(t, row):
        i = 2 * order[t] + row
        gn = dot(gt[:, lanes(i)].T, wct[0:GRADS])
        e[pl.ds(2 * i, 2)] = gn.astype(BF16).reshape(2, TOK, MODEL)
        core2(t, row)
        dshift[...] += jnp.sum(gn.reshape(BT // 8, 8, MODEL), 0)
        dgain[...] += jnp.sum((gn * unit[i].astype(F32)).reshape(BT // 8, 8, MODEL), 0)

    dgain[...] = jnp.zeros_like(dgain)
    dshift[...] = jnp.zeros_like(dshift)
    dbout[...] = jnp.zeros_like(dbout)

    def wd_arrive():
        for copy in wd_copies:
            copy.wait_send()
        remote(wd.at[down_other], wd.at[down_other], wd_ss.at[0], wd_rs.at[0], xn).wait_recv()
        remote(wd.at[out_other], wd.at[out_other], wd_ss.at[1], wd_rs.at[1], xn).wait_recv()

    def fwd(lo, hi):
        for qb in range(lo, hi):
            attend_fwd(qb)

    def grads(t, row):
        g_core(t, row)
        grads_at(chip_of(t, row))

    def bwd(lo, hi):
        for qb in range(lo, hi):
            attend_bwd(qb)

    def bwd_keys():
        gt[320:384, :] = turn(dkt[...], cost[...], -sint[...]).astype(BF16)
        gt[384:448, :] = dvt[...].astype(BF16)

    dx_copies = [remote(dws.at[p, ob], xrecv.at[p], dx_ss.at[p], dx_rs.at[p], xn) for p in range(2)]

    def turn_out(p, extra):
        for j in range(2 * SEQ // 4):
            turned = dwct[256 * p : 256 * (p + 1), 128 * j : 128 * (j + 1)].T
            for i in range(4):
                piece = turned[32 * i : 32 * (i + 1)]
                dev = 4 * j + i
                at = dws.at[p, dev % 2, dev // 2]
                if extra is None:
                    at[...] = piece.astype(BF16)
                else:
                    at[:, 0:128] = piece[:, 0:128].astype(BF16)
                    at[:, 128:256] = (piece[:, 128:256] + extra).astype(BF16)
        dx_copies[p].start()

    def up_grads():
        nn = normed.reshape(SEQ * TOK, MODEL)
        for n in range(4):
            dwct[0:256, lanes(n)] = dot(gt[0:256], nn[:, lanes(n)])
        turn_out(0, None)

    def qkv_grads():
        nn = normed.reshape(SEQ * TOK, MODEL)
        for n in range(4):
            dwct[256:GRADS, lanes(n)] = dot(gt[256:GRADS], nn[:, lanes(n)])
        dwct[GRADS:WIDE] = jnp.zeros((WIDE - GRADS, MODEL), F32)
        dwct[VEC : VEC + 1] = jnp.sum(dbout[...], 0, keepdims=True)
        bias_col = jnp.sum(gt[...].astype(F32), 1, keepdims=True)
        turn_out(
            1,
            jnp.concatenate(
                [jnp.zeros((32, HD + 1), F32)]
                + [bias_col[32 * n : 32 * (n + 1)] for n in range(14)]
                + [jnp.zeros((32, 128 - HD - 15), F32)],
                1,
            ),
        )

    vx_copy = remote(vsend, vrecv, vx_ss, vx_rs, xn)

    def ln_grads():
        vsend[0:1] = jnp.sum(dgain[...], 0, keepdims=True)
        vsend[1:2] = jnp.sum(dshift[...], 0, keepdims=True)
        vsend[2:8] = jnp.zeros((6, MODEL), F32)
        vx_copy.start()

    d_copy = remote(dsend, drecv, d_ss, d_rs, xn)

    def down_grads():
        gg = g.reshape(SEQ * TOK, MODEL)
        for n in range(4):
            dwd[:, lanes(n)] = dot(amt[...], gg[:, lanes(n)])
        dsend[0:128] = dwd[down_other].astype(BF16)
        dsend[128:160] = dwd[out_other].astype(BF16)
        d_copy.start()

    def a_copy(p, source, target):
        return remote(
            dws.at[p, b, target], arecv.at[p, source], a_ss.at[p, target], a_rs.at[p, source],
            (target, b),
        )

    def wide_out(p):
        dx_copies[p].wait_recv()
        dws[p, b] = (dws[p, b].astype(F32) + xrecv[p].astype(F32)).astype(BF16)
        for off in offsets:
            a_copy(p, s, shifted(off, 1)).start()
        arecv[p, s] = dws[p, b, s]

    res_copies = [
        pltpu.make_async_copy(src, dst, res_sems.at[n])
        for n, (src, dst) in enumerate(
            [
                (out, out_h), (tmp, gn_sum_h), (gv, norm_gain_h), (d_rows, d_rows_h),
                (arecv, arecv_h), (ln_sums, ln_sums_h),
            ]
        )
    ]

    def end1():
        last1()
        out[...] = (tmp[...] + tok[s].astype(F32) + gv[2:3]).astype(BF16)
        res_copies[0].start()

    def v_copy(source, target):
        piece = pl.ds(pl.multiple_of(128 * (target // 2), 128), 128)
        return remote(
            vrecv.at[:, piece], vparts.at[source], v_ss.at[target], v_rs.at[source], (target, b)
        )

    def ln_out():
        vx_copy.wait()
        vrecv[...] += vsend[...]
        for off in offsets:
            v_copy(s, shifted(off, 1)).start()
        vparts[s] = vrecv[:, pl.ds(pl.multiple_of(128 * (s // 2), 128), 128)]

    def down_out():
        d_copy.wait_recv()
        d_rows[0:128] = dwd[down_own] + drecv[0:128].astype(F32)
        d_rows[128:160] = dwd[out_own] + drecv[128:160].astype(F32)
        res_copies[2].start()
        res_copies[3].start()

    def ln_arrive():
        for off in offsets:
            v_copy(shifted(off, -1), s).wait_recv()
        ln_sums[...] = jnp.sum(vparts[...], 0)
        res_copies[5].start()

    def end2():
        last2()
        res_copies[1].start()

    def wide_arrive():
        for off in offsets:
            a_copy(0, shifted(off, -1), s).wait_recv()
            a_copy(1, shifted(off, -1), s).wait_recv()
        res_copies[4].start()

    both((wd_arrive,), (fwd, 0, 5))
    mid((g_y, 1))
    end((g_z, 2))
    both((fwd, 5, 8))
    end((g_y, 1))
    both((grads, 0, y), (out_block, 0, oy), (out_block, 1, oy), (out_block, 2, oy), (out_block, 3, oy))
    end((g_z, 3))
    both((y1, 0), (y1, 1), (y1, 2), (y1, 3))
    both((out_block, 0, y), (out_block, 1, y), (out_block, 2, y), (out_block, 3, y))
    both((grads, 0, oy), (grads, 1, y), (grads, 1, oy), (grads, 2, y), (g_y, 2), (grads, 2, oy), (grads, 3, y))
    both((g_y, 3), (grads, 3, oy))
    both((up_grads,))
    both((bwd, 0, 4))
    end((pass1, 0))
    both((bwd, 4, 8), (bwd_keys,))
    end((pass1, 1))
    both((qkv_grads,))
    both((wide_out, 0))
    both((norm_grads, 0, oy), (norm_grads, 1, oy), (norm_grads, 2, oy), (norm_grads, 3, oy))
    both((y2, 0), (y2, 1), (y2, 2), (y2, 3))
    end((pass1, 2))
    mid((pass1, 0))
    both((norm_grads, 0, y), (norm_grads, 1, y), (norm_grads, 2, y), (norm_grads, 3, y))
    mid((pass1, 1), (pass1, 2))
    both((ln_grads,), (down_grads,))
    both((wide_out, 1))
    end((end1,), (pass2, 0), (ln_out,))
    mid((ln_out,), (end1,), (pass2, 0))
    both((pass2, 1))
    both((down_out,))
    both((pass2, 2), (ln_arrive,), (wide_arrive,), (end2,))

    for off in offsets:
        w_copy(s, shifted(off, 1)).wait_send()
        a_copy(0, s, shifted(off, 1)).wait_send()
        a_copy(1, s, shifted(off, 1)).wait_send()
        v_copy(s, shifted(off, 1)).wait_send()
    for t in range(SEQ):
        x_copy(t, b).wait_send()
    tok_drain()
    g_drain()
    drain_core1()
    drain1()
    drain_core2()
    drain2()
    d_copy.wait_send()
    for copy in dx_copies:
        copy.wait_send()
    for copy in res_copies:
        copy.wait()


def finish(
    tokens_h, cot_h, out_h, gn_sum_h, norm_gain_h, d_rows_h, arecv_h, ln_sums_h,
    out, d_tok_h, d_gain, d_shift, d_qkv_h, d_bqkv, d_out, d_up_h, d_bup, d_down, d_bout,
    tokens, cot, gn_sum, norm_gain, arecv, ln_sums, d_tok, d_qkv, d_up, kept, rows, sems, out_sems,
):
    loads = [
        pltpu.make_async_copy(src, dst, sems.at[n])
        for n, (src, dst) in enumerate(
            [
                (arecv_h.at[0], arecv.at[0]), (arecv_h.at[1], arecv.at[1]),
                (gn_sum_h, gn_sum), (tokens_h, tokens), (norm_gain_h, norm_gain), (cot_h, cot),
                (ln_sums_h, ln_sums), (out_h, kept), (d_rows_h, rows),
            ]
        )
    ]
    stores = [
        pltpu.make_async_copy(src, dst, out_sems.at[n])
        for n, (src, dst) in enumerate(
            [
                (kept, out), (rows.at[0:128], d_down), (rows.at[128:160], d_out),
                (d_up, d_up_h), (d_qkv, d_qkv_h), (d_tok, d_tok_h),
            ]
        )
    ]
    for move in loads:
        move.start()
    s = lax.axis_index("seq")
    b = lax.axis_index("batch")
    loads[0].wait()
    for t in range(SEQ):
        d_up[:, UP * t : UP * (t + 1)] = arecv[0, t].astype(F32)
    stores[3].start()
    loads[7].wait()
    loads[8].wait()
    for move in stores[0:3]:
        move.start()
    loads[1].wait()
    for t in range(0, SEQ, 2):
        even, odd = arecv[1, t].astype(F32), arecv[1, t + 1].astype(F32)
        for which in range(3):
            lo = HD * which
            d_qkv[:, MODEL * which + HD * t : MODEL * which + HD * (t + 2)] = jnp.concatenate(
                [even[:, lo : lo + HD], odd[:, lo : lo + HD]], 1
            )
    stores[4].start()
    for move in loads[2:7]:
        move.wait()
    x = tokens[...].astype(F32)
    centered = x - jnp.mean(x, -1, keepdims=True)
    inv = lax.rsqrt(jnp.mean(centered * centered, -1, keepdims=True) + eps_norm)
    u = centered * inv
    gu = gn_sum[...] * norm_gain[0:1]
    d_tok[...] = cot[...].astype(F32) + inv * (
        gu - jnp.mean(gu, -1, keepdims=True) - u * jnp.mean(gu * u, -1, keepdims=True)
    )
    stores[5].start()
    lane_of = lax.broadcasted_iota(jnp.int32, (32, 128), 1)

    def pick(block, lane):
        return jnp.sum(jnp.where(lane_of == lane, block, 0.0), 1, keepdims=True)

    mine = arecv[1, s][:, 128:256].astype(F32)
    picked = [mine[:, HD : HD + 1]]
    for i in range(4):
        picked.append(pick(mine, HD + 1 + 4 * b + i))
    for i in range(3):
        chunk = 3 * (2 * s + b) + i
        block = arecv[1, lax.rem(chunk, 32) // 2][:, 128:256].astype(F32)
        picked.append(pick(block, HD + 1 + 8 + 2 * (chunk // 32) + lax.rem(chunk, 2)))
    rows = jnp.concatenate(picked + [jnp.zeros((32, 120), F32)], 1).T
    d_bout[...] = rows[0:1]
    d_bup[...] = jnp.concatenate([rows[1 + i : 2 + i] for i in range(4)], 1)
    d_bqkv[...] = jnp.concatenate([rows[5 + i : 6 + i] for i in range(3)], 1)
    turned = pltpu.roll(ln_sums[...], lax.rem(128 - 32 * lax.rem(2 * s + b, 4), 128), 1)
    d_gain[...] = turned[0:1, 0:32]
    d_shift[...] = turned[1:2, 0:32]
    for move in stores:
        move.wait()


def fast_local(
    tokens, ln_gain, ln_bias, w_qkv, b_qkv, w_out, w_up, b_up, w_down, b_out, cotangent
):
    length = SEQ * TOK
    frequency = rotary_base ** (-(2.0 * np.arange(8)) / 16.0)
    angles = frequency.astype(np.float32)[:, None] * np.arange(length, dtype=np.float32)[None]
    cost = jnp.asarray(np.cos(angles.astype(np.float64)).astype(np.float32))
    sint = jnp.asarray(np.sin(angles.astype(np.float64)).astype(np.float32))
    vm = pl.BlockSpec(memory_space=pltpu.VMEM)
    far = pl.BlockSpec(memory_space=pl.ANY)
    shape = jax.ShapeDtypeStruct
    dma = pltpu.SemaphoreType.DMA

    def reduce_buffers():
        return [
            pltpu.VMEM((CHIPS, TOK, MODEL), BF16),
            pltpu.VMEM((4, TOK, MODEL), BF16),
            pltpu.VMEM((4, TOK, MODEL), BF16),
            pltpu.VMEM((4, TOK, MODEL), BF16),
        ]

    reduce_sems = [dma((8,)), dma((8,))] + [dma((4,))] * 6
    results = pl.pallas_call(
        fused,
        out_shape=[
            shape((TOK, MODEL), BF16),
            shape((TOK, MODEL), F32),
            shape((8, MODEL), F32),
            shape((160, MODEL), F32),
            shape((2, SEQ, 32, 256), BF16),
            shape((8, 128), F32),
        ],
        in_specs=[far] * 6 + [vm] * 7,
        out_specs=[far] * 6,
        scratch_shapes=[
            pltpu.VMEM((TOK, MODEL), BF16),
            pltpu.VMEM((160, MODEL), F32),
            pltpu.VMEM((2, SEQ, 32, 256), BF16),
            pltpu.VMEM((8, 128), F32),
            dma((6,)),
            pltpu.VMEM((32, 3 * MODEL), BF16),
            pltpu.VMEM((32, 4 * MODEL), BF16),
            dma((6,)),
            pltpu.VMEM((SEQ, TOK, MODEL), BF16),
            pltpu.VMEM((SEQ, TOK, MODEL), BF16),
            pltpu.VMEM((SEQ, 32, WIDE), BF16),
            pltpu.VMEM((2 * SEQ, 32, WIDE), BF16),
            pltpu.VMEM((WIDE, MODEL), BF16),
            pltpu.VMEM((UP + HD, MODEL), BF16),
            pltpu.VMEM((8, MODEL), F32),
            pltpu.VMEM((VEC, 1), F32),
            pltpu.VMEM((CHIPS, BT, MODEL), BF16),
            pltpu.VMEM((CHIPS, BT, MODEL), BF16),
            pltpu.VMEM((UP + HD, length), BF16),
            pltpu.VMEM((UP, length), F32),
            pltpu.VMEM((HD, length), BF16),
            pltpu.VMEM((HD, length), BF16),
            pltpu.VMEM((HD, length), BF16),
            pltpu.VMEM((CHIPS, BT, HD), BF16),
            pltpu.VMEM((CHIPS, BT, HD), BF16),
            pltpu.VMEM((CHIPS, BT, BT), F32),
            pltpu.VMEM((18, TOK, MODEL), BF16),
            pltpu.VMEM((1, length), F32),
            pltpu.VMEM((HD, length), F32),
            pltpu.VMEM((GRADS, length), BF16),
            pltpu.VMEM((HD, length), BF16),
            pltpu.VMEM((1, length), F32),
            pltpu.VMEM((HD, length), F32),
            pltpu.VMEM((HD, length), F32),
            pltpu.VMEM((SEQ, TOK, MODEL), BF16),
        ]
        + reduce_buffers()
        + reduce_buffers()
        + [
            pltpu.VMEM((TOK, MODEL), F32),
            pltpu.VMEM((8, MODEL), F32),
            pltpu.VMEM((8, MODEL), F32),
            pltpu.VMEM((8, MODEL), F32),
            pltpu.VMEM((WIDE, MODEL), F32),
            pltpu.VMEM((UP + HD, MODEL), F32),
            pltpu.VMEM((160, MODEL), BF16),
            pltpu.VMEM((160, MODEL), BF16),
            pltpu.VMEM((2, 2, SEQ, 32, 256), BF16),
            pltpu.VMEM((2, SEQ, 32, 256), BF16),
            pltpu.VMEM((8, MODEL), F32),
            pltpu.VMEM((8, MODEL), F32),
            pltpu.VMEM((SEQ, 8, 128), F32),
            dma((SEQ,)), dma((SEQ,)), dma((SEQ,)), dma((SEQ,)), dma((2,)), dma((2,)),
            dma((4, SEQ)), dma((SEQ,)), dma((4, SEQ)), dma((SEQ,)),
        ]
        + reduce_sems
        + reduce_sems
        + [dma, dma, dma((2,)), dma((2,)), dma((2, SEQ)), dma((2, SEQ)), dma, dma, dma((SEQ,)), dma((SEQ,))],
        compiler_params=pltpu.CompilerParams(
            collective_id=0, has_side_effects=True, vmem_limit_bytes=62 * 2**20
        ),
    )(
        tokens.reshape(TOK, MODEL), cotangent.reshape(TOK, MODEL),
        w_qkv, w_out, w_up, w_down,
        ln_gain.reshape(1, 32), ln_bias.reshape(1, 32), b_out.reshape(1, 32),
        b_up.reshape(1, 128), b_qkv.reshape(1, 96), cost, sint,
    )
    out, gn_sum, norm_gain, d_rows, arecv, ln_sums = results
    (out, d_tok, d_gain, d_shift, d_qkv, d_bqkv, d_out, d_up, d_bup, d_down, d_bout) = pl.pallas_call(
        finish,
        out_shape=[
            shape((TOK, MODEL), BF16),
            shape((TOK, MODEL), F32),
            shape((1, 32), F32),
            shape((1, 32), F32),
            shape((32, 3 * MODEL), F32),
            shape((1, 96), F32),
            shape((32, MODEL), F32),
            shape((32, 4 * MODEL), F32),
            shape((1, 128), F32),
            shape((128, MODEL), F32),
            shape((1, 32), F32),
        ],
        in_specs=[far] * 8,
        out_specs=[far, far, vm, vm, far, vm, far, far, vm, far, vm],
        scratch_shapes=[
            pltpu.VMEM((TOK, MODEL), BF16),
            pltpu.VMEM((TOK, MODEL), BF16),
            pltpu.VMEM((TOK, MODEL), F32),
            pltpu.VMEM((8, MODEL), F32),
            pltpu.VMEM((2, SEQ, 32, 256), BF16),
            pltpu.VMEM((8, 128), F32),
            pltpu.VMEM((TOK, MODEL), F32),
            pltpu.VMEM((32, 3 * MODEL), F32),
            pltpu.VMEM((32, 4 * MODEL), F32),
            pltpu.VMEM((TOK, MODEL), BF16),
            pltpu.VMEM((160, MODEL), F32),
            dma((9,)),
            dma((6,)),
        ],
        compiler_params=pltpu.CompilerParams(vmem_limit_bytes=62 * 2**20),
    )(
        tokens.reshape(TOK, MODEL), cotangent.reshape(TOK, MODEL),
        out, gn_sum, norm_gain, d_rows, arecv, ln_sums,
    )
    return (
        out.reshape(tokens.shape),
        d_tok.reshape(tokens.shape),
        d_gain.reshape(32),
        d_shift.reshape(32),
        d_qkv,
        d_bqkv.reshape(96),
        d_out,
        d_up,
        d_bup.reshape(128),
        d_down,
        d_bout.reshape(32),
    )


def solution(mesh):
    in_specs = (
        P("batch", "seq", None),
        P(("seq", "batch")),
        P(("seq", "batch")),
        P(("seq", "batch"), None),
        P(("seq", "batch")),
        P(("seq", "batch"), None),
        P(("seq", "batch"), None),
        P(("seq", "batch")),
        P(("seq", "batch"), None),
        P(("seq", "batch")),
        P("batch", "seq", None),
    )
    out_specs = (
        P("batch", "seq", None),
        P("batch", "seq", None),
        P(("seq", "batch")),
        P(("seq", "batch")),
        P(("seq", "batch"), None),
        P(("seq", "batch")),
        P(("seq", "batch"), None),
        P(("seq", "batch"), None),
        P(("seq", "batch")),
        P(("seq", "batch"), None),
        P(("seq", "batch")),
    )
    fits = mesh.shape["seq"] == SEQ and mesh.shape["batch"] == 2
    body = fast_local if fits else local
    return jax.shard_map(body, mesh=mesh, in_specs=in_specs, out_specs=out_specs, check_vma=False)
```

```python
import math

import jax
import jax.numpy as jnp
import numpy as np
from jax import lax
from jax.experimental import pallas as pl
from jax.experimental.pallas import tpu as pltpu
from jax.sharding import PartitionSpec as P

HEADS = 16
ROTARY = 16


eps_norm = 1e-05
neg_big = -1e30
rotary_base = 10000.0


def rotary_tables(positions, half_width):
    frequency = rotary_base ** (
        -(2.0 * jnp.arange(half_width, dtype=jnp.float32)) / (2.0 * half_width)
    )
    angles = positions[:, None] * frequency[None, :]
    return (jnp.cos(angles)[:, None, :], jnp.sin(angles)[:, None, :])


def rotate(section, cosine_table, sine_table):
    half_width = cosine_table.shape[-1]
    first_half = section[..., :half_width]
    second_half = section[..., half_width : 2 * half_width]
    return jnp.concatenate(
        [
            first_half * cosine_table - second_half * sine_table,
            second_half * cosine_table + first_half * sine_table,
            section[..., 2 * half_width :],
        ],
        -1,
    )


def exact_gelu(values):
    return jax.nn.gelu(values, approximate=False)


def contract_rows(left, right):
    return lax.dot_general(
        left, right, (((0,), (0,)), ((), ())), preferred_element_type=jnp.float32
    )


def times_transposed(left, right):
    return lax.dot_general(
        left, right, (((1,), (1,)), ((), ())), preferred_element_type=jnp.float32
    )


def masked_scores(queries, key_rows, query_pos, key_pos, score_scale):
    scores = (
        jnp.einsum("qhd,khd->hqk", queries, key_rows, preferred_element_type=jnp.float32)
        * score_scale
    )
    allowed = key_pos[None, :] <= query_pos[:, None]
    return jnp.where(allowed[None], scores, neg_big)


def split_blocks(flat_rows, block_rows, head_count, head_dim):
    length = flat_rows.shape[0]
    return flat_rows.reshape(length // block_rows, block_rows, head_count, head_dim)


def attend(queries, key_all, value_all, query_pos, score_scale, block_rows):
    head_count, head_dim = (queries.shape[1], queries.shape[2])
    length = key_all.shape[0]
    key_blocks = split_blocks(key_all, block_rows, head_count, head_dim)
    value_blocks = split_blocks(value_all, block_rows, head_count, head_dim)
    position_blocks = jnp.arange(length, dtype=jnp.int32).reshape(length // block_rows, block_rows)

    def statistics(state_in, entry):
        running_max, running_sum = state_in
        key_rows, key_pos = entry
        scores = masked_scores(queries, key_rows, query_pos, key_pos, score_scale)
        new_max = jnp.maximum(running_max, jnp.max(scores, -1))
        running_sum = running_sum * jnp.exp(running_max - new_max) + jnp.sum(
            jnp.exp(scores - new_max[..., None]), -1
        )
        return ((new_max, running_sum), None)

    start_state = (
        jnp.full((head_count, queries.shape[0]), neg_big, jnp.float32),
        jnp.zeros((head_count, queries.shape[0]), jnp.float32),
    )
    (running_max, running_sum), _ = lax.scan(statistics, start_state, (key_blocks, position_blocks))
    log_total = running_max + jnp.log(running_sum)

    def attend_accumulate(mixed_heads, entry):
        key_rows, value_rows, key_pos = entry
        scores = masked_scores(queries, key_rows, query_pos, key_pos, score_scale)
        probs_low = jnp.exp(scores - log_total[..., None]).astype(jnp.bfloat16)
        return (
            mixed_heads
            + jnp.einsum("hqk,khd->qhd", probs_low, value_rows, preferred_element_type=jnp.float32),
            None,
        )

    mixed_heads, _ = lax.scan(
        attend_accumulate,
        jnp.zeros(queries.shape, jnp.float32),
        (key_blocks, value_blocks, position_blocks),
    )
    return (mixed_heads, log_total)


def query_grads(
    queries,
    grad_heads,
    key_all,
    value_all,
    log_total,
    delta_rows,
    query_pos,
    score_scale,
    block_rows,
):
    head_count, head_dim = (queries.shape[1], queries.shape[2])
    length = key_all.shape[0]
    key_blocks = split_blocks(key_all, block_rows, head_count, head_dim)
    value_blocks = split_blocks(value_all, block_rows, head_count, head_dim)
    position_blocks = jnp.arange(length, dtype=jnp.int32).reshape(length // block_rows, block_rows)

    def query_accumulate(grad_queries, entry):
        key_rows, value_rows, key_pos = entry
        scores = masked_scores(queries, key_rows, query_pos, key_pos, score_scale)
        probs = jnp.exp(scores - log_total[..., None])
        grad_probs = jnp.einsum(
            "qhd,khd->hqk", grad_heads, value_rows, preferred_element_type=jnp.float32
        )
        grad_scores = (probs * (grad_probs - delta_rows[..., None])).astype(jnp.bfloat16)
        return (
            grad_queries
            + jnp.einsum("hqk,khd->qhd", grad_scores, key_rows, preferred_element_type=jnp.float32),
            None,
        )

    grad_queries, _ = lax.scan(
        query_accumulate,
        jnp.zeros(queries.shape, jnp.float32),
        (key_blocks, value_blocks, position_blocks),
    )
    return grad_queries * score_scale


def key_terms(
    queries,
    grad_heads,
    log_total,
    delta_rows,
    query_pos,
    key_rows,
    value_rows,
    key_pos,
    score_scale,
):
    scores = masked_scores(queries, key_rows, query_pos, key_pos, score_scale)
    probs = jnp.exp(scores - log_total[..., None])
    grad_probs = jnp.einsum(
        "qhd,khd->hqk", grad_heads, value_rows, preferred_element_type=jnp.float32
    )
    grad_scores = (probs * (grad_probs - delta_rows[..., None])).astype(jnp.bfloat16)
    grad_keys = (
        jnp.einsum("hqk,qhd->khd", grad_scores, queries, preferred_element_type=jnp.float32)
        * score_scale
    )
    grad_values = jnp.einsum(
        "hqk,qhd->khd", probs.astype(jnp.bfloat16), grad_heads, preferred_element_type=jnp.float32
    )
    key_count = key_rows.shape[0]
    return jnp.concatenate(
        [grad_keys.reshape(key_count, -1), grad_values.reshape(key_count, -1)], -1
    )


def local(tokens, ln_gain, ln_bias, w_qkv, b_qkv, w_out, w_up, b_up, w_down, b_out, cotangent):
    seq_count, tok_rows, model_width = tokens.shape
    head_count = HEADS
    head_dim = model_width // head_count
    score_scale = head_dim ** (-0.5)
    length = tok_rows * lax.axis_size("seq")
    block_rows = math.gcd(length, 512)
    token_count = seq_count * tok_rows
    owned_shards = (ln_gain, ln_bias, w_qkv, b_qkv, w_out, w_up, b_up, w_down, b_out)
    norm_gain, norm_shift, wqkv, bqkv, wout, wup, bup, wdown, bout = (
        lax.all_gather(owned_shards[0], ("seq", "batch"), axis=0, tiled=True),
        lax.all_gather(owned_shards[1], ("seq", "batch"), axis=0, tiled=True),
        lax.all_gather(owned_shards[2], ("seq", "batch"), axis=0, tiled=True),
        lax.all_gather(owned_shards[3], ("seq", "batch"), axis=0, tiled=True),
        lax.all_gather(owned_shards[4], ("seq", "batch"), axis=0, tiled=True),
        lax.all_gather(owned_shards[5], ("seq", "batch"), axis=0, tiled=True),
        lax.all_gather(owned_shards[6], ("seq", "batch"), axis=0, tiled=True),
        lax.all_gather(owned_shards[7], ("seq", "batch"), axis=0, tiled=True),
        lax.all_gather(owned_shards[8], ("seq", "batch"), axis=0, tiled=True),
    )
    inputs = tokens.reshape(token_count, model_width).astype(jnp.float32)
    average = jnp.mean(inputs, -1, keepdims=True)
    centered = inputs - average
    inv_root = lax.rsqrt(jnp.mean(centered * centered, -1, keepdims=True) + eps_norm)
    unit_rows = centered * inv_root
    normed = (unit_rows * norm_gain.astype(jnp.float32) + norm_shift.astype(jnp.float32)).astype(
        jnp.bfloat16
    )
    joined_qkv = (
        jnp.dot(normed, wqkv, preferred_element_type=jnp.float32) + bqkv.astype(jnp.float32)
    ).reshape(seq_count, tok_rows, 3, head_count, head_dim)
    query_pos = lax.axis_index("seq") * tok_rows + jnp.arange(tok_rows, dtype=jnp.int32)
    cosine_table, sine_table = rotary_tables(query_pos.astype(jnp.float32), ROTARY // 2)
    queries = rotate(joined_qkv[:, :, 0], cosine_table, sine_table).astype(jnp.bfloat16)
    key_local = rotate(joined_qkv[:, :, 1], cosine_table, sine_table).astype(jnp.bfloat16)
    value_local = joined_qkv[:, :, 2].astype(jnp.bfloat16)
    key_all, value_all = (
        lax.all_gather(
            key_local.reshape(seq_count, tok_rows, model_width), "seq", axis=1, tiled=True
        ),
        lax.all_gather(
            value_local.reshape(seq_count, tok_rows, model_width), "seq", axis=1, tiled=True
        ),
    )

    def forward_sequence(entry):
        query_seq, key_seq, value_seq = entry
        return attend(query_seq, key_seq, value_seq, query_pos, score_scale, block_rows)

    mixed_heads, log_total = lax.map(forward_sequence, (queries, key_all, value_all))
    mixed_low = mixed_heads.reshape(token_count, model_width).astype(jnp.bfloat16)
    attn_out = jnp.dot(mixed_low, wout, preferred_element_type=jnp.float32)
    up_proj = jnp.dot(normed, wup, preferred_element_type=jnp.float32) + bup.astype(jnp.float32)
    activation = exact_gelu(up_proj).astype(jnp.bfloat16)
    mlp_out = jnp.dot(activation, wdown, preferred_element_type=jnp.float32)
    result = (inputs + attn_out + mlp_out + bout.astype(jnp.float32)).astype(jnp.bfloat16)
    norm_gain, norm_shift, wqkv, bqkv, wout, wup, bup, wdown, bout = (
        lax.all_gather(owned_shards[0], ("seq", "batch"), axis=0, tiled=True),
        lax.all_gather(owned_shards[1], ("seq", "batch"), axis=0, tiled=True),
        lax.all_gather(owned_shards[2], ("seq", "batch"), axis=0, tiled=True),
        lax.all_gather(owned_shards[3], ("seq", "batch"), axis=0, tiled=True),
        lax.all_gather(owned_shards[4], ("seq", "batch"), axis=0, tiled=True),
        lax.all_gather(owned_shards[5], ("seq", "batch"), axis=0, tiled=True),
        lax.all_gather(owned_shards[6], ("seq", "batch"), axis=0, tiled=True),
        lax.all_gather(owned_shards[7], ("seq", "batch"), axis=0, tiled=True),
        lax.all_gather(owned_shards[8], ("seq", "batch"), axis=0, tiled=True),
    )
    cotangent_rows = cotangent.reshape(token_count, model_width)
    cotangent_f = cotangent_rows.astype(jnp.float32)
    grad_bout = jnp.sum(cotangent_f, 0)
    grad_wout = contract_rows(mixed_low, cotangent_rows)
    grad_wdown = contract_rows(activation, cotangent_rows)
    grad_act = times_transposed(cotangent_rows, wdown)
    _, gelu_back = jax.vjp(exact_gelu, up_proj)
    grad_up = gelu_back(grad_act)[0].astype(jnp.bfloat16)
    grad_wup = contract_rows(normed, grad_up)
    grad_bup = jnp.sum(grad_up.astype(jnp.float32), 0)
    grad_heads = (
        times_transposed(cotangent_rows, wout)
        .astype(jnp.bfloat16)
        .reshape(seq_count, tok_rows, head_count, head_dim)
    )
    delta_rows = jnp.swapaxes(jnp.sum(grad_heads.astype(jnp.float32) * mixed_heads, -1), 1, 2)

    def backward_sequence(entry):
        query_seq, grad_seq, key_seq, value_seq, total_seq, delta_seq = entry
        return query_grads(
            query_seq,
            grad_seq,
            key_seq,
            value_seq,
            total_seq,
            delta_seq,
            query_pos,
            score_scale,
            block_rows,
        )

    grad_queries = lax.map(
        backward_sequence, (queries, grad_heads, key_all, value_all, log_total, delta_rows)
    )
    row_count = tok_rows * lax.axis_size("seq")
    sub_rows = math.gcd(row_count, 512)

    def one_block(block_index):
        first_key = block_index * sub_rows
        key_pos = first_key + jnp.arange(sub_rows, dtype=jnp.int32)

        def one_sequence(entry):
            query_seq, grad_seq, total_seq, delta_seq, key_seq, value_seq = entry
            key_rows = lax.dynamic_slice_in_dim(key_seq, first_key, sub_rows, 0).reshape(
                sub_rows, head_count, head_dim
            )
            value_rows = lax.dynamic_slice_in_dim(value_seq, first_key, sub_rows, 0).reshape(
                sub_rows, head_count, head_dim
            )
            return key_terms(
                query_seq,
                grad_seq,
                total_seq,
                delta_seq,
                query_pos,
                key_rows,
                value_rows,
                key_pos,
                score_scale,
            )

        per_sequence = lax.map(
            one_sequence, (queries, grad_heads, log_total, delta_rows, key_all, value_all)
        )
        return jnp.swapaxes(per_sequence, 0, 1)

    block_terms = lax.map(one_block, jnp.arange(row_count // sub_rows, dtype=jnp.int32))
    summed = lax.psum_scatter(
        block_terms.reshape(row_count, seq_count, 2 * model_width).astype(jnp.bfloat16),
        "seq",
        scatter_dimension=0,
        tiled=True,
    ).astype(jnp.float32)
    key_grads_all = jnp.swapaxes(summed, 0, 1)
    grad_keys = key_grads_all[..., :model_width].reshape(seq_count, tok_rows, head_count, head_dim)
    grad_values = key_grads_all[..., model_width:].reshape(
        seq_count, tok_rows, head_count, head_dim
    )
    grad_q_turned = rotate(grad_queries, cosine_table, -sine_table)
    grad_k_turned = rotate(grad_keys, cosine_table, -sine_table)
    grad_joined = (
        jnp.stack([grad_q_turned, grad_k_turned, grad_values], 2)
        .reshape(token_count, 3 * model_width)
        .astype(jnp.bfloat16)
    )
    grad_wqkv = contract_rows(normed, grad_joined)
    grad_bqkv = jnp.sum(grad_joined.astype(jnp.float32), 0)
    grad_normed = times_transposed(grad_joined, wqkv) + times_transposed(grad_up, wup)
    grad_gain = jnp.sum(grad_normed * unit_rows, 0)
    grad_shift = jnp.sum(grad_normed, 0)
    grad_unit = grad_normed * norm_gain.astype(jnp.float32)
    grad_inputs = cotangent_f + inv_root * (
        grad_unit
        - jnp.mean(grad_unit, -1, keepdims=True)
        - unit_rows * jnp.mean(grad_unit * unit_rows, -1, keepdims=True)
    )
    owner_grads = (
        lax.psum_scatter(grad_gain, ("seq", "batch"), scatter_dimension=0, tiled=True),
        lax.psum_scatter(grad_shift, ("seq", "batch"), scatter_dimension=0, tiled=True),
        lax.psum_scatter(grad_wqkv, ("seq", "batch"), scatter_dimension=0, tiled=True),
        lax.psum_scatter(grad_bqkv, ("seq", "batch"), scatter_dimension=0, tiled=True),
        lax.psum_scatter(grad_wout, ("seq", "batch"), scatter_dimension=0, tiled=True),
        lax.psum_scatter(grad_wup, ("seq", "batch"), scatter_dimension=0, tiled=True),
        lax.psum_scatter(grad_bup, ("seq", "batch"), scatter_dimension=0, tiled=True),
        lax.psum_scatter(grad_wdown, ("seq", "batch"), scatter_dimension=0, tiled=True),
        lax.psum_scatter(grad_bout, ("seq", "batch"), scatter_dimension=0, tiled=True),
    )
    return (
        result.reshape(seq_count, tok_rows, model_width),
        grad_inputs.reshape(seq_count, tok_rows, model_width),
        owner_grads[0],
        owner_grads[1],
        owner_grads[2],
        owner_grads[3],
        owner_grads[4],
        owner_grads[5],
        owner_grads[6],
        owner_grads[7],
        owner_grads[8],
    )


MESH = pl.DeviceIdType.MESH
F32, BF16 = jnp.float32, jnp.bfloat16
TOK = 128
BT = 256
MODEL = 1024
SEQ = 16
CHIPS = 8
UP = 256
HD = 64
WIDE = 512
VEC = 448
GRADS = 448


def dot(left, right):
    return jnp.dot(left, right, preferred_element_type=F32)


def dot_nt(left, right):
    return lax.dot_general(left, right, (((1,), (1,)), ((), ())), preferred_element_type=F32)


def lanes(block):
    if isinstance(block, int):
        return slice(block * BT, (block + 1) * BT)
    return pl.ds(pl.multiple_of(block * BT, BT), BT)


def turn(rows, cosine, sine):
    first, second = rows[0:8], rows[8:16]
    return jnp.concatenate(
        [first * cosine - second * sine, second * cosine + first * sine, rows[16:]], 0
    )


def remote(src, dst, send_sem, recv_sem, device):
    return pltpu.make_async_remote_copy(
        src_ref=src,
        dst_ref=dst,
        send_sem=send_sem,
        recv_sem=recv_sem,
        device_id=device,
        device_id_type=MESH,
    )


def fused(
    tokens_h, cot_h, w_qkv_h, w_out_h, w_up_h, w_down_h, gain, shift, bout, bup, bqkv, cost, sint,
    out_h, gn_sum_h, norm_gain_h, d_rows_h, arecv_h, ln_sums_h,
    out, d_rows, arecv, ln_sums, res_sems, w_qkv, w_up, in_sems, tok, g, wsend, wc, wct, wd, gv, bct, normed, unit, amt, dactt, qt, kt, vt, k, v, sbuf, e,
    linv, ot, gt, dost, delta, dkt, dvt, part1, rc1, ry1, rzl1, rzr1, rc2, ry2, rzl2, rzr2, tmp,
    dgain, dshift, dbout, dwct, dwd, dsend, drecv, dws, xrecv, vsend, vrecv, vparts,
    w_ss, w_rs, x_ss, x_rs, wd_ss, wd_rs, t_ss, t_rs, g_ss, g_rs,
    c1_ss, c1_rs, y1_ss, y1_rs, zp1_ss, zl1_rs, zm1_ss, zr1_rs,
    c2_ss, c2_rs, y2_ss, y2_rs, zp2_ss, zl2_rs, zm2_ss, zr2_rs,
    d_ss, d_rs, dx_ss, dx_rs, a_ss, a_rs, vx_ss, vx_rs, v_ss, v_rs,
):
    s = lax.axis_index("seq")
    b = lax.axis_index("batch")
    z, y, c = s // 4, (s // 2) % 2, s % 2
    oy, oc, ob = 1 - y, 1 - c, 1 - b
    sib = (s + 1 - 2 * c, b)
    yn = (s + 2 - 4 * y, b)
    zp = (lax.rem(s + 4, SEQ), b)
    zm = (lax.rem(s + SEQ - 4, SEQ), b)
    xn = (s, ob)
    offsets = [(dz, dy, dc) for dz in (0, 1, 3, 2) for dy in (0, 1) for dc in (0, 1)][1:]

    def shifted(offset, sign):
        dz, dy, dc = offset
        return (
            4 * lax.rem(z + 4 + sign * dz, 4)
            + 2 * lax.rem(y + 2 + sign * dy, 2)
            + lax.rem(c + 2 + sign * dc, 2)
        )

    high = z // 2
    zo = [z, z + 1 - 2 * lax.rem(z, 2), 2 - high, 3 - 3 * high]
    inner = jnp.logical_and(z > 0, z < 3)
    outer = jnp.logical_or(z == 0, z == 3)

    def mid(*steps):
        @pl.when(inner)
        def _():
            for step in steps:
                step[0](*step[1:])

    def end(*steps):
        @pl.when(outer)
        def _():
            for step in steps:
                step[0](*step[1:])

    def both(*steps):
        for step in steps:
            step[0](*step[1:])

    barrier = pltpu.get_barrier_semaphore()
    for off in offsets:
        pl.semaphore_signal(
            barrier, inc=1, device_id=(shifted(off, 1), b), device_id_type=MESH
        )
    pl.semaphore_signal(barrier, inc=1, device_id=xn, device_id_type=MESH)

    down_own = pl.ds(pl.multiple_of(128 * b, 128), 128)
    down_other = pl.ds(pl.multiple_of(128 * ob, 128), 128)
    out_own = pl.ds(pl.multiple_of(UP + 32 * b, 32), 32)
    out_other = pl.ds(pl.multiple_of(UP + 32 * ob, 32), 32)
    loads = [
        pltpu.make_async_copy(src, dst, in_sems.at[n])
        for n, (src, dst) in enumerate(
            [
                (w_up_h, w_up), (w_qkv_h, w_qkv), (tokens_h, tok.at[s]), (cot_h, g.at[s]),
                (w_down_h, wd.at[down_own]), (w_out_h, wd.at[out_own]),
            ]
        )
    ]
    for load in loads:
        load.start()

    vectors = [gain[...], shift[...], bout[...]]
    vectors += [bup[:, 32 * i : 32 * (i + 1)] for i in range(4)]
    vectors += [bqkv[:, 32 * i : 32 * (i + 1)] for i in range(3)]
    vec = jnp.concatenate([w.astype(F32) for w in vectors] + [jnp.zeros((6, 32), F32)], 0).T
    vec = jnp.concatenate([vec, jnp.zeros((32, HD - 16), F32)], 1).astype(BF16)
    loads[0].wait()
    loads[1].wait()
    for t in range(SEQ):
        wsend[t] = jnp.concatenate(
            [
                w_up[:, UP * t : UP * (t + 1)],
                w_qkv[:, HD * t : HD * (t + 1)],
                w_qkv[:, MODEL + HD * t : MODEL + HD * (t + 1)],
                w_qkv[:, 2 * MODEL + HD * t : 2 * MODEL + HD * (t + 1)],
                vec,
            ],
            1,
        )
    wc[2 * s + b] = wsend[s]
    for load in loads[2:6]:
        load.wait()
    pl.semaphore_wait(barrier, SEQ)

    def w_copy(source, target):
        return remote(
            wsend.at[target], wc.at[2 * source + b], w_ss.at[target], w_rs.at[source], (target, b)
        )

    def x_copy(source, plane):
        return remote(
            wc.at[2 * source + plane], wc.at[2 * source + plane],
            x_ss.at[source], x_rs.at[source], xn,
        )

    wd_copies = [
        remote(wd.at[down_own], wd.at[down_own], wd_ss.at[0], wd_rs.at[0], xn),
        remote(wd.at[out_own], wd.at[out_own], wd_ss.at[1], wd_rs.at[1], xn),
    ]

    def gather(buf, ss, rs):
        def send(shard, way, device):
            return remote(buf.at[shard], buf.at[shard], ss.at[way, shard], rs.at[shard], device)

        def arrived(shard):
            send(shard, 0, sib).wait_recv()

        def on_own_z(act):
            @pl.when(z < 3)
            def _():
                act(send(s, 0, zp))

            @pl.when(z > 0)
            def _():
                act(send(s, 1, zm))

        def on_own_y(act):
            act(send(s, 2, yn))
            act(send(s, 3, sib))

        def own_z():
            on_own_z(start)

        def own_y():
            on_own_y(start)

        def on_z(t, act):
            shard = 4 * zo[t] + 2 * y + c

            @pl.when(jnp.logical_and(zo[t] < z, z < 3))
            def _():
                act(send(shard, 0, zp))

            @pl.when(jnp.logical_and(zo[t] > z, z > 0))
            def _():
                act(send(shard, 1, zm))

            act(send(shard, 2, yn))
            act(send(shard, 3, sib))

        def on_y(t, act):
            act(send(4 * zo[t] + 2 * oy + c, 3, sib))

        start = lambda copy: copy.start()
        finish = lambda copy: copy.wait_send()

        def step_z(t):
            arrived(4 * zo[t] + 2 * y + c)
            on_z(t, start)

        def step_y(t):
            arrived(4 * zo[t] + 2 * oy + c)
            on_y(t, start)

        def step_core(t, row):
            arrived(4 * zo[t] + 2 * row + oc)

        def drain():
            on_own_z(finish)
            on_own_y(finish)
            for t in range(1, 4):
                on_z(t, finish)
            for t in range(4):
                on_y(t, finish)

        return own_z, own_y, step_z, step_y, step_core, drain

    tok_oz, tok_oy, tok_z, tok_y, tok_core, tok_drain = gather(tok, t_ss, t_rs)
    g_oz, g_oy, g_z, g_y, g_core, g_drain = gather(g, g_ss, g_rs)

    def w_send(lo, hi):
        for off in offsets[lo:hi]:
            w_copy(s, shifted(off, 1)).start()

    def w_arrive(lo, hi):
        for off in offsets[lo:hi]:
            source = shifted(off, -1)
            w_copy(source, s).wait_recv()
            x_copy(source, b).start()

    both((tok_oz,), (tok_oy,))
    for off in offsets: w_copy(s, shifted(off, 1)).start()
    x_copy(s, b).start()
    mid((tok_z, 1), (tok_z, 2), (tok_y, 0))
    end((tok_z, 1), (tok_y, 0))
    both((g_oy,))
    end((g_oz,))
    both((w_arrive, 0, 7))
    both((w_arrive, 7, 15))
    mid((tok_z, 3), (tok_y, 1))
    end((tok_z, 2), (tok_y, 1))
    for copy in wd_copies: copy.start()
    for t in range(SEQ): x_copy(t, ob).wait_recv()
    wct[...] = wc[...].reshape(MODEL, WIDE).T
    rows = wct[VEC : VEC + 16, :].astype(F32)
    gv[...] = jnp.zeros_like(gv)
    gv[0:1] = rows[0:1]
    gv[1:2] = rows[1:2]
    gv[2:3] = rows[2:3]
    cols = []
    for half in range(2):
        tail = wc[2 * s + half][:, VEC - HD :].astype(F32)
        for i in range(4):
            cols.append(tail[:, HD + 3 + i : HD + 4 + i])
    lane_of = lax.broadcasted_iota(jnp.int32, (32, 128), 1)
    for which in range(3):
        for half in range(2):
            chunk = 32 * which + 2 * s + half
            tail = wc[chunk // 3][:, VEC - HD :].astype(F32)
            cols.append(
                jnp.sum(jnp.where(lane_of == HD + 7 + lax.rem(chunk, 3), tail, 0.0), 1, keepdims=True)
            )
    bct[...] = jnp.concatenate(cols, 0)

    def project(i):
        x = tok[pl.ds(2 * i, 2)].reshape(BT, MODEL).astype(F32)
        centered = x - jnp.mean(x, -1, keepdims=True)
        inv = lax.rsqrt(jnp.mean(centered * centered, -1, keepdims=True) + eps_norm)
        u = centered * inv
        n = (u * gv[0:1] + gv[1:2]).astype(BF16)
        normed[i] = n
        unit[i] = u.astype(BF16)
        jt = dot_nt(wct[0:VEC], n) + bct[...]
        up = jt[0:UP]
        half = 0.5 + 0.5 * lax.erf(up * 0.7071067811865476)
        at = lanes(i)
        amt[0:UP, at] = (up * half).astype(BF16)
        dactt[:, at] = half + up * (jnp.exp(-0.5 * up * up) * 0.3989422804014327)
        cs, sn = cost[:, at], sint[:, at]
        qt[:, at] = (turn(jt[256:320], cs, sn) * 0.125).astype(BF16)
        keys = turn(jt[320:384], cs, sn)
        kt[:, at] = keys.astype(BF16)
        vt[:, at] = jt[384:448].astype(BF16)
        k[i] = keys.T.astype(BF16)
        v[i] = jt[384:448].T.astype(BF16)

    def chip_of(t, row):
        return 2 * zo[t] + row

    def proj(t, row):
        tok_core(t, row)
        project(chip_of(t, row))

    both((proj, 0, y))
    mid((g_oz,))
    both((proj, 0, oy), (proj, 1, y))
    both((proj, 1, oy))
    end((tok_z, 3), (g_y, 0))
    mid((g_z, 1), (g_y, 0), (tok_y, 2))
    both((proj, 2, y))
    mid((g_z, 2))
    end((tok_y, 2))
    both((proj, 2, oy))
    both((proj, 3, y))
    end((g_z, 1))
    both((tok_y, 3), (proj, 3, oy))
    mid((g_z, 3))

    def e_put(n, block):
        m, at = 2 * (n // 4), 256 * (n % 4)
        e[m : m + 2, :, at : at + 256] = block.reshape(2, TOK, BT)

    def e_get(n):
        m, at = 2 * (n // 4), 256 * (n % 4)
        return e[m : m + 2, :, at : at + 256].reshape(BT, BT)

    def attend_fwd(qb):
        at = lanes(qb)
        base = qb * (qb + 1) // 2
        q = qt[:, at]
        top = None
        for kb in range(qb + 1):
            st = dot(k[kb], q)
            if kb == qb:
                key_at = lax.broadcasted_iota(jnp.int32, (BT, BT), 0)
                query_at = lax.broadcasted_iota(jnp.int32, (BT, BT), 1)
                st = jnp.where(key_at <= query_at, st, neg_big)
            sbuf[kb] = st
            here = jnp.max(st, 0, keepdims=True)
            top = here if top is None else jnp.maximum(top, here)
        total = jnp.zeros((1, BT), F32)
        o = jnp.zeros((HD, BT), F32)
        for kb in range(qb + 1):
            ee = jnp.exp(sbuf[kb] - top)
            total = total + jnp.sum(ee, 0, keepdims=True)
            eb = ee.astype(BF16)
            e_put(base + kb, eb)
            o = o + dot(vt[:, lanes(kb)], eb)
        li = 1.0 / total
        linv[:, at] = li
        o = o * li
        ot[:, at] = o
        amt[UP : UP + HD, at] = o.astype(BF16)

    def reducer(part, rc, ry, rzl, rzr, c_ss, c_rs, y_ss, y_rs, zp_ss, zl_rs, zm_ss, zr_rs):
        order = [zo[3], zo[2], zo[1], zo[0]]

        def core_copy(t, row, color):
            chip = 2 * order[t] + row
            return remote(
                part.at[2 * chip + color], rc.at[chip], c_ss.at[chip], c_rs.at[chip], sib
            )

        def y_copy(t, row):
            return remote(
                rc.at[2 * order[t] + row], ry.at[order[t]], y_ss.at[order[t]], y_rs.at[order[t]], yn
            )

        def zp_copy(t):
            at = order[t]
            return remote(rc.at[2 * at + y], rzl.at[at], zp_ss.at[at], zl_rs.at[at], zp)

        def zm_copy(t):
            at = order[t]
            return remote(rc.at[2 * at + y], rzr.at[at], zm_ss.at[at], zr_rs.at[at], zm)

        def send_core(t, row):
            core_copy(t, row, oc).start()

        def send_y(t):
            chip = 2 * order[t] + oy
            core_copy(t, oy, oc).wait_recv()
            rc[chip] = (rc[chip].astype(F32) + part[2 * chip + c].astype(F32)).astype(BF16)
            y_copy(t, oy).start()

        def sum_here(t):
            chip = 2 * order[t] + y
            core_copy(t, y, oc).wait_recv()
            y_copy(t, y).wait_recv()
            tmp[...] = (
                rc[chip].astype(F32) + part[2 * chip + c].astype(F32) + ry[order[t]].astype(F32)
            )

        def add_left(t):
            zp_copy(t).wait_recv()
            tmp[...] += rzl[order[t]].astype(F32)

        def add_right(t):
            zm_copy(t).wait_recv()
            tmp[...] += rzr[order[t]].astype(F32)

        def pass_on(t):
            at = order[t]
            sum_here(t)

            @pl.when(jnp.logical_and(at > z, z > 0))
            def _():
                add_left(t)

            @pl.when(jnp.logical_and(at < z, z < 3))
            def _():
                add_right(t)

            rc[2 * at + y] = tmp[...].astype(BF16)

            @pl.when(at > z)
            def _():
                zp_copy(t).start()

            @pl.when(at < z)
            def _():
                zm_copy(t).start()

        def last():
            sum_here(3)

            @pl.when(z > 0)
            def _():
                add_left(3)

            @pl.when(z < 3)
            def _():
                add_right(3)

        def drain_core():
            for t in range(4):
                for row in (oy, y):
                    core_copy(t, row, oc).wait_send()

        def drain():
            for t in range(4):
                y_copy(t, oy).wait_send()
            for t in range(3):
                at = order[t]

                @pl.when(at > z)
                def _():
                    zp_copy(t).wait_send()

                @pl.when(at < z)
                def _():
                    zm_copy(t).wait_send()

        return order, send_core, send_y, pass_on, last, drain_core, drain

    order, core1, y1, pass1, last1, drain_core1, drain1 = reducer(
        part1, rc1, ry1, rzl1, rzr1, c1_ss, c1_rs, y1_ss, y1_rs, zp1_ss, zl1_rs, zm1_ss, zr1_rs
    )
    _, core2, y2, pass2, last2, drain_core2, drain2 = reducer(
        e, rc2, ry2, rzl2, rzr2, c2_ss, c2_rs, y2_ss, y2_rs, zp2_ss, zl2_rs, zm2_ss, zr2_rs
    )

    def out_block(t, row):
        i = 2 * order[t] + row
        part1[pl.ds(2 * i, 2)] = (
            dot(amt[:, lanes(i)].T, wd[...]).astype(BF16).reshape(2, TOK, MODEL)
        )
        core1(t, row)

    def grads_at(i):
        gb = g[pl.ds(2 * i, 2)].reshape(BT, MODEL)
        at = lanes(i)
        r = dot_nt(wd[...], gb)
        gt[0:UP, at] = (r[0:UP] * dactt[:, at]).astype(BF16)
        li = linv[:, at]
        gm = r[UP : UP + HD]
        dost[:, at] = (gm * li).astype(BF16)
        delta[:, at] = jnp.sum(gm * ot[:, at], 0, keepdims=True) * li
        dbout[...] += jnp.sum(gb.astype(F32).reshape(BT // 8, 8, MODEL), 0)

    def attend_bwd(qb):
        at = lanes(qb)
        base = qb * (qb + 1) // 2
        do, q, de = dost[:, at], qt[:, at], delta[:, at]
        dq = jnp.zeros((HD, BT), F32)
        for kb in range(qb + 1):
            ks = lanes(kb)
            eb = e_get(base + kb)
            dp = dot(v[kb], do)
            ds = (eb.astype(F32) * (dp - de)).astype(BF16)
            dv = dot_nt(do, eb)
            dk = dot_nt(q, ds)
            if kb == qb:
                dvt[:, ks] = dv
                dkt[:, ks] = dk
            else:
                dvt[:, ks] += dv
                dkt[:, ks] += dk
            dq = dq + dot(kt[:, ks], ds)
        gt[256:320, at] = turn(dq * 0.125, cost[:, at], -sint[:, at]).astype(BF16)

    def norm_grads(t, row):
        i = 2 * order[t] + row
        gn = dot(gt[:, lanes(i)].T, wct[0:GRADS])
        e[pl.ds(2 * i, 2)] = gn.astype(BF16).reshape(2, TOK, MODEL)
        core2(t, row)
        dshift[...] += jnp.sum(gn.reshape(BT // 8, 8, MODEL), 0)
        dgain[...] += jnp.sum((gn * unit[i].astype(F32)).reshape(BT // 8, 8, MODEL), 0)

    dgain[...] = jnp.zeros_like(dgain)
    dshift[...] = jnp.zeros_like(dshift)
    dbout[...] = jnp.zeros_like(dbout)

    def wd_arrive():
        for copy in wd_copies:
            copy.wait_send()
        remote(wd.at[down_other], wd.at[down_other], wd_ss.at[0], wd_rs.at[0], xn).wait_recv()
        remote(wd.at[out_other], wd.at[out_other], wd_ss.at[1], wd_rs.at[1], xn).wait_recv()

    def fwd(lo, hi):
        for qb in range(lo, hi):
            attend_fwd(qb)

    def grads(t, row):
        g_core(t, row)
        grads_at(chip_of(t, row))

    def bwd(lo, hi):
        for qb in range(lo, hi):
            attend_bwd(qb)

    def bwd_keys():
        gt[320:384, :] = turn(dkt[...], cost[...], -sint[...]).astype(BF16)
        gt[384:448, :] = dvt[...].astype(BF16)

    dx_copies = [remote(dws.at[p, ob], xrecv.at[p], dx_ss.at[p], dx_rs.at[p], xn) for p in range(2)]

    def turn_out(p, extra):
        for j in range(2 * SEQ // 4):
            turned = dwct[256 * p : 256 * (p + 1), 128 * j : 128 * (j + 1)].T
            for i in range(4):
                piece = turned[32 * i : 32 * (i + 1)]
                dev = 4 * j + i
                at = dws.at[p, dev % 2, dev // 2]
                if extra is None:
                    at[...] = piece.astype(BF16)
                else:
                    at[:, 0:128] = piece[:, 0:128].astype(BF16)
                    at[:, 128:256] = (piece[:, 128:256] + extra).astype(BF16)
        dx_copies[p].start()

    def up_grads():
        nn = normed.reshape(SEQ * TOK, MODEL)
        for n in range(4):
            dwct[0:256, lanes(n)] = dot(gt[0:256], nn[:, lanes(n)])
        turn_out(0, None)

    def qkv_grads():
        nn = normed.reshape(SEQ * TOK, MODEL)
        for n in range(4):
            dwct[256:GRADS, lanes(n)] = dot(gt[256:GRADS], nn[:, lanes(n)])
        dwct[GRADS:WIDE] = jnp.zeros((WIDE - GRADS, MODEL), F32)
        dwct[VEC : VEC + 1] = jnp.sum(dbout[...], 0, keepdims=True)
        bias_col = jnp.sum(gt[...].astype(F32), 1, keepdims=True)
        turn_out(
            1,
            jnp.concatenate(
                [jnp.zeros((32, HD + 1), F32)]
                + [bias_col[32 * n : 32 * (n + 1)] for n in range(14)]
                + [jnp.zeros((32, 128 - HD - 15), F32)],
                1,
            ),
        )

    vx_copy = remote(vsend, vrecv, vx_ss, vx_rs, xn)

    def ln_grads():
        vsend[0:1] = jnp.sum(dgain[...], 0, keepdims=True)
        vsend[1:2] = jnp.sum(dshift[...], 0, keepdims=True)
        vsend[2:8] = jnp.zeros((6, MODEL), F32)
        vx_copy.start()

    d_copy = remote(dsend, drecv, d_ss, d_rs, xn)

    def down_grads():
        gg = g.reshape(SEQ * TOK, MODEL)
        for n in range(4):
            dwd[:, lanes(n)] = dot(amt[...], gg[:, lanes(n)])
        dsend[0:128] = dwd[down_other].astype(BF16)
        dsend[128:160] = dwd[out_other].astype(BF16)
        d_copy.start()

    def a_copy(p, source, target):
        return remote(
            dws.at[p, b, target], arecv.at[p, source], a_ss.at[p, target], a_rs.at[p, source],
            (target, b),
        )

    def wide_out(p):
        dx_copies[p].wait_recv()
        dws[p, b] = (dws[p, b].astype(F32) + xrecv[p].astype(F32)).astype(BF16)
        for off in offsets:
            a_copy(p, s, shifted(off, 1)).start()
        arecv[p, s] = dws[p, b, s]

    res_copies = [
        pltpu.make_async_copy(src, dst, res_sems.at[n])
        for n, (src, dst) in enumerate(
            [
                (out, out_h), (tmp, gn_sum_h), (gv, norm_gain_h), (d_rows, d_rows_h),
                (arecv, arecv_h), (ln_sums, ln_sums_h),
            ]
        )
    ]

    def end1():
        last1()
        out[...] = (tmp[...] + tok[s].astype(F32) + gv[2:3]).astype(BF16)
        res_copies[0].start()

    def v_copy(source, target):
        piece = pl.ds(pl.multiple_of(128 * (target // 2), 128), 128)
        return remote(
            vrecv.at[:, piece], vparts.at[source], v_ss.at[target], v_rs.at[source], (target, b)
        )

    def ln_out():
        vx_copy.wait()
        vrecv[...] += vsend[...]
        for off in offsets:
            v_copy(s, shifted(off, 1)).start()
        vparts[s] = vrecv[:, pl.ds(pl.multiple_of(128 * (s // 2), 128), 128)]

    def down_out():
        d_copy.wait_recv()
        d_rows[0:128] = dwd[down_own] + drecv[0:128].astype(F32)
        d_rows[128:160] = dwd[out_own] + drecv[128:160].astype(F32)
        res_copies[2].start()
        res_copies[3].start()

    def ln_arrive():
        for off in offsets:
            v_copy(shifted(off, -1), s).wait_recv()
        ln_sums[...] = jnp.sum(vparts[...], 0)
        res_copies[5].start()

    def end2():
        last2()
        res_copies[1].start()

    def wide_arrive():
        for off in offsets:
            a_copy(0, shifted(off, -1), s).wait_recv()
            a_copy(1, shifted(off, -1), s).wait_recv()
        res_copies[4].start()

    both((wd_arrive,), (fwd, 0, 5))
    mid((g_y, 1))
    end((g_z, 2))
    both((fwd, 5, 8))
    end((g_y, 1))
    both((grads, 0, y), (out_block, 0, oy), (out_block, 1, oy), (out_block, 2, oy), (out_block, 3, oy))
    end((g_z, 3))
    both((y1, 0), (y1, 1), (y1, 2), (y1, 3))
    both((out_block, 0, y), (out_block, 1, y), (out_block, 2, y), (out_block, 3, y))
    both((grads, 0, oy), (grads, 1, y), (grads, 1, oy), (grads, 2, y), (g_y, 2), (grads, 2, oy), (grads, 3, y))
    both((g_y, 3), (grads, 3, oy))
    both((up_grads,))
    both((bwd, 0, 4))
    end((pass1, 0))
    both((bwd, 4, 8), (bwd_keys,))
    end((pass1, 1))
    both((qkv_grads,))
    both((wide_out, 0))
    both((norm_grads, 0, oy), (norm_grads, 1, oy), (norm_grads, 2, oy), (norm_grads, 3, oy))
    both((y2, 0), (y2, 1), (y2, 2), (y2, 3))
    end((pass1, 2))
    mid((pass1, 0))
    both((norm_grads, 0, y), (norm_grads, 1, y), (norm_grads, 2, y), (norm_grads, 3, y))
    mid((pass1, 1), (pass1, 2))
    both((ln_grads,), (down_grads,))
    both((wide_out, 1), (ln_out,), (end1,), (pass2, 0))
    both((pass2, 1))
    both((down_out,))
    both((pass2, 2), (ln_arrive,), (wide_arrive,), (end2,))

    for off in offsets:
        w_copy(s, shifted(off, 1)).wait_send()
        a_copy(0, s, shifted(off, 1)).wait_send()
        a_copy(1, s, shifted(off, 1)).wait_send()
        v_copy(s, shifted(off, 1)).wait_send()
    for t in range(SEQ):
        x_copy(t, b).wait_send()
    tok_drain()
    g_drain()
    drain_core1()
    drain1()
    drain_core2()
    drain2()
    d_copy.wait_send()
    for copy in dx_copies:
        copy.wait_send()
    for copy in res_copies:
        copy.wait()


def finish(
    tokens_h, cot_h, out_h, gn_sum_h, norm_gain_h, d_rows_h, arecv_h, ln_sums_h,
    out, d_tok_h, d_gain, d_shift, d_qkv_h, d_bqkv, d_out, d_up_h, d_bup, d_down, d_bout,
    tokens, cot, gn_sum, norm_gain, arecv, ln_sums, d_tok, d_qkv, d_up, kept, rows, sems, out_sems,
):
    loads = [
        pltpu.make_async_copy(src, dst, sems.at[n])
        for n, (src, dst) in enumerate(
            [
                (arecv_h.at[0], arecv.at[0]), (arecv_h.at[1], arecv.at[1]),
                (gn_sum_h, gn_sum), (tokens_h, tokens), (norm_gain_h, norm_gain), (cot_h, cot),
                (ln_sums_h, ln_sums), (out_h, kept), (d_rows_h, rows),
            ]
        )
    ]
    stores = [
        pltpu.make_async_copy(src, dst, out_sems.at[n])
        for n, (src, dst) in enumerate(
            [
                (kept, out), (rows.at[0:128], d_down), (rows.at[128:160], d_out),
                (d_up, d_up_h), (d_qkv, d_qkv_h), (d_tok, d_tok_h),
            ]
        )
    ]
    for move in loads:
        move.start()
    s = lax.axis_index("seq")
    b = lax.axis_index("batch")
    loads[0].wait()
    for t in range(SEQ):
        d_up[:, UP * t : UP * (t + 1)] = arecv[0, t].astype(F32)
    stores[3].start()
    loads[7].wait()
    loads[8].wait()
    for move in stores[0:3]:
        move.start()
    loads[1].wait()
    for t in range(0, SEQ, 2):
        even, odd = arecv[1, t].astype(F32), arecv[1, t + 1].astype(F32)
        for which in range(3):
            lo = HD * which
            d_qkv[:, MODEL * which + HD * t : MODEL * which + HD * (t + 2)] = jnp.concatenate(
                [even[:, lo : lo + HD], odd[:, lo : lo + HD]], 1
            )
    stores[4].start()
    for move in loads[2:7]:
        move.wait()
    x = tokens[...].astype(F32)
    centered = x - jnp.mean(x, -1, keepdims=True)
    inv = lax.rsqrt(jnp.mean(centered * centered, -1, keepdims=True) + eps_norm)
    u = centered * inv
    gu = gn_sum[...] * norm_gain[0:1]
    d_tok[...] = cot[...].astype(F32) + inv * (
        gu - jnp.mean(gu, -1, keepdims=True) - u * jnp.mean(gu * u, -1, keepdims=True)
    )
    stores[5].start()
    lane_of = lax.broadcasted_iota(jnp.int32, (32, 128), 1)

    def pick(block, lane):
        return jnp.sum(jnp.where(lane_of == lane, block, 0.0), 1, keepdims=True)

    mine = arecv[1, s][:, 128:256].astype(F32)
    picked = [mine[:, HD : HD + 1]]
    for i in range(4):
        picked.append(pick(mine, HD + 1 + 4 * b + i))
    for i in range(3):
        chunk = 3 * (2 * s + b) + i
        block = arecv[1, lax.rem(chunk, 32) // 2][:, 128:256].astype(F32)
        picked.append(pick(block, HD + 1 + 8 + 2 * (chunk // 32) + lax.rem(chunk, 2)))
    rows = jnp.concatenate(picked + [jnp.zeros((32, 120), F32)], 1).T
    d_bout[...] = rows[0:1]
    d_bup[...] = jnp.concatenate([rows[1 + i : 2 + i] for i in range(4)], 1)
    d_bqkv[...] = jnp.concatenate([rows[5 + i : 6 + i] for i in range(3)], 1)
    turned = pltpu.roll(ln_sums[...], lax.rem(128 - 32 * lax.rem(2 * s + b, 4), 128), 1)
    d_gain[...] = turned[0:1, 0:32]
    d_shift[...] = turned[1:2, 0:32]
    for move in stores:
        move.wait()


def fast_local(
    tokens, ln_gain, ln_bias, w_qkv, b_qkv, w_out, w_up, b_up, w_down, b_out, cotangent
):
    length = SEQ * TOK
    frequency = rotary_base ** (-(2.0 * np.arange(8)) / 16.0)
    angles = frequency.astype(np.float32)[:, None] * np.arange(length, dtype=np.float32)[None]
    cost = jnp.asarray(np.cos(angles.astype(np.float64)).astype(np.float32))
    sint = jnp.asarray(np.sin(angles.astype(np.float64)).astype(np.float32))
    vm = pl.BlockSpec(memory_space=pltpu.VMEM)
    far = pl.BlockSpec(memory_space=pl.ANY)
    shape = jax.ShapeDtypeStruct
    dma = pltpu.SemaphoreType.DMA

    def reduce_buffers():
        return [
            pltpu.VMEM((CHIPS, TOK, MODEL), BF16),
            pltpu.VMEM((4, TOK, MODEL), BF16),
            pltpu.VMEM((4, TOK, MODEL), BF16),
            pltpu.VMEM((4, TOK, MODEL), BF16),
        ]

    reduce_sems = [dma((8,)), dma((8,))] + [dma((4,))] * 6
    results = pl.pallas_call(
        fused,
        out_shape=[
            shape((TOK, MODEL), BF16),
            shape((TOK, MODEL), F32),
            shape((8, MODEL), F32),
            shape((160, MODEL), F32),
            shape((2, SEQ, 32, 256), BF16),
            shape((8, 128), F32),
        ],
        in_specs=[far] * 6 + [vm] * 7,
        out_specs=[far] * 6,
        scratch_shapes=[
            pltpu.VMEM((TOK, MODEL), BF16),
            pltpu.VMEM((160, MODEL), F32),
            pltpu.VMEM((2, SEQ, 32, 256), BF16),
            pltpu.VMEM((8, 128), F32),
            dma((6,)),
            pltpu.VMEM((32, 3 * MODEL), BF16),
            pltpu.VMEM((32, 4 * MODEL), BF16),
            dma((6,)),
            pltpu.VMEM((SEQ, TOK, MODEL), BF16),
            pltpu.VMEM((SEQ, TOK, MODEL), BF16),
            pltpu.VMEM((SEQ, 32, WIDE), BF16),
            pltpu.VMEM((2 * SEQ, 32, WIDE), BF16),
            pltpu.VMEM((WIDE, MODEL), BF16),
            pltpu.VMEM((UP + HD, MODEL), BF16),
            pltpu.VMEM((8, MODEL), F32),
            pltpu.VMEM((VEC, 1), F32),
            pltpu.VMEM((CHIPS, BT, MODEL), BF16),
            pltpu.VMEM((CHIPS, BT, MODEL), BF16),
            pltpu.VMEM((UP + HD, length), BF16),
            pltpu.VMEM((UP, length), F32),
            pltpu.VMEM((HD, length), BF16),
            pltpu.VMEM((HD, length), BF16),
            pltpu.VMEM((HD, length), BF16),
            pltpu.VMEM((CHIPS, BT, HD), BF16),
            pltpu.VMEM((CHIPS, BT, HD), BF16),
            pltpu.VMEM((CHIPS, BT, BT), F32),
            pltpu.VMEM((18, TOK, MODEL), BF16),
            pltpu.VMEM((1, length), F32),
            pltpu.VMEM((HD, length), F32),
            pltpu.VMEM((GRADS, length), BF16),
            pltpu.VMEM((HD, length), BF16),
            pltpu.VMEM((1, length), F32),
            pltpu.VMEM((HD, length), F32),
            pltpu.VMEM((HD, length), F32),
            pltpu.VMEM((SEQ, TOK, MODEL), BF16),
        ]
        + reduce_buffers()
        + reduce_buffers()
        + [
            pltpu.VMEM((TOK, MODEL), F32),
            pltpu.VMEM((8, MODEL), F32),
            pltpu.VMEM((8, MODEL), F32),
            pltpu.VMEM((8, MODEL), F32),
            pltpu.VMEM((WIDE, MODEL), F32),
            pltpu.VMEM((UP + HD, MODEL), F32),
            pltpu.VMEM((160, MODEL), BF16),
            pltpu.VMEM((160, MODEL), BF16),
            pltpu.VMEM((2, 2, SEQ, 32, 256), BF16),
            pltpu.VMEM((2, SEQ, 32, 256), BF16),
            pltpu.VMEM((8, MODEL), F32),
            pltpu.VMEM((8, MODEL), F32),
            pltpu.VMEM((SEQ, 8, 128), F32),
            dma((SEQ,)), dma((SEQ,)), dma((SEQ,)), dma((SEQ,)), dma((2,)), dma((2,)),
            dma((4, SEQ)), dma((SEQ,)), dma((4, SEQ)), dma((SEQ,)),
        ]
        + reduce_sems
        + reduce_sems
        + [dma, dma, dma((2,)), dma((2,)), dma((2, SEQ)), dma((2, SEQ)), dma, dma, dma((SEQ,)), dma((SEQ,))],
        compiler_params=pltpu.CompilerParams(
            collective_id=0, has_side_effects=True, vmem_limit_bytes=62 * 2**20
        ),
    )(
        tokens.reshape(TOK, MODEL), cotangent.reshape(TOK, MODEL),
        w_qkv, w_out, w_up, w_down,
        ln_gain.reshape(1, 32), ln_bias.reshape(1, 32), b_out.reshape(1, 32),
        b_up.reshape(1, 128), b_qkv.reshape(1, 96), cost, sint,
    )
    out, gn_sum, norm_gain, d_rows, arecv, ln_sums = results
    (out, d_tok, d_gain, d_shift, d_qkv, d_bqkv, d_out, d_up, d_bup, d_down, d_bout) = pl.pallas_call(
        finish,
        out_shape=[
            shape((TOK, MODEL), BF16),
            shape((TOK, MODEL), F32),
            shape((1, 32), F32),
            shape((1, 32), F32),
            shape((32, 3 * MODEL), F32),
            shape((1, 96), F32),
            shape((32, MODEL), F32),
            shape((32, 4 * MODEL), F32),
            shape((1, 128), F32),
            shape((128, MODEL), F32),
            shape((1, 32), F32),
        ],
        in_specs=[far] * 8,
        out_specs=[far, far, vm, vm, far, vm, far, far, vm, far, vm],
        scratch_shapes=[
            pltpu.VMEM((TOK, MODEL), BF16),
            pltpu.VMEM((TOK, MODEL), BF16),
            pltpu.VMEM((TOK, MODEL), F32),
            pltpu.VMEM((8, MODEL), F32),
            pltpu.VMEM((2, SEQ, 32, 256), BF16),
            pltpu.VMEM((8, 128), F32),
            pltpu.VMEM((TOK, MODEL), F32),
            pltpu.VMEM((32, 3 * MODEL), F32),
            pltpu.VMEM((32, 4 * MODEL), F32),
            pltpu.VMEM((TOK, MODEL), BF16),
            pltpu.VMEM((160, MODEL), F32),
            dma((9,)),
            dma((6,)),
        ],
        compiler_params=pltpu.CompilerParams(vmem_limit_bytes=62 * 2**20),
    )(
        tokens.reshape(TOK, MODEL), cotangent.reshape(TOK, MODEL),
        out, gn_sum, norm_gain, d_rows, arecv, ln_sums,
    )
    return (
        out.reshape(tokens.shape),
        d_tok.reshape(tokens.shape),
        d_gain.reshape(32),
        d_shift.reshape(32),
        d_qkv,
        d_bqkv.reshape(96),
        d_out,
        d_up,
        d_bup.reshape(128),
        d_down,
        d_bout.reshape(32),
    )


def solution(mesh):
    in_specs = (
        P("batch", "seq", None),
        P(("seq", "batch")),
        P(("seq", "batch")),
        P(("seq", "batch"), None),
        P(("seq", "batch")),
        P(("seq", "batch"), None),
        P(("seq", "batch"), None),
        P(("seq", "batch")),
        P(("seq", "batch"), None),
        P(("seq", "batch")),
        P("batch", "seq", None),
    )
    out_specs = (
        P("batch", "seq", None),
        P("batch", "seq", None),
        P(("seq", "batch")),
        P(("seq", "batch")),
        P(("seq", "batch"), None),
        P(("seq", "batch")),
        P(("seq", "batch"), None),
        P(("seq", "batch"), None),
        P(("seq", "batch")),
        P(("seq", "batch"), None),
        P(("seq", "batch")),
    )
    fits = mesh.shape["seq"] == SEQ and mesh.shape["batch"] == 2
    body = fast_local if fits else local
    return jax.shard_map(body, mesh=mesh, in_specs=in_specs, out_specs=out_specs, check_vma=False)
```
